32 devices in a mesh: wide: 8 (over z, y), narrow: 4 (over x, core).
Axes of the slice: x: 2, y: 2, z: 4, core: 2. Of those that a mesh axis runs over, the one named last changes fastest.
Arguments:
- block_input: bfloat16 [4096, 2048], P('wide'), may hold values from -6 to 6
- gain_attn: float32 [2048], replicated, may hold values from 0.5 to 1.5
- w_query: bfloat16 [2048, 2048], P('wide', 'narrow'), may hold values from -0.125 to 0.125
- w_key: bfloat16 [2048, 2048], P('wide', 'narrow'), may hold values from -0.125 to 0.125
- w_value: bfloat16 [2048, 4096], P('wide', 'narrow'), may hold values from -0.125 to 0.125
- w_gate_out: bfloat16 [2048, 4096], P('wide', 'narrow'), may hold values from -0.125 to 0.125
- w_decay: bfloat16 [2048, 16], P('wide', 'narrow'), may hold values from -0.0625 to 0.0625
- w_beta: bfloat16 [2048, 16], P('wide', 'narrow'), may hold values from -0.125 to 0.125
- conv_query: float32 [4, 2048], P(None, 'narrow'), may hold values from -3 to 3
- conv_key: float32 [4, 2048], P(None, 'narrow'), may hold values from -3 to 3
- conv_value: float32 [4, 4096], P(None, 'narrow'), may hold values from -3 to 3
- a_log: float32 [16], P('narrow'), may hold values from -1.5 to 1
- dt_bias: float32 [16], P('narrow'), may hold values from -6 to -1
- out_gain: float32 [256], replicated, may hold values from 0.5 to 1.5
- w_out: bfloat16 [2048, 4096], P('wide', 'narrow'), may hold values from -0.1875 to 0.1875
- gain_mlp: float32 [2048], replicated, may hold values from 0.5 to 1.5
- w_gate: bfloat16 [2048, 5504], P(None, 'wide'), may hold values from -0.125 to 0.125
- w_up: bfloat16 [2048, 5504], P(None, 'wide'), may hold values from -0.125 to 0.125
- w_down: bfloat16 [5504, 2048], P('wide'), may hold values from -0.109375 to 0.109375
- doc_lengths: int32 [9], replicated, may hold values from 1 to 3584, as said below
- cotangent: bfloat16 [4096, 2048], P(('wide', 'narrow')), may hold values from -6 to 6
Outputs:
- output: bfloat16 [4096, 2048], P(('wide', 'narrow'))
- grad_input: float32 [4096, 2048], P(('wide', 'narrow'))
- grad_gain_attn: float32 [2048], replicated
- grad_w_query: float32 [2048, 2048], P('wide', 'narrow')
- grad_w_key: float32 [2048, 2048], P('wide', 'narrow')
- grad_w_value: float32 [2048, 4096], P('wide', 'narrow')
- grad_w_gate_out: float32 [2048, 4096], P('wide', 'narrow')
- grad_w_decay: float32 [2048, 16], P('wide', 'narrow')
- grad_w_beta: float32 [2048, 16], P('wide', 'narrow')
- grad_conv_query: float32 [4, 2048], replicated
- grad_conv_key: float32 [4, 2048], replicated
- grad_conv_value: float32 [4, 4096], replicated
- grad_a_log: float32 [16], replicated
- grad_dt_bias: float32 [16], replicated
- grad_out_gain: float32 [256], replicated
- grad_w_out: float32 [2048, 4096], P('wide', 'narrow')
- grad_gain_mlp: float32 [2048], replicated
- grad_w_gate: float32 [2048, 5504], P('narrow', 'wide')
- grad_w_up: float32 [2048, 5504], P('narrow', 'wide')
- grad_w_down: float32 [5504, 2048], P('wide', 'narrow')
The draws below stay inside these ranges and needn't reach their ends.
Inputs may be any that keep to these rules, and one draw needn't show every extreme that they name: `doc_lengths`: sequences lie end to end from row 0 in order, each taking its length rounded up to a multiple of 64 rows; these rounded lengths add up to 4096. One sequence, at a place drawn from the seed, starts within the first 512 rows and ends within the last 512 rows.
All inputs are finite; a program needn't handle non-finite values.
Results may differ from the reference program's by a relative error of at most 0.019.
Values may be sent and summed in bfloat16 or wider, within the bound.
A program may use at most 384 MiB of HBM per device.

```python
import jax
import jax.numpy as jnp
from jax import lax

D = 2048
NH = 16
DK = 128
DV = 256
FF = 5504
CONV = 4
BLOCK = 64
TOK_DEV = 512
TOKENS = 4096
NSEQ = 9


def draw_doc_lengths(key, part):
    key = jax.random.fold_in(key, 11)
    per_device = TOK_DEV // BLOCK
    short_key, slot_key = jax.random.split(key)
    shorts = jax.random.randint(short_key, (per_device,), 1, BLOCK + 1, dtype=jnp.int32)
    long_slot = jax.random.randint(slot_key, (), 1, per_device, dtype=jnp.int32)
    longest = (TOKENS // BLOCK - per_device) * BLOCK
    slot_ids = jnp.arange(NSEQ, dtype=jnp.int32)
    short_ids = jnp.clip(slot_ids - (slot_ids > long_slot).astype(jnp.int32), 0, per_device - 1)
    return jnp.where(slot_ids == long_slot, longest, shorts[short_ids]).astype(jnp.int32)


def shard_levels(own_key, dims, cuts, least, high):
    factor_of = 1.0
    for dim, blocks in cuts:
        heights = jax.random.uniform(jax.random.fold_in(jax.random.fold_in(own_key, 6), dim), (blocks,), jnp.float32, least / len(cuts), high / len(cuts))
        factor_of = factor_of * jnp.repeat(jnp.exp(heights), dims[dim] // blocks).reshape((-1,) + (1,) * (len(dims) - 1 - dim))
    return factor_of


def normal_values(own_key, dims, width, bound, shards=(), kind=jnp.bfloat16):
    level = shard_levels(own_key, dims, shards, -0.22, 0.18) if shards else 1.0
    entries = jax.random.normal(own_key, dims, jnp.float32) * width * level
    return jnp.minimum(jnp.maximum(entries, -bound), bound).astype(kind)


def setup_inputs(seed: int = 0) -> dict:
    arg_keys = jax.random.split(jax.random.key(seed), 22)
    block_input = normal_values(arg_keys[0], (TOKENS, D), 1.0, 6.0, ((0, 8),))
    gain_attn = jnp.clip(1.0 + 0.1 * jax.random.normal(arg_keys[1], (D,), jnp.float32), 0.5, 1.5)
    w_query = normal_values(arg_keys[2], (D, NH * DK), D ** -0.5, 0.125, ((0, 8), (1, 4)))
    w_key = normal_values(arg_keys[3], (D, NH * DK), D ** -0.5, 0.125, ((0, 8), (1, 4)))
    w_value = normal_values(arg_keys[4], (D, NH * DV), D ** -0.5, 0.125, ((0, 8), (1, 4)))
    w_gate_out = normal_values(arg_keys[5], (D, NH * DV), D ** -0.5, 0.125, ((0, 8), (1, 4)))
    w_decay = normal_values(arg_keys[6], (D, NH), (4 * D) ** -0.5, 0.0625, ((0, 8), (1, 4)))
    w_beta = normal_values(arg_keys[7], (D, NH), D ** -0.5, 0.125, ((0, 8), (1, 4)))
    conv_query = normal_values(arg_keys[8], (CONV, NH * DK), CONV ** -0.5, 3.0, ((1, 4),), jnp.float32)
    conv_key = normal_values(arg_keys[9], (CONV, NH * DK), CONV ** -0.5, 3.0, ((1, 4),), jnp.float32)
    conv_value = normal_values(arg_keys[10], (CONV, NH * DV), CONV ** -0.5, 3.0, ((1, 4),), jnp.float32)
    a_log = jnp.clip(-1.5 + 2.5 * jax.random.uniform(arg_keys[11], (NH,), jnp.float32) ** shard_levels(arg_keys[11], (NH,), ((0, 4),), -0.2, 0.2), -1.5, 1.0)
    dt_bias = jnp.clip(-6.0 + 5.0 * jax.random.uniform(arg_keys[12], (NH,), jnp.float32) ** shard_levels(arg_keys[12], (NH,), ((0, 4),), -0.2, 0.2), -6.0, -1.0)
    out_gain = jnp.clip(1.0 + 0.1 * jax.random.normal(arg_keys[13], (DV,), jnp.float32), 0.5, 1.5)
    w_out = normal_values(arg_keys[14], (D, NH * DV), (NH * DV // 4) ** -0.5, 0.1875, ((0, 8), (1, 4)))
    gain_mlp = jnp.clip(1.0 + 0.1 * jax.random.normal(arg_keys[15], (D,), jnp.float32), 0.5, 1.5)
    w_gate = normal_values(arg_keys[16], (D, FF), D ** -0.5, 0.125, ((1, 8),))
    w_up = normal_values(arg_keys[17], (D, FF), D ** -0.5, 0.125, ((1, 8),))
    w_down = normal_values(arg_keys[18], (FF, D), (FF // 2) ** -0.5, 0.109375, ((0, 8),))
    doc_lengths = draw_doc_lengths(jax.random.fold_in(arg_keys[21], 71), 0)
    cotangent = normal_values(arg_keys[20], (TOKENS, D), 1.0, 6.0, ((0, 32),))
    return {"block_input": block_input, "gain_attn": gain_attn, "w_query": w_query, "w_key": w_key, "w_value": w_value, "w_gate_out": w_gate_out, "w_decay": w_decay, "w_beta": w_beta, "conv_query": conv_query, "conv_key": conv_key, "conv_value": conv_value, "a_log": a_log, "dt_bias": dt_bias, "out_gain": out_gain, "w_out": w_out, "gain_mlp": gain_mlp, "w_gate": w_gate, "w_up": w_up, "w_down": w_down, "doc_lengths": doc_lengths, "cotangent": cotangent}


EPS = 1e-06
HIGH = lax.Precision.HIGHEST

@jax.custom_vjp
def low(v):
    return lax.optimization_barrier(v.astype(jnp.bfloat16)).astype(jnp.float32)

@jax.custom_vjp
def low_back(v):
    return v

def low_keep(v):
    return (low(v), None)

def low_pass(kept, grad):
    return (grad,)

def back_keep(v):
    return (v, None)

def back_low(kept, grad):
    return (low(grad),)
low.defvjp(low_keep, low_pass)
low_back.defvjp(back_keep, back_low)

def rms_norm(value, gain):
    return value * lax.rsqrt(lax.optimization_barrier(jnp.mean(value * value, axis=-1, keepdims=True)) + EPS) * gain

def unit_rows(value):
    return value * lax.rsqrt(lax.optimization_barrier(jnp.sum(value * value, axis=-1, keepdims=True)) + EPS)

def sequence_tables(doc_lengths, first_row, row_count, block_size):
    padded = (doc_lengths + block_size - 1) // block_size * block_size
    seq_ends = jnp.cumsum(padded).astype(jnp.int32)
    seq_starts = (seq_ends - padded).astype(jnp.int32)
    row_places = (first_row + jnp.arange(row_count, dtype=jnp.int32)).astype(jnp.int32)
    inside_mask = (row_places[:, None] >= seq_starts[None, :]) & (row_places[:, None] < seq_ends[None, :])
    live_mask = jnp.any(inside_mask & (row_places[:, None] < (seq_starts + doc_lengths)[None, :]), axis=1)
    row_start = lax.optimization_barrier(jnp.sum(jnp.where(inside_mask, seq_starts[None, :], 0), axis=1)).astype(jnp.int32)
    block_heads = row_places[::block_size]
    fresh_block = jnp.any(block_heads[:, None] == seq_starts[None, :], axis=1)
    return (live_mask.astype(jnp.float32), row_start, row_places, jnp.where(fresh_block, 0.0, 1.0).astype(jnp.float32))

def short_conv(mixed_rows, rim_rows, conv_weight, row_start, row_places):
    row_count = mixed_rows.shape[0]
    taps_count = conv_weight.shape[0]
    extended = jnp.concatenate([rim_rows, mixed_rows], axis=0)
    running_sum = jnp.zeros_like(mixed_rows)
    for tap_index in range(taps_count):
        reach_back = taps_count - 1 - tap_index
        within = (row_places - reach_back >= row_start).astype(jnp.float32)
        running_sum = running_sum + conv_weight[tap_index] * extended[tap_index:tap_index + row_count] * within[:, None]
    return jax.nn.silu(running_sum)

def split_heads(active, gate_part, a_log, dt_bias, live_rows):
    row_count = active.shape[0]
    head_count = a_log.shape[0]
    key_width = head_count * DK
    value_width = head_count * DV
    queries = low(unit_rows(active[:, :key_width].reshape(row_count, head_count, DK)) * DK ** (-0.5))
    key_rows = low(unit_rows(active[:, key_width:2 * key_width].reshape(row_count, head_count, DK)))
    value_rows = low(active[:, 2 * key_width:].reshape(row_count, head_count, DV))
    beta_rows = jax.nn.sigmoid(gate_part[:, value_width + head_count:]) * live_rows[:, None]
    log_decay = -jnp.exp(a_log) * jax.nn.softplus(gate_part[:, value_width:value_width + head_count] + dt_bias)
    return (queries, key_rows, value_rows, beta_rows, log_decay, gate_part[:, :value_width])

def to_blocks(array, block_size):
    block_count = array.shape[0] // block_size
    shaped = array.reshape((block_count, block_size) + array.shape[1:])
    if array.ndim == 3:
        return shaped.transpose(0, 2, 1, 3)
    return shaped.transpose(0, 2, 1)

def from_blocks(array):
    if array.ndim == 4:
        moved = array.transpose(0, 2, 1, 3)
        return moved.reshape((moved.shape[0] * moved.shape[1],) + moved.shape[2:])
    moved = array.transpose(0, 2, 1)
    return moved.reshape(moved.shape[0] * moved.shape[1], moved.shape[2])

def block_terms(key_rows, value_rows, beta_rows, log_decay, carry_flag):
    block_size = key_rows.shape[1]
    running = jnp.cumsum(log_decay, axis=1)
    row_ids = lax.broadcasted_iota(jnp.int32, (block_size, block_size), 0)
    col_ids = lax.broadcasted_iota(jnp.int32, (block_size, block_size), 1)
    lower_mask = row_ids >= col_ids
    spread = running[:, :, None] - running[:, None, :]
    decay_table = jnp.where(lower_mask, jnp.exp(jnp.where(lower_mask, spread, 0.0)), 0.0)
    opening = carry_flag * jnp.exp(running)
    closing = jnp.exp(running[:, -1:] - running)
    key_inner = jnp.einsum('hik,hjk->hij', key_rows, key_rows, precision=HIGH)
    strict = jnp.where(row_ids > col_ids, beta_rows[:, :, None] * decay_table * key_inner, 0.0)
    system = strict + jnp.eye(block_size, dtype=jnp.float32)
    right_side = jnp.concatenate([beta_rows[:, :, None] * value_rows, (beta_rows * opening)[:, :, None] * key_rows], axis=2)
    solved = jax.scipy.linalg.solve_triangular(system, right_side, lower=True, unit_diagonal=True)
    value_width = value_rows.shape[2]
    return (decay_table, opening, closing, solved[:, :, :value_width], solved[:, :, value_width:])

def block_step(carry_state, queries, key_rows, value_rows, beta_rows, log_decay, carry_flag):
    decay_table, opening, closing, updates, weights = block_terms(key_rows, value_rows, beta_rows, log_decay, carry_flag)
    corrected = updates - jnp.einsum('hck,hvk->hcv', weights, carry_state, precision=HIGH)
    scores = jnp.einsum('hik,hjk->hij', queries, key_rows, precision=HIGH) * decay_table
    outputs = opening[:, :, None] * jnp.einsum('hck,hvk->hcv', queries, carry_state, precision=HIGH)
    outputs = outputs + jnp.einsum('hij,hjv->hiv', scores, corrected, precision=HIGH)
    keyed_rows = closing[:, :, None] * key_rows
    new_state = opening[:, -1][:, None, None] * carry_state + jnp.einsum('hcv,hck->hvk', corrected, keyed_rows, precision=HIGH)
    return (new_state, outputs)

def delta_rule(queries, key_rows, value_rows, beta_rows, log_decay, carry_flags):
    head_count = key_rows.shape[1]
    start_state = jnp.zeros((head_count, DV, DK), jnp.float32)
    step_block = jax.checkpoint(block_step)

    def advance(carry_state, block_item):
        return step_block(carry_state, *block_item)
    final_state, outputs = lax.scan(advance, start_state, (to_blocks(queries, BLOCK), to_blocks(key_rows, BLOCK), to_blocks(value_rows, BLOCK), to_blocks(beta_rows, BLOCK), to_blocks(log_decay, BLOCK), carry_flags))
    return from_blocks(outputs)

def block_forward(input_rows, gain_attn, w_query, w_key, w_value, w_gate_out, w_decay, w_beta, conv_query, conv_key, conv_value, a_log, dt_bias, out_gain, w_out, gain_mlp, w_gate, w_up, w_down, tables):
    live_rows, row_start, row_places, carry_flags = tables
    row_count = input_rows.shape[0]
    head_count = a_log.shape[0]
    normed = low(rms_norm(input_rows, gain_attn))
    mixed_rows = low(low_back(jnp.dot(normed, jnp.concatenate([w_query, w_key, w_value], axis=1), precision=HIGH)))
    gate_part = low_back(jnp.dot(normed, jnp.concatenate([w_gate_out, w_decay, w_beta], axis=1), precision=HIGH))
    conv_weight = jnp.concatenate([conv_query, conv_key, conv_value], axis=1)
    rim_rows = jnp.zeros((CONV - 1, mixed_rows.shape[1]), jnp.float32)
    active = short_conv(mixed_rows, rim_rows, conv_weight, row_start, row_places)
    queries, key_rows, value_rows, beta_rows, log_decay, gate_rows = split_heads(active, gate_part, a_log, dt_bias, live_rows)
    outputs = delta_rule(queries, key_rows, value_rows, beta_rows, log_decay, carry_flags) * live_rows[:, None, None]
    shaped = rms_norm(outputs, out_gain) * jax.nn.silu(gate_rows.reshape(row_count, head_count, DV))
    mixer = low(shaped.reshape(row_count, head_count * DV))
    attention = low_back(jnp.dot(mixer, w_out.T, precision=HIGH))
    residual = input_rows + attention
    normed_mlp = low(rms_norm(residual, gain_mlp))
    gate_up = low_back(jnp.dot(normed_mlp, jnp.concatenate([w_gate, w_up], axis=1), precision=HIGH))
    hidden = low(jax.nn.silu(gate_up[:, :FF]) * gate_up[:, FF:])
    return residual + jnp.dot(hidden, w_down, precision=HIGH)

def reference(block_input, gain_attn, w_query, w_key, w_value, w_gate_out, w_decay, w_beta, conv_query, conv_key, conv_value, a_log, dt_bias, out_gain, w_out, gain_mlp, w_gate, w_up, w_down, doc_lengths, cotangent):
    tables = sequence_tables(doc_lengths, 0, block_input.shape[0], BLOCK)
    params = (block_input.astype(jnp.float32), gain_attn.astype(jnp.float32), w_query.astype(jnp.float32), w_key.astype(jnp.float32), w_value.astype(jnp.float32), w_gate_out.astype(jnp.float32), w_decay.astype(jnp.float32), w_beta.astype(jnp.float32), conv_query.astype(jnp.float32), conv_key.astype(jnp.float32), conv_value.astype(jnp.float32), a_log.astype(jnp.float32), dt_bias.astype(jnp.float32), out_gain.astype(jnp.float32), w_out.astype(jnp.float32), gain_mlp.astype(jnp.float32), w_gate.astype(jnp.float32), w_up.astype(jnp.float32), w_down.astype(jnp.float32))

    def run_block(*values):
        return block_forward(*values, tables)
    result, run_back = jax.vjp(run_block, *params)
    grads = run_back(cotangent.astype(jnp.float32))
    return (result.astype(jnp.bfloat16), grads[0], grads[1], grads[2], grads[3], grads[4], grads[5], grads[6], grads[7], grads[8], grads[9], grads[10], grads[11], grads[12], grads[13], grads[14], grads[15], grads[16], grads[17], grads[18])
```

```python
import functools
import jax
import jax.numpy as jnp
from jax import lax
from jax.experimental import pallas as pl
from jax.experimental.pallas import tpu as pltpu
from jax.sharding import PartitionSpec as P

DK, DV, BLOCK, EPS = 128, 256, 64, 1e-6
BF = jnp.bfloat16
F32 = jnp.float32


def mm(a, b):
    return jnp.dot(a.astype(BF), b.astype(BF), preferred_element_type=F32)


def mm_nt(a, b):
    return lax.dot_general(a.astype(BF), b.astype(BF), (((1,), (1,)), ((), ())), preferred_element_type=F32)


def mm_tn(a, b):
    return lax.dot_general(a.astype(BF), b.astype(BF), (((0,), (0,)), ((), ())), preferred_element_type=F32)


def split(a):
    high = a.astype(BF)
    return high, (a - high.astype(F32)).astype(BF)


def mm_fine(a, b):
    ah, al = split(a)
    bh, bl = split(b)
    return mm(ah, bh) + (mm(ah, bl) + mm(al, bh))


def unit_lower_inverses(systems, rows, cols):
    gap = rows ^ cols
    below = rows > cols
    unit = jnp.where(rows == cols, 1.0, 0.0)
    found = [unit - jnp.where(below & (gap < 2), a, 0.0) for a in systems]
    size = 2
    while size < systems[0].shape[0]:
        mask = below & (gap >= size) & (gap < 2 * size)
        inner = [mm_fine(jnp.where(mask, a, 0.0), t) for a, t in zip(systems, found)]
        found = [t - mm_fine(t, m) for t, m in zip(found, inner)]
        size *= 2
    return found


def block_tables(g_col, g_row, rows, cols):
    lower = rows >= cols
    return jnp.where(lower, jnp.exp(jnp.where(lower, g_col - g_row, 0.0)), 0.0)


def forward_kernel(heads, q_ref, k_ref, v_ref, beta_ref, open_ref, close_ref, gc_ref, gr_ref,
                   o_ref, e_ref, t_ref, z_ref, end_ref, carry):
    step = pl.program_id(0)
    rows = lax.broadcasted_iota(jnp.int32, (BLOCK, BLOCK), 0)
    cols = lax.broadcasted_iota(jnp.int32, (BLOCK, BLOCK), 1)

    @pl.when(step == 0)
    def _():
        unit = (lax.broadcasted_iota(jnp.int32, (DK, DK), 0) == lax.broadcasted_iota(jnp.int32, (DK, DK), 1)).astype(F32)
        for h in range(heads):
            carry[h, :, :DV] = jnp.zeros((DK, DV), F32)
            carry[h, :, DV:] = unit

    tables, systems = [], []
    for h in range(heads):
        k = k_ref[:, h * DK:(h + 1) * DK]
        table = block_tables(gc_ref[:, h:h + 1], gr_ref[0, h:h + 1, :], rows, cols)
        tables.append(table)
        systems.append(jnp.where(rows > cols, beta_ref[:, h:h + 1] * table * mm_nt(k, k), 0.0))
    inverses = unit_lower_inverses(systems, rows, cols)
    for h in range(heads):
        q = q_ref[:, h * DK:(h + 1) * DK]
        k = k_ref[:, h * DK:(h + 1) * DK]
        v = v_ref[:, h * DV:(h + 1) * DV]
        beta, opening, closing = beta_ref[:, h:h + 1], open_ref[:, h:h + 1], close_ref[:, h:h + 1]
        low_t = inverses[h].astype(BF)
        t_ref[0, h] = low_t
        u = mm(low_t, beta * v.astype(F32))
        w = mm(low_t, (beta * opening) * k.astype(F32))
        scores = mm_nt(q, k) * tables[h]
        state = carry[h]
        low_state = state.astype(BF)
        z_ref[0, h] = low_state
        reach = mm(jnp.concatenate([w.astype(BF), (opening * q.astype(F32)).astype(BF)], axis=0), low_state)
        c = jnp.concatenate([u, jnp.zeros((BLOCK, DK), F32)], axis=1) - reach[:BLOCK]
        low_c = c.astype(BF)
        out = reach[BLOCK:] + mm(scores, low_c)
        o_ref[:, h * DV:(h + 1) * DV] = out[:, :DV]
        e_ref[:, h * DK:(h + 1) * DK] = out[:, DV:].astype(BF)
        new = opening[BLOCK - 1:BLOCK] * state + mm_tn(closing * k.astype(F32), low_c)
        carry[h] = new
        end_ref[h] = new


def forward_blocks(q, k, v, beta, opening, closing, g_col, g_row, heads):
    rows = q.shape[0]
    nb = rows // BLOCK
    row = lambda width: pl.BlockSpec((BLOCK, width), lambda i: (i, 0))
    return pl.pallas_call(
        functools.partial(forward_kernel, heads),
        grid=(nb,),
        in_specs=[row(heads * DK), row(heads * DK), row(heads * DV), row(heads), row(heads), row(heads), row(heads),
                  pl.BlockSpec((1, heads, BLOCK), lambda i: (i, 0, 0))],
        out_specs=[row(heads * DV), row(heads * DK),
                   pl.BlockSpec((1, heads, BLOCK, BLOCK), lambda i: (i, 0, 0, 0)),
                   pl.BlockSpec((1, heads, DK, DV + DK), lambda i: (i, 0, 0, 0)),
                   pl.BlockSpec((heads, DK, DV + DK), lambda i: (0, 0, 0))],
        out_shape=[jax.ShapeDtypeStruct((rows, heads * DV), F32), jax.ShapeDtypeStruct((rows, heads * DK), BF),
                   jax.ShapeDtypeStruct((nb, heads, BLOCK, BLOCK), BF),
                   jax.ShapeDtypeStruct((nb, heads, DK, DV + DK), BF),
                   jax.ShapeDtypeStruct((heads, DK, DV + DK), F32)],
        scratch_shapes=[pltpu.VMEM((heads, DK, DV + DK), F32)],
        compiler_params=pltpu.CompilerParams(vmem_limit_bytes=48 * 2**20),
    )(q, k, v, beta, opening, closing, g_col, g_row)


def finish_kernel(heads, o_ref, e_ref, s_ref, gate_ref, live_ref, gain_ref, m_ref):
    live = live_ref[...]
    gain = gain_ref[...]
    for h in range(heads):
        vs = slice(h * DV, (h + 1) * DV)
        y = (o_ref[:, vs] + mm(e_ref[:, h * DK:(h + 1) * DK], s_ref[h])) * live
        r = lax.rsqrt(jnp.mean(y * y, axis=1, keepdims=True) + EPS)
        gate = gate_ref[:, vs]
        m_ref[:, vs] = (y * r * gain * (gate * jax.nn.sigmoid(gate))).astype(BF)


def finish(o, e, entry, gate, live, gain, heads, tile=128):
    rows = o.shape[0]
    row = lambda width: pl.BlockSpec((tile, width), lambda i: (i, 0))
    return pl.pallas_call(
        functools.partial(finish_kernel, heads),
        grid=(rows // tile,),
        in_specs=[row(heads * DV), row(heads * DK), pl.BlockSpec((heads, DK, DV), lambda i: (0, 0, 0)), row(heads * DV),
                  row(1), pl.BlockSpec((1, DV), lambda i: (0, 0))],
        out_specs=row(heads * DV),
        out_shape=jax.ShapeDtypeStruct((rows, heads * DV), BF),
        compiler_params=pltpu.CompilerParams(vmem_limit_bytes=48 * 2**20),
    )(o, e, entry, gate, live, gain)


def unfinish_kernel(heads, o_ref, e_ref, s_ref, gate_ref, live_ref, gain_ref, gm_ref, go_ref, gg_ref, ggain_ref, direct_ref):
    @pl.when(pl.program_id(0) == 0)
    def _():
        ggain_ref[...] = jnp.zeros_like(ggain_ref)
        direct_ref[...] = jnp.zeros_like(direct_ref)

    live = live_ref[...]
    gain = gain_ref[...]
    total = jnp.zeros((1, DV), F32)
    for h in range(heads):
        vs = slice(h * DV, (h + 1) * DV)
        e = e_ref[:, h * DK:(h + 1) * DK]
        y = (o_ref[:, vs] + mm(e, s_ref[h])) * live
        r = lax.rsqrt(jnp.mean(y * y, axis=1, keepdims=True) + EPS)
        gate = gate_ref[:, vs]
        sig = jax.nn.sigmoid(gate)
        act = gate * sig
        gm = gm_ref[:, vs]
        unit = y * r
        gn = gm * act
        total = total + jnp.sum(gn * unit, axis=0, keepdims=True)
        gn = gn * gain
        gg_ref[:, vs] = (gm * unit * gain * (sig * (1.0 + gate * (1.0 - sig)))).astype(BF)
        go = (r * (gn - unit * jnp.mean(gn * unit, axis=1, keepdims=True)) * live).astype(BF)
        go_ref[:, vs] = go
        direct_ref[h] += mm_tn(e, go)
    ggain_ref[...] += total


def unfinish(o, e, entry, gate, live, gain, gm, heads, tile=128):
    rows = o.shape[0]
    row = lambda width: pl.BlockSpec((tile, width), lambda i: (i, 0))
    return pl.pallas_call(
        functools.partial(unfinish_kernel, heads),
        grid=(rows // tile,),
        in_specs=[row(heads * DV), row(heads * DK), pl.BlockSpec((heads, DK, DV), lambda i: (0, 0, 0)), row(heads * DV),
                  row(1), pl.BlockSpec((1, DV), lambda i: (0, 0)), row(heads * DV)],
        out_specs=[row(heads * DV), row(heads * DV), pl.BlockSpec((1, DV), lambda i: (0, 0)),
                   pl.BlockSpec((heads, DK, DV), lambda i: (0, 0, 0))],
        out_shape=[jax.ShapeDtypeStruct((rows, heads * DV), BF), jax.ShapeDtypeStruct((rows, heads * DV), BF),
                   jax.ShapeDtypeStruct((1, DV), F32), jax.ShapeDtypeStruct((heads, DK, DV), F32)],
        compiler_params=pltpu.CompilerParams(vmem_limit_bytes=48 * 2**20),
    )(o, e, entry, gate, live, gain, gm)


def backward_kernel(heads, q_ref, k_ref, v_ref, beta_ref, open_ref, close_ref, gc_ref, gr_ref, t_ref, z_ref, go_ref,
                    s_ref, exit_ref, dq_ref, dk_ref, dv_ref, db_ref, dg_ref, carry):
    rows = lax.broadcasted_iota(jnp.int32, (BLOCK, BLOCK), 0)
    cols = lax.broadcasted_iota(jnp.int32, (BLOCK, BLOCK), 1)
    last = lax.broadcasted_iota(jnp.int32, (BLOCK, 1), 0) == BLOCK - 1

    @pl.when(pl.program_id(0) == 0)
    def _():
        carry[...] = exit_ref[...]

    for h in range(heads):
        q = q_ref[:, h * DK:(h + 1) * DK]
        k = k_ref[:, h * DK:(h + 1) * DK]
        v = v_ref[:, h * DV:(h + 1) * DV]
        qf, kf, vf = q.astype(F32), k.astype(F32), v.astype(F32)
        beta, opening, closing = beta_ref[:, h:h + 1], open_ref[:, h:h + 1], close_ref[:, h:h + 1]
        gamma = opening[BLOCK - 1:BLOCK]
        table = block_tables(gc_ref[:, h:h + 1], gr_ref[0, h:h + 1, :], rows, cols)
        strict = rows > cols
        kk = mm_nt(k, k)
        scores = mm_nt(q, k) * table
        low_t = t_ref[0, h]
        u = mm(low_t, beta * vf)
        w = mm(low_t, (beta * opening) * kf)
        low_w = w.astype(BF)
        state = z_ref[0, h, :, :DV].astype(F32) + mm(z_ref[0, h, :, DV:], s_ref[h])
        low_s = state.astype(BF)
        c = u - mm(low_w, low_s)
        low_c = c.astype(BF)
        go = go_ref[:, h * DV:(h + 1) * DV]
        g = carry[h]
        low_g = g.astype(BF)
        low_ck = (closing * kf).astype(BF)
        low_oq = (opening * qf).astype(BF)
        dc = mm_tn(scores, go) + mm(low_ck, low_g)
        low_dc = dc.astype(BF)
        both = jnp.concatenate([go, low_dc], axis=0)
        carry[h] = gamma * g + mm_tn(jnp.concatenate([low_oq, -low_w], axis=0), both)
        dkeyed = mm_nt(low_c, low_g)
        dgamma = jnp.sum(jnp.sum(state * g, axis=1, keepdims=True), axis=0, keepdims=True)
        dscore = jnp.where(rows >= cols, mm_nt(go, low_c), 0.0)
        back = mm_nt(both, low_s)
        doq, dw = back[:BLOCK], -back[BLOCK:]
        drv = mm_tn(low_t, low_dc)
        drw = mm_tn(low_t, dw)
        low_drv, low_drw = drv.astype(BF), drw.astype(BF)
        da = jnp.where(strict, -(mm_nt(low_drv, u) + mm_nt(low_drw, low_w)), 0.0)
        dat = da * table
        dkk = (beta * dat).astype(BF)
        dqk = (dscore * table).astype(BF)
        dq_ref[:, h * DK:(h + 1) * DK] = opening * doq + mm(dqk, k)
        dk_ref[:, h * DK:(h + 1) * DK] = (mm_tn(dqk, q) + mm(dkk, k) + mm_tn(dkk, k) + closing * dkeyed
                                          + (beta * opening) * drw)
        dv_ref[:, h * DV:(h + 1) * DV] = beta * drv
        rk = jnp.sum(drw * kf, axis=1, keepdims=True)
        atk = dat * kk
        db_ref[:, h:h + 1] = (jnp.sum(drv * vf, axis=1, keepdims=True) + opening * rk
                              + jnp.sum(atk, axis=1, keepdims=True))
        dopen = opening * (jnp.sum(doq * qf, axis=1, keepdims=True) + beta * rk)
        dclose = closing * jnp.sum(dkeyed * kf, axis=1, keepdims=True)
        e = dscore * scores + beta * atk
        by_col = lax.dot_general(e, jnp.ones((BLOCK, 8), F32), (((0,), (0,)), ((), ())),
                                 precision=lax.Precision.HIGHEST, preferred_element_type=F32)[:, :1]
        dg = jnp.sum(e, axis=1, keepdims=True) - by_col + dopen - dclose
        dg = dg + jnp.where(last, jnp.sum(dclose, axis=0, keepdims=True) + dgamma * gamma, 0.0)
        dg_ref[:, h:h + 1] = dg


def backward_blocks(q, k, v, beta, opening, closing, g_col, g_row, t, z, go, entry, leaving, heads):
    rows = q.shape[0]
    nb = rows // BLOCK
    row = lambda width: pl.BlockSpec((BLOCK, width), lambda i: (nb - 1 - i, 0))
    whole = pl.BlockSpec((heads, DK, DV), lambda i: (0, 0, 0))
    return pl.pallas_call(
        functools.partial(backward_kernel, heads),
        grid=(nb,),
        in_specs=[row(heads * DK), row(heads * DK), row(heads * DV), row(heads), row(heads), row(heads), row(heads),
                  pl.BlockSpec((1, heads, BLOCK), lambda i: (nb - 1 - i, 0, 0)),
                  pl.BlockSpec((1, heads, BLOCK, BLOCK), lambda i: (nb - 1 - i, 0, 0, 0)),
                  pl.BlockSpec((1, heads, DK, DV + DK), lambda i: (nb - 1 - i, 0, 0, 0)),
                  row(heads * DV), whole, whole],
        out_specs=[row(heads * DK), row(heads * DK), row(heads * DV), row(heads), row(heads)],
        out_shape=[jax.ShapeDtypeStruct((rows, heads * DK), F32), jax.ShapeDtypeStruct((rows, heads * DK), F32),
                   jax.ShapeDtypeStruct((rows, heads * DV), F32), jax.ShapeDtypeStruct((rows, heads), F32),
                   jax.ShapeDtypeStruct((rows, heads), F32)],
        scratch_shapes=[pltpu.VMEM((heads, DK, DV), F32)],
        compiler_params=pltpu.CompilerParams(vmem_limit_bytes=48 * 2**20),
    )(q, k, v, beta, opening, closing, g_col, g_row, t, z, go, entry, leaving)


def block_decays(log_decay, flags, heads):
    rows = log_decay.shape[0]
    nb = rows // BLOCK
    blocked = log_decay.reshape(nb, BLOCK, heads)
    run = jnp.cumsum(blocked, axis=1)
    opening = flags[:, None, None] * jnp.exp(run)
    closing = jnp.exp(run[:, -1:] - run)
    flat = lambda a: a.reshape(rows, heads)
    return flat(opening), flat(closing), flat(run), run.transpose(0, 2, 1)


CONV = 4


def rms_norm(value, gain):
    return value * lax.rsqrt(jnp.mean(value * value, axis=-1, keepdims=True) + EPS) * gain


def unit_rows(value):
    return value * lax.rsqrt(jnp.sum(value * value, axis=-1, keepdims=True) + EPS)


def rounded(value):
    return lax.optimization_barrier(value.astype(BF)).astype(F32)


def from_behind(value, axis, steps):
    count = lax.axis_size(axis)
    initial, last = (max(0, -steps), min(count, count - steps))
    return lax.ppermute(value, axis, [(source, source + steps) for source in range(initial, last)])


def turn(value, k):
    count = lax.axis_size("wide")
    if k % (count // 2) == 0:
        return value
    return lax.ppermute(value, "wide", [(w, (w + 2 * k) % count) for w in range(count)])


def across(value, axis, bit):
    return lax.ppermute(value, axis, [(i, i ^ bit) for i in range(lax.axis_size(axis))])


def gather_wide(value):
    places = lax.axis_size("wide") // 2
    own = [turn(value, k) for k in range(places)]
    return [piece for part in own for piece in (part, across(part, "wide", 1))]


def scatter_wide(parts):
    places = lax.axis_size("wide") // 2
    own = [(parts[2 * k].astype(F32) + across(parts[2 * k + 1], "wide", 1).astype(F32)) for k in range(places)]
    total = own[0]
    for k in range(1, places):
        total = total + turn(own[k].astype(BF), places - k).astype(F32)
    return total


def relative(value, axis):
    count = lax.axis_size("wide")
    me = lax.axis_index("wide")
    place, side = me // 2, me % 2
    size = value.shape[axis] // count
    pieces = [
        lax.dynamic_slice_in_dim(value, (2 * ((place - k) % (count // 2)) + (side ^ s)) * size, size, axis)
        for k in range(count // 2) for s in range(2)
    ]
    return jnp.concatenate(pieces, axis=axis)


def gather_narrow(value):
    near = across(value, "narrow", 1)
    return [value, near, across(value, "narrow", 2), across(near, "narrow", 2)]


def scatter_narrow(parts):
    first = parts[0].astype(F32) + across(parts[1], "narrow", 1).astype(F32)
    second = (parts[2].astype(F32) + across(parts[3], "narrow", 1).astype(F32)).astype(parts[2].dtype)
    return first + across(second, "narrow", 2).astype(F32)


def blocks_of(value, axis, count):
    me = lax.axis_index("narrow")
    size = value.shape[axis] // count
    return [lax.dynamic_slice_in_dim(value, (me ^ j) * size, size, axis) for j in range(count)]


def placed(pieces, axis):
    me = lax.axis_index("narrow")
    size = pieces[0].shape[axis]
    shape = list(pieces[0].shape)
    shape[axis] = size * len(pieces)
    whole = jnp.zeros(shape, pieces[0].dtype)
    for j, piece in enumerate(pieces):
        whole = lax.dynamic_update_slice_in_dim(whole, piece, (me ^ j) * size, axis)
    return whole


def sum_all(value, axis):
    bit = 1
    while bit < lax.axis_size(axis):
        value = value + across(value, axis, bit)
        bit *= 2
    return value


def sequence_tables(doc_lengths, first_row, row_count, block_size):
    padded = (doc_lengths + block_size - 1) // block_size * block_size
    seq_ends = jnp.cumsum(padded)
    seq_starts = seq_ends - padded
    row_places = first_row + jnp.arange(row_count, dtype=jnp.int32)
    inside_mask = (row_places[:, None] >= seq_starts[None, :]) & (row_places[:, None] < seq_ends[None, :])
    live_mask = jnp.any(inside_mask & (row_places[:, None] < (seq_starts + doc_lengths)[None, :]), axis=1)
    row_start = jnp.sum(jnp.where(inside_mask, seq_starts[None, :], 0), axis=1)
    block_heads = row_places[::block_size]
    fresh_block = jnp.any(block_heads[:, None] == seq_starts[None, :], axis=1)
    return live_mask.astype(F32), row_start, row_places, jnp.where(fresh_block, 0.0, 1.0).astype(F32)


def short_conv(mixed_rows, rim_rows, conv_weight, row_start, row_places):
    row_count = mixed_rows.shape[0]
    taps_count = conv_weight.shape[0]
    extended = jnp.concatenate([rim_rows, mixed_rows], axis=0)
    running_sum = jnp.zeros_like(mixed_rows)
    for tap_index in range(taps_count):
        reach_back = taps_count - 1 - tap_index
        within = (row_places - reach_back >= row_start).astype(F32)
        running_sum = running_sum + conv_weight[tap_index] * extended[tap_index:tap_index + row_count] * within[:, None]
    return jax.nn.silu(running_sum)


def split_heads(active, decay_part, beta_part, a_log, dt_bias, live_rows):
    row_count = active.shape[0]
    head_count = a_log.shape[0]
    key_width = head_count * DK
    queries = unit_rows(active[:, :key_width].reshape(row_count, head_count, DK)) * DK ** (-0.5)
    key_rows = unit_rows(active[:, key_width:2 * key_width].reshape(row_count, head_count, DK))
    value_rows = active[:, 2 * key_width:]
    beta_rows = jax.nn.sigmoid(beta_part) * live_rows[:, None]
    log_decay = -jnp.exp(a_log) * jax.nn.softplus(decay_part + dt_bias)
    flat = lambda a: a.reshape(row_count, key_width)
    return flat(queries), flat(key_rows), value_rows, beta_rows, log_decay


def contract_rows(left, right):
    return lax.dot_general(left, right, (((0,), (0,)), ((), ())), preferred_element_type=F32)


def contract_cols(left, right):
    return lax.dot_general(left, right, (((1,), (1,)), ((), ())), preferred_element_type=F32)


def heads_dot(left, right):
    return jnp.einsum("hij,hjk->hik", left, right, preferred_element_type=F32)


def heads_dot_t(left, right):
    return jnp.einsum("hji,hjk->hik", left, right, preferred_element_type=F32)


def pick(value, side):
    half = value.shape[0] // 2
    return lax.dynamic_slice_in_dim(value, side * half, half, 0)


def join_halves(own, other, side):
    return jnp.concatenate([jnp.where(side == 0, own, other), jnp.where(side == 0, other, own)], axis=0)


def entering(end, place, side):
    places = lax.axis_size("wide") // 2
    mine = end.astype(BF)
    theirs = across(mine, "wide", 1)
    early = jnp.where(side == 0, mine, theirs)
    late = jnp.where(side == 0, theirs, mine)
    early_half, late_half = pick(early, side), pick(late, side)
    joined = heads_dot(late_half[:, :, DV:], early_half)
    joined = jnp.concatenate([joined[:, :, :DV] + late_half[:, :, :DV].astype(F32), joined[:, :, DV:]], axis=2).astype(BF)
    turned = [turn(joined, k) for k in range(places)]
    state = jnp.zeros(joined.shape[:2] + (DV,), F32)
    for k in range(places - 1, 0, -1):
        longer = heads_dot(turned[k][:, :, DV:], state.astype(BF)) + turned[k][:, :, :DV].astype(F32)
        state = jnp.where(place >= k, longer, state)
    state = state.astype(BF)
    state = join_halves(state, across(state, "wide", 1), side)
    after = (heads_dot(theirs[:, :, DV:], state) + theirs[:, :, :DV].astype(F32)).astype(BF)
    entry = jnp.where(side == 0, state, after)
    return entry, (mine[:, :, DV:], theirs[:, :, DV:], [t[:, :, DV:] for t in turned])


def leaving(direct, maps, place, side):
    mine_map, their_map, turned_maps = maps
    places = len(turned_maps)
    mine = direct.astype(BF)
    theirs = across(mine, "wide", 1)
    early = jnp.where(side == 0, mine, theirs)
    late = jnp.where(side == 0, theirs, mine)
    early_map = jnp.where(side == 0, mine_map, their_map)
    joined = (heads_dot_t(pick(early_map, side), pick(late, side)) + pick(early, side).astype(F32)).astype(BF)
    turned = [turn(joined, k) for k in range(places)]
    state = jnp.zeros(joined.shape, F32)
    for k in range(1, places):
        longer = heads_dot_t(turned_maps[k], state.astype(BF)) + turned[k].astype(F32)
        state = jnp.where(k > place, longer, state)
    state = state.astype(BF)
    state = join_halves(state, across(state, "wide", 1), side)
    before = (heads_dot_t(their_map, state) + theirs.astype(F32)).astype(BF)
    return jnp.where(side == 1, state, before).astype(F32)


def shards(block_input, gain_attn, w_query, w_key, w_value, w_gate_out, w_decay, w_beta, conv_query, conv_key,
           conv_value, a_log, dt_bias, out_gain, w_out, gain_mlp, w_gate, w_up, w_down, doc_lengths, cotangent):
    row_count = block_input.shape[0]
    quarter = cotangent.shape[0]
    heads = a_log.shape[0]
    narrow = lax.axis_size("narrow")
    wide_index = lax.axis_index("wide")
    place, side = wide_index // 2, wide_index % 2
    live_rows, row_start, row_places, flags = sequence_tables(doc_lengths, wide_index * row_count, row_count, BLOCK)
    live_col = live_rows[:, None]
    gain_row = out_gain[None, :]
    key_width, value_width = heads * DK, heads * DV

    w_first = jnp.concatenate([w_query, w_key, w_value, w_decay, w_beta], axis=1)
    first = jnp.concatenate(gather_wide(w_first), axis=0)
    gate_weight = jnp.concatenate(gather_wide(w_gate_out), axis=0)
    out_weight = jnp.concatenate(gather_wide(w_out), axis=0)
    cot_parts = gather_wide(cotangent)

    input_rel = relative(block_input, 1).astype(F32)
    gain_rel = relative(gain_attn, 0)
    normed, attn_norm_back = jax.vjp(rms_norm, input_rel, gain_rel)
    normed_low = normed.astype(BF)
    projected = jnp.dot(normed_low, first, preferred_element_type=F32)
    mixed_width = 2 * key_width + value_width
    mixed_low = projected[:, :mixed_width].astype(BF)
    decay_part = projected[:, mixed_width:mixed_width + heads]
    beta_part = projected[:, mixed_width + heads:]
    rim_rows = from_behind(mixed_low[row_count - (CONV - 1):], "wide", 1)
    conv_weight = jnp.concatenate([conv_query, conv_key, conv_value], axis=1)

    def prepare(mixed_rows, rim_in, decay_in, beta_in, conv_in, a_log_in, dt_in):
        active = short_conv(mixed_rows, rim_in, conv_in, row_start, row_places)
        return split_heads(active, decay_in, beta_in, a_log_in, dt_in, live_rows)

    prepared, prepare_back = jax.vjp(prepare, mixed_low.astype(F32), rim_rows.astype(F32), decay_part, beta_part,
                                     conv_weight, a_log, dt_bias)
    queries, keys, values = [a.astype(BF) for a in prepared[:3]]
    beta_rows, log_decay = prepared[3:]
    opening, closing, run_col, run_row = block_decays(log_decay, flags, heads)
    local_out, reach, inverses, states, end = forward_blocks(queries, keys, values, beta_rows, opening, closing, run_col,
                                                             run_row, heads)
    entry, maps = entering(end, place, side)
    gate_rows = jnp.dot(normed_low, gate_weight, preferred_element_type=F32)
    mixer_low = finish(local_out, reach, entry, gate_rows, live_col, gain_row, heads)
    head_part = contract_cols(mixer_low, out_weight)
    own_rel = scatter_narrow(blocks_of(head_part, 0, narrow))
    own_rows = relative(own_rel, 1) + lax.dynamic_slice_in_dim(
        block_input, lax.axis_index("narrow") * quarter, quarter, 0).astype(F32)
    mlp_normed, mlp_norm_back = jax.vjp(rms_norm, own_rows, gain_mlp)
    mlp_low = mlp_normed.astype(BF)
    gathered_rows = jnp.concatenate(gather_wide(mlp_low), axis=0)
    gathered_cot = jnp.concatenate(cot_parts, axis=0)
    gate_pre = jnp.dot(gathered_rows, w_gate, preferred_element_type=F32)
    up_pre = jnp.dot(gathered_rows, w_up, preferred_element_type=F32)
    gate_sig = jax.nn.sigmoid(gate_pre)
    gate_act = gate_pre * gate_sig
    hidden_low = (gate_act * up_pre).astype(BF)
    grad_hidden = contract_cols(gathered_cot, w_down)
    grad_gate_low = (grad_hidden * up_pre * gate_sig * (1.0 + gate_pre * (1.0 - gate_sig))).astype(BF)
    grad_up_low = (grad_hidden * gate_act).astype(BF)
    grad_rows = (contract_cols(grad_gate_low, w_gate) + contract_cols(grad_up_low, w_up)).astype(BF)
    row_blocks = lambda a: [a[j * quarter:(j + 1) * quarter] for j in range(a.shape[0] // quarter)]
    grad_mlp_normed = scatter_wide(row_blocks(grad_rows))
    grad_own_norm, grad_gain_mlp = mlp_norm_back(grad_mlp_normed)
    grad_own = cotangent.astype(F32) + grad_own_norm
    grad_attn_low = placed(gather_narrow(grad_own.astype(BF)), 0)
    grad_attn_rel = relative(grad_attn_low, 1)

    down_rows = jnp.dot(hidden_low, w_down, preferred_element_type=F32).astype(BF)
    output = (own_rows + scatter_wide(row_blocks(down_rows))).astype(BF)
    grad_w_down = contract_rows(hidden_low, gathered_cot).astype(BF)
    grad_w_gate = contract_rows(gathered_rows, grad_gate_low).astype(BF)
    grad_w_up = contract_rows(gathered_rows, grad_up_low).astype(BF)
    share_gate = scatter_narrow(blocks_of(grad_w_gate, 0, narrow))
    share_up = scatter_narrow(blocks_of(grad_w_up, 0, narrow))
    share_down = scatter_narrow(blocks_of(grad_w_down, 1, narrow))

    grad_mixer = jnp.dot(grad_attn_rel, out_weight, preferred_element_type=F32)
    grad_outputs, grad_gate_rows, grad_out_gain, direct = unfinish(local_out, reach, entry, gate_rows, live_col, gain_row,
                                                                   grad_mixer, heads)
    exit_grad = leaving(direct, maps, place, side)
    grad_w_out = contract_rows(grad_attn_rel, mixer_low).astype(BF)
    grad_w_gate_out = contract_rows(normed_low, grad_gate_rows).astype(BF)
    wide_count = lax.axis_size("wide")
    depth = w_query.shape[0]
    depth_blocks = lambda a: [a[j * depth:(j + 1) * depth] for j in range(wide_count)]
    sum_w_out = scatter_wide(depth_blocks(grad_w_out))
    sum_w_gate_out = scatter_wide(depth_blocks(grad_w_gate_out))

    grad_q, grad_k, grad_v, grad_beta, grad_run = backward_blocks(queries, keys, values, beta_rows, opening, closing,
                                                                  run_col, run_row, inverses, states, grad_outputs,
                                                                  entry, exit_grad, heads)
    nb = row_count // BLOCK
    grad_decay = lax.cumsum(grad_run.reshape(nb, BLOCK, heads), axis=1, reverse=True).reshape(row_count, heads)
    grad_mixed, grad_rim, grad_decay_part, grad_beta_part, grad_conv, grad_a_log, grad_dt = prepare_back(
        (grad_q, grad_k, grad_v, grad_beta, grad_decay))
    grad_next = from_behind(grad_rim, "wide", -1)
    grad_mixed = grad_mixed.at[row_count - (CONV - 1):].add(grad_next)
    grad_first = jnp.concatenate([grad_mixed, grad_decay_part, grad_beta_part], axis=1).astype(BF)
    grad_projection = contract_rows(normed_low, grad_first).astype(BF)
    grad_normed = contract_cols(grad_first, first) + contract_cols(grad_gate_rows, gate_weight)
    grad_input_part, grad_gain_rel = attn_norm_back(grad_normed)
    sum_first = scatter_wide(depth_blocks(grad_projection))
    bounds = [0, key_width, 2 * key_width, mixed_width, mixed_width + heads, mixed_width + 2 * heads]
    sums = [sum_first[:, bounds[i]:bounds[i + 1]] for i in range(5)]
    grad_input = relative(scatter_narrow(blocks_of(grad_input_part.astype(BF), 0, narrow)), 1) + grad_own

    columns = mixed_width
    head_sums = jnp.concatenate([grad_conv.reshape(-1), grad_a_log, grad_dt])
    whole_sums = jnp.concatenate([relative(grad_gain_rel, 0), grad_gain_mlp, grad_out_gain[0]])
    small = sum_all(jnp.concatenate([head_sums, whole_sums]), "wide")
    parts = small[:head_sums.shape[0]]
    whole_sums = sum_all(small[head_sums.shape[0]:], "narrow")
    every = placed([p[None] for p in gather_narrow(parts)], 0)
    conv_all = every[:, :CONV * columns].reshape(narrow, CONV, columns).transpose(1, 0, 2)
    conv_parts = [conv_all[:, :, lo:hi].reshape(CONV, -1) for lo, hi in
                  ((0, key_width), (key_width, 2 * key_width), (2 * key_width, columns))]
    d_model = gain_attn.shape[0]
    return (
        output, grad_input, whole_sums[:d_model], sums[0], sums[1], sums[2], sum_w_gate_out, sums[3], sums[4],
        conv_parts[0], conv_parts[1], conv_parts[2],
        every[:, CONV * columns:CONV * columns + heads].reshape(-1), every[:, CONV * columns + heads:].reshape(-1),
        whole_sums[2 * d_model:], sum_w_out, whole_sums[d_model:2 * d_model], share_gate, share_up, share_down,
    )


def solution(mesh):
    both = P("wide", "narrow")
    rows = P(("wide", "narrow"), None)
    return jax.shard_map(
        shards,
        mesh=mesh,
        in_specs=(P("wide", None), P(), both, both, both, both, both, both, P(None, "narrow"), P(None, "narrow"),
                  P(None, "narrow"), P("narrow"), P("narrow"), P(), both, P(), P(None, "wide"), P(None, "wide"),
                  P("wide", None), P(), rows),
        out_specs=(rows, rows, P(), both, both, both, both, both, both, P(), P(), P(), P(), P(), P(), both, P(),
                   P("narrow", "wide"), P("narrow", "wide"), both),
        check_vma=False,
    )
```

```python
import functools
import jax
import jax.numpy as jnp
from jax import lax
from jax.experimental import pallas as pl
from jax.experimental.pallas import tpu as pltpu
from jax.sharding import PartitionSpec as P

DK, DV, BLOCK, EPS = 128, 256, 64, 1e-6
BF = jnp.bfloat16
F32 = jnp.float32


def mm(a, b):
    return jnp.dot(a.astype(BF), b.astype(BF), preferred_element_type=F32)


def mm_nt(a, b):
    return lax.dot_general(a.astype(BF), b.astype(BF), (((1,), (1,)), ((), ())), preferred_element_type=F32)


def mm_tn(a, b):
    return lax.dot_general(a.astype(BF), b.astype(BF), (((0,), (0,)), ((), ())), preferred_element_type=F32)


def split(a):
    high = a.astype(BF)
    return high, (a - high.astype(F32)).astype(BF)


def mm_fine(a, b):
    ah, al = split(a)
    bh, bl = split(b)
    return mm(ah, bh) + (mm(ah, bl) + mm(al, bh))


def unit_lower_inverses(systems, rows, cols):
    gap = rows ^ cols
    below = rows > cols
    unit = jnp.where(rows == cols, 1.0, 0.0)
    found = [unit - jnp.where(below & (gap < 2), a, 0.0) for a in systems]
    size = 2
    while size < systems[0].shape[0]:
        mask = below & (gap >= size) & (gap < 2 * size)
        inner = [mm_fine(jnp.where(mask, a, 0.0), t) for a, t in zip(systems, found)]
        found = [t - mm_fine(t, m) for t, m in zip(found, inner)]
        size *= 2
    return found


def block_tables(g_col, g_row, rows, cols):
    lower = rows >= cols
    return jnp.where(lower, jnp.exp(jnp.where(lower, g_col - g_row, 0.0)), 0.0)


def shifted(rows, before, back):
    if back == 0:
        return rows
    return jnp.concatenate([before[8 - back:], rows[:rows.shape[0] - back]], axis=0)


def conv_rows(rows, before, taps):
    count = taps.shape[0]
    total = taps[count - 1:count] * rows
    for back in range(1, count):
        total = total + taps[count - 1 - back:count - back] * shifted(rows, before, back)
    return total


def head_slices(heads, h):
    key = heads * DK
    return slice(h * DK, (h + 1) * DK), slice(key + h * DK, key + (h + 1) * DK), slice(2 * key + h * DV, 2 * key + (h + 1) * DV)


def unit_factor(rows):
    return lax.rsqrt(jnp.sum(rows * rows, axis=1, keepdims=True) + EPS)


def exact_tn(a, b):
    return lax.dot_general(a, b, (((0,), (0,)), ((), ())), precision=lax.Precision.HIGHEST, preferred_element_type=F32)


def softplus(x):
    return jnp.maximum(x, 0.0) + jnp.log(1.0 + jnp.exp(-jnp.abs(x)))


def decay_tables(heads, small, a_log, dt_bias, live, rows, cols):
    speed = -jnp.exp(a_log)
    biased = small[:, :heads] + dt_bias
    log_decay = speed * softplus(biased)
    sig = jax.nn.sigmoid(small[:, heads:2 * heads])
    upto = jnp.where(rows <= cols, 1.0, 0.0)
    run = exact_tn(upto, log_decay)
    run_row = exact_tn(log_decay, upto)
    return speed, biased, log_decay, sig, sig * live, run, run_row


def forward_kernel(heads, flag_ref, x_ref, rim_ref, taps_ref, small_ref, live_ref, alog_ref, dt_ref,
                   o_ref, e_ref, t_ref, z_ref, end_ref, carry, before_ref):
    step = pl.program_id(0)
    rows = lax.broadcasted_iota(jnp.int32, (BLOCK, BLOCK), 0)
    cols = lax.broadcasted_iota(jnp.int32, (BLOCK, BLOCK), 1)
    flag = flag_ref[step]

    @pl.when(step == 0)
    def _():
        before_ref[...] = rim_ref[8:16, :].astype(F32)
        unit = jnp.where(lax.broadcasted_iota(jnp.int32, (DK, DK), 0) == lax.broadcasted_iota(jnp.int32, (DK, DK), 1), 1.0, 0.0)
        for h in range(heads):
            carry[h, :, :DV] = jnp.zeros((DK, DV), F32)
            carry[h, :, DV:] = unit

    _, _, _, _, betas, run, run_row = decay_tables(heads, small_ref[...], alog_ref[...], dt_ref[...], live_ref[...], rows, cols)
    openings = flag * jnp.exp(run)
    closings = jnp.exp(run[BLOCK - 1:BLOCK] - run)

    def active(columns):
        c = conv_rows(x_ref[:, columns].astype(F32), before_ref[:, columns] * flag, taps_ref[:, columns])
        return c * jax.nn.sigmoid(c)

    tables, systems, parts = [], [], []
    for h in range(heads):
        qs, ks, vs = head_slices(heads, h)
        q, k, v = active(qs), active(ks), active(vs).astype(BF)
        q = (q * unit_factor(q) * DK ** (-0.5)).astype(BF)
        k = (k * unit_factor(k)).astype(BF)
        parts.append((q, k, v))
        table = block_tables(run[:, h:h + 1], run_row[h:h + 1, :], rows, cols)
        tables.append(table)
        systems.append(jnp.where(rows > cols, betas[:, h:h + 1] * table * mm_nt(k, k), 0.0))
    before_ref[...] = x_ref[BLOCK - 8:, :].astype(F32)
    inverses = unit_lower_inverses(systems, rows, cols)
    for h in range(heads):
        q, k, v = parts[h]
        beta, opening, closing = betas[:, h:h + 1], openings[:, h:h + 1], closings[:, h:h + 1]
        low_t = inverses[h].astype(BF)
        t_ref[0, h] = low_t
        u = mm(low_t, beta * v.astype(F32))
        w = mm(low_t, (beta * opening) * k.astype(F32))
        scores = mm_nt(q, k) * tables[h]
        state = carry[h]
        low_state = state.astype(BF)
        z_ref[0, h] = low_state
        reach = mm(jnp.concatenate([w.astype(BF), (opening * q.astype(F32)).astype(BF)], axis=0), low_state)
        c = jnp.concatenate([u, jnp.zeros((BLOCK, DK), F32)], axis=1) - reach[:BLOCK]
        low_c = c.astype(BF)
        out = reach[BLOCK:] + mm(scores, low_c)
        o_ref[:, h * DV:(h + 1) * DV] = out[:, :DV]
        e_ref[:, h * DK:(h + 1) * DK] = out[:, DV:].astype(BF)
        new = opening[BLOCK - 1:BLOCK] * state + mm_tn(closing * k.astype(F32), low_c)
        carry[h] = new
        end_ref[h] = new


def finish_kernel(heads, o_ref, e_ref, s_ref, gate_ref, live_ref, gain_ref, m_ref):
    live = live_ref[...]
    gain = gain_ref[...]
    for h in range(heads):
        vs = slice(h * DV, (h + 1) * DV)
        y = (o_ref[:, vs] + mm(e_ref[:, h * DK:(h + 1) * DK], s_ref[h])) * live
        r = lax.rsqrt(jnp.mean(y * y, axis=1, keepdims=True) + EPS)
        gate = gate_ref[:, vs]
        m_ref[:, vs] = (y * r * gain * (gate * jax.nn.sigmoid(gate))).astype(BF)


def finish(o, e, entry, gate, live, gain, heads, tile=128):
    rows = o.shape[0]
    row = lambda width: pl.BlockSpec((tile, width), lambda i: (i, 0))
    return pl.pallas_call(
        functools.partial(finish_kernel, heads),
        grid=(rows // tile,),
        in_specs=[row(heads * DV), row(heads * DK), pl.BlockSpec((heads, DK, DV), lambda i: (0, 0, 0)), row(heads * DV),
                  row(1), pl.BlockSpec((1, DV), lambda i: (0, 0))],
        out_specs=row(heads * DV),
        out_shape=jax.ShapeDtypeStruct((rows, heads * DV), BF),
        compiler_params=pltpu.CompilerParams(vmem_limit_bytes=48 * 2**20),
    )(o, e, entry, gate, live, gain)


def unfinish_kernel(heads, o_ref, e_ref, s_ref, gate_ref, live_ref, gain_ref, gm_ref, go_ref, gg_ref, ggain_ref, direct_ref):
    @pl.when(pl.program_id(0) == 0)
    def _():
        ggain_ref[...] = jnp.zeros_like(ggain_ref)
        direct_ref[...] = jnp.zeros_like(direct_ref)

    live = live_ref[...]
    gain = gain_ref[...]
    total = jnp.zeros((1, DV), F32)
    for h in range(heads):
        vs = slice(h * DV, (h + 1) * DV)
        e = e_ref[:, h * DK:(h + 1) * DK]
        y = (o_ref[:, vs] + mm(e, s_ref[h])) * live
        r = lax.rsqrt(jnp.mean(y * y, axis=1, keepdims=True) + EPS)
        gate = gate_ref[:, vs]
        sig = jax.nn.sigmoid(gate)
        act = gate * sig
        gm = gm_ref[:, vs]
        unit = y * r
        gn = gm * act
        total = total + jnp.sum(gn * unit, axis=0, keepdims=True)
        gn = gn * gain
        gg_ref[:, vs] = (gm * unit * gain * (sig * (1.0 + gate * (1.0 - sig)))).astype(BF)
        go = (r * (gn - unit * jnp.mean(gn * unit, axis=1, keepdims=True)) * live).astype(BF)
        go_ref[:, vs] = go
        direct_ref[h] += mm_tn(e, go)
    ggain_ref[...] += total


def unfinish(o, e, entry, gate, live, gain, gm, heads, tile=128):
    rows = o.shape[0]
    row = lambda width: pl.BlockSpec((tile, width), lambda i: (i, 0))
    return pl.pallas_call(
        functools.partial(unfinish_kernel, heads),
        grid=(rows // tile,),
        in_specs=[row(heads * DV), row(heads * DK), pl.BlockSpec((heads, DK, DV), lambda i: (0, 0, 0)), row(heads * DV),
                  row(1), pl.BlockSpec((1, DV), lambda i: (0, 0)), row(heads * DV)],
        out_specs=[row(heads * DV), row(heads * DV), pl.BlockSpec((1, DV), lambda i: (0, 0)),
                   pl.BlockSpec((heads, DK, DV), lambda i: (0, 0, 0))],
        out_shape=[jax.ShapeDtypeStruct((rows, heads * DV), BF), jax.ShapeDtypeStruct((rows, heads * DV), BF),
                   jax.ShapeDtypeStruct((1, DV), F32), jax.ShapeDtypeStruct((heads, DK, DV), F32)],
        compiler_params=pltpu.CompilerParams(vmem_limit_bytes=48 * 2**20),
    )(o, e, entry, gate, live, gain, gm)


def silu_back(c, grad):
    sig = jax.nn.sigmoid(c)
    return grad * (sig * (1.0 + c * (1.0 - sig)))


def backward_kernel(heads, flag_ref, x_ref, prev_ref, rim_ref, taps_ref, small_ref, live_ref, alog_ref, dt_ref, t_ref, z_ref,
                    go_ref, s_ref, exit_ref, gx_ref, gsmall_ref, gtaps_ref, gscalar_ref, carry, after_ref):
    step = pl.program_id(0)
    nb = pl.num_programs(0)
    at = nb - 1 - step
    rows = lax.broadcasted_iota(jnp.int32, (BLOCK, BLOCK), 0)
    cols = lax.broadcasted_iota(jnp.int32, (BLOCK, BLOCK), 1)
    last = lax.broadcasted_iota(jnp.int32, (BLOCK, 1), 0) == BLOCK - 1
    flag = flag_ref[at]
    taps_count = taps_ref.shape[0]

    @pl.when(step == 0)
    def _():
        carry[...] = exit_ref[...].astype(F32)
        after_ref[...] = jnp.zeros_like(after_ref)
        gtaps_ref[...] = jnp.zeros_like(gtaps_ref)
        gscalar_ref[...] = jnp.zeros_like(gscalar_ref)

    live = live_ref[...]
    speed, biased, log_decay, sig, betas, run, run_row = decay_tables(
        heads, small_ref[...], alog_ref[...], dt_ref[...], live, rows, cols)
    openings = flag * jnp.exp(run)
    closings = jnp.exp(run[BLOCK - 1:BLOCK] - run)
    row_block = pl.ds(pl.multiple_of(at * BLOCK, BLOCK), BLOCK)

    def inputs(columns):
        x = x_ref[:, columns].astype(F32)
        before = jnp.where(at == 0, rim_ref[8:16, columns].astype(F32), prev_ref[8:16, columns].astype(F32)) * flag
        return x, before, conv_rows(x, before, taps_ref[:, columns])

    def conv_back(columns, x, before, grad):
        taps = taps_ref[:, columns]
        later = after_ref[:, columns]
        longer = jnp.concatenate([grad, later], axis=0)
        gx = taps[taps_count - 1:taps_count] * grad
        sums = [jnp.sum(grad * x, axis=0, keepdims=True)]
        for back in range(1, taps_count):
            gx = gx + taps[taps_count - 1 - back:taps_count - back] * longer[back:back + BLOCK]
            sums.append(jnp.sum(grad * shifted(x, before, back), axis=0, keepdims=True))
        gx_ref[row_block, columns] = gx.astype(BF)
        gtaps_ref[:, columns] += jnp.concatenate(sums[::-1], axis=0)
        after_ref[:, columns] = grad[:8] * flag

    grad_runs, grad_betas = [], []
    for h in range(heads):
        qs, ks, vs = head_slices(heads, h)
        xq, bq, cq = inputs(qs)
        xk, bk, ck = inputs(ks)
        xv, bv, cv = inputs(vs)
        aq, ak = cq * jax.nn.sigmoid(cq), ck * jax.nn.sigmoid(ck)
        rq, rk_unit = unit_factor(aq), unit_factor(ak)
        uq, uk = aq * rq, ak * rk_unit
        q, k = (uq * DK ** (-0.5)).astype(BF), uk.astype(BF)
        v = (cv * jax.nn.sigmoid(cv)).astype(BF)
        qf, kf, vf = q.astype(F32), k.astype(F32), v.astype(F32)
        beta, opening, closing = betas[:, h:h + 1], openings[:, h:h + 1], closings[:, h:h + 1]
        gamma = opening[BLOCK - 1:BLOCK]
        table = block_tables(run[:, h:h + 1], run_row[h:h + 1, :], rows, cols)
        kk = mm_nt(k, k)
        scores = mm_nt(q, k) * table
        low_t = t_ref[0, h]
        u = mm(low_t, beta * vf)
        w = mm(low_t, (beta * opening) * kf)
        low_w = w.astype(BF)
        state = z_ref[0, h, :, :DV].astype(F32) + mm(z_ref[0, h, :, DV:], s_ref[h])
        low_s = state.astype(BF)
        c = u - mm(low_w, low_s)
        low_c = c.astype(BF)
        go = go_ref[:, h * DV:(h + 1) * DV]
        g = carry[h]
        low_g = g.astype(BF)
        low_ck = (closing * kf).astype(BF)
        low_oq = (opening * qf).astype(BF)
        dc = mm_tn(scores, go) + mm(low_ck, low_g)
        low_dc = dc.astype(BF)
        both = jnp.concatenate([go, low_dc], axis=0)
        carry[h] = gamma * g + mm_tn(jnp.concatenate([low_oq, -low_w], axis=0), both)
        dkeyed = mm_nt(low_c, low_g)
        dgamma = jnp.sum(jnp.sum(state * g, axis=1, keepdims=True), axis=0, keepdims=True)
        dscore = jnp.where(rows >= cols, mm_nt(go, low_c), 0.0)
        back = mm_nt(both, low_s)
        doq, dw = back[:BLOCK], -back[BLOCK:]
        drv = mm_tn(low_t, low_dc)
        drw = mm_tn(low_t, dw)
        low_drv, low_drw = drv.astype(BF), drw.astype(BF)
        da = jnp.where(rows > cols, -(mm_nt(low_drv, u) + mm_nt(low_drw, low_w)), 0.0)
        dat = da * table
        dkk = (beta * dat).astype(BF)
        dqk = (dscore * table).astype(BF)
        gq = (opening * doq + mm(dqk, k)) * DK ** (-0.5)
        gk = mm_tn(dqk, q) + mm(dkk, k) + mm_tn(dkk, k) + closing * dkeyed + (beta * opening) * drw
        gq = rq * (gq - uq * jnp.sum(gq * uq, axis=1, keepdims=True))
        gk = rk_unit * (gk - uk * jnp.sum(gk * uk, axis=1, keepdims=True))
        conv_back(qs, xq, bq, silu_back(cq, gq))
        conv_back(ks, xk, bk, silu_back(ck, gk))
        conv_back(vs, xv, bv, silu_back(cv, beta * drv))
        rk = jnp.sum(drw * kf, axis=1, keepdims=True)
        atk = dat * kk
        grad_betas.append(jnp.sum(drv * vf, axis=1, keepdims=True) + opening * rk + jnp.sum(atk, axis=1, keepdims=True))
        dopen = opening * (jnp.sum(doq * qf, axis=1, keepdims=True) + beta * rk)
        dclose = closing * jnp.sum(dkeyed * kf, axis=1, keepdims=True)
        e = dscore * scores + beta * atk
        by_col = exact_tn(e, jnp.ones((BLOCK, 8), F32))[:, :1]
        dg = jnp.sum(e, axis=1, keepdims=True) - by_col + dopen - dclose
        grad_runs.append(dg + jnp.where(last, jnp.sum(dclose, axis=0, keepdims=True) + dgamma * gamma, 0.0))

    lane = lax.broadcasted_iota(jnp.int32, (BLOCK, heads), 1)
    grad_run = sum(jnp.where(lane == h, grad_runs[h], 0.0) for h in range(heads))
    grad_beta = sum(jnp.where(lane == h, grad_betas[h], 0.0) for h in range(heads))
    grad_log = exact_tn(jnp.where(cols <= rows, 1.0, 0.0), grad_run)
    grad_biased = grad_log * speed * jax.nn.sigmoid(biased)
    gsmall_ref[:, :heads] = grad_biased
    gsmall_ref[:, heads:] = grad_beta * live * sig * (1.0 - sig)
    gscalar_ref[0:1, :] += jnp.sum(grad_log * log_decay, axis=0, keepdims=True)
    gscalar_ref[1:2, :] += jnp.sum(grad_biased, axis=0, keepdims=True)

    @pl.when(step == nb - 1)
    def _():
        longer = jnp.concatenate([jnp.zeros((16, taps_ref.shape[1]), F32), after_ref[...]], axis=0)
        gx = jnp.zeros((16, taps_ref.shape[1]), F32)
        for back in range(1, taps_count):
            gx = gx + taps_ref[taps_count - 1 - back:taps_count - back, :] * longer[back:back + 16]
        gx_ref[pl.ds(nb * BLOCK, 16), :] = gx.astype(BF)


MESH = pl.DeviceIdType.MESH


def line_position():
    w = lax.axis_index("wide")
    return w, w // 2, w % 2, lax.axis_index("narrow")


def greet_line(places, w, place, side, n):
    barrier = pltpu.get_barrier_semaphore()
    pl.semaphore_signal(barrier, inc=1, device_id=(w + 1 - 2 * side, n), device_id_type=MESH)

    @pl.when(place > 0)
    def _():
        pl.semaphore_signal(barrier, inc=1, device_id=(w - 2, n), device_id_type=MESH)

    @pl.when(place < places - 1)
    def _():
        pl.semaphore_signal(barrier, inc=1, device_id=(w + 2, n), device_id_type=MESH)

    pl.semaphore_wait(barrier, 1 + jnp.where(place > 0, 1, 0) + jnp.where(place < places - 1, 1, 0))


def row_cuts(rows, chunks):
    units = rows // 16
    chunks = min(chunks, units)
    edges = [16 * (units * c // chunks) for c in range(chunks + 1)]
    return [(edges[c], edges[c + 1] - edges[c], chunks >= 5 and c == 0) for c in range(chunks)]


class LineGather:
    def __init__(self, places, cuts, sources, targets, local_sems, send_sems, recv_sems):
        self.places, self.sources, self.targets = places, sources, targets
        self.local_sems, self.send_sems, self.recv_sems = local_sems, send_sems, recv_sems
        self.w, self.place, self.side, self.n = line_position()
        self.items = [(i,) + cut for i, found in enumerate(cuts) for cut in found]

    def copy(self, item, slot, way, own=False):
        number, (i, start, size, _) = item, self.items[item]
        rows = pl.ds(start, size)
        source = self.sources[i].at[rows] if own else self.targets[i].at[slot, rows]
        device = [self.w + 1 - 2 * self.side, self.w + 2, self.w - 2][way]
        return pltpu.make_async_remote_copy(
            src_ref=source, dst_ref=self.targets[i].at[slot, rows], send_sem=self.send_sems.at[way, slot, number],
            recv_sem=self.recv_sems.at[slot, number], device_id=(device, self.n), device_id_type=MESH)

    def start(self):
        for i, source in enumerate(self.sources):
            pltpu.make_async_copy(source, self.targets[i].at[self.w], self.local_sems.at[i]).start()
        for item in range(len(self.items)):
            self.copy(item, self.w, 0, True).start()
            self.along(item, self.w, 1, True)
            self.along(item, self.w, 2, True)

    def along(self, item, slot, way, own=False):
        @pl.when(self.place < self.places - 1 if way == 1 else self.place > 0)
        def _():
            self.copy(item, slot, way, own).start()

    def events(self):
        found = []
        for item in range(len(self.items)):
            if self.items[item][3]:
                found.append((item, 0, -1))
        for t in range(1, self.places):
            for item in range(len(self.items)):
                found += [(item, t, s) for s in ((0, 1) if self.items[item][3] else (0,))]
        return found

    def run(self, event):
        item, t, s = event
        if s < 0:
            slot = self.w + 1 - 2 * self.side
            self.copy(item, slot, 0).wait_recv()
            self.along(item, slot, 1)
            self.along(item, slot, 2)
            return

        for way, there in ((1, self.place - t), (2, self.place + t)):
            slot = 2 * there + (self.side if s == 0 else 1 - self.side)

            @pl.when((there >= 0) & (there < self.places))
            def _():
                self.copy(item, slot, way).wait_recv()
                self.along(item, slot, way)
                if not self.items[item][3]:
                    self.copy(item, slot, 0).start()

    def finish(self):
        for item in range(len(self.items)):
            if not self.items[item][3]:
                for t in range(self.places):
                    self.copy(item, 2 * t + 1 - self.side, 0).wait_recv()
        for i, source in enumerate(self.sources):
            pltpu.make_async_copy(source, self.targets[i].at[self.w], self.local_sems.at[i]).wait()
        for item in range(len(self.items)):
            both = self.items[item][3]
            for t in range(self.places):
                slot = 2 * t + self.side
                if both:
                    @pl.when(t == self.place)
                    def _():
                        self.copy(item, slot, 0).wait_send()
                else:
                    self.copy(item, slot, 0).wait_send()
                for s in ((0, 1) if both else (0,)):
                    slot = 2 * t + (self.side if s == 0 else 1 - self.side)

                    @pl.when((self.place < self.places - 1) & (t <= self.place))
                    def _():
                        self.copy(item, slot, 1).wait_send()

                    @pl.when((self.place > 0) & (t >= self.place))
                    def _():
                        self.copy(item, slot, 2).wait_send()

    @staticmethod
    def scratch(count, cuts):
        items = sum(len(found) for found in cuts)
        return [pltpu.SemaphoreType.DMA((len(cuts),)), pltpu.SemaphoreType.DMA((3, count, items)),
                pltpu.SemaphoreType.DMA((count, items))]


def gather_kernel(places, cuts, *refs):
    amount = len(cuts)
    gather = LineGather(places, cuts, refs[:amount], refs[amount:2 * amount], *refs[2 * amount:])
    greet_line(places, gather.w, gather.place, gather.side, gather.n)
    gather.start()
    for event in gather.events():
        gather.run(event)
    gather.finish()


def line_gather(values, call_id, chunks=6):
    count = lax.axis_size("wide")
    cuts = [row_cuts(value.shape[0], chunks if value.shape[0] > 64 else 1) for value in values]
    hbm = pl.BlockSpec(memory_space=pl.ANY)
    gathered = pl.pallas_call(
        functools.partial(gather_kernel, count // 2, cuts),
        out_shape=[jax.ShapeDtypeStruct((count,) + value.shape, value.dtype) for value in values],
        in_specs=[hbm] * len(values),
        out_specs=[hbm] * len(values),
        scratch_shapes=LineGather.scratch(count, cuts),
        compiler_params=pltpu.CompilerParams(collective_id=call_id, has_side_effects=True),
    )(*values)
    return [g.reshape((count * g.shape[1],) + g.shape[2:]) for g in gathered]


class LineScatter:
    def __init__(self, places, cuts, sources, owns, pairs, lines, load_sems, pair_send, pair_recv, right_send,
                 right_recv, left_send, left_recv):
        self.places, self.sources, self.owns, self.pairs, self.lines = places, sources, owns, pairs, lines
        self.load_sems, self.pair_sems = load_sems, (pair_send, pair_recv)
        self.right_sems, self.left_sems = (right_send, right_recv), (left_send, left_recv)
        self.w, self.place, self.side, self.n = line_position()
        self.items = [(i,) + cut[:2] for i, found in enumerate(cuts) for cut in found]
        self.order = [t for j in range(places // 2) for t in (places - 1 - j, j)]

    def remote(self, source, target, sems, t, item, device):
        return pltpu.make_async_remote_copy(src_ref=source, dst_ref=target, send_sem=sems[0].at[t, item],
                                            recv_sem=sems[1].at[t, item], device_id=(device, self.n), device_id_type=MESH)

    def at(self, t, item):
        i, start, size = self.items[item]
        return t, pl.ds(start, size)

    def across(self, t, item):
        i = self.items[item][0]
        source = self.sources[i].at[2 * t + 1 - self.side, self.at(t, item)[1]]
        return self.remote(source, self.pairs[i].at[self.at(t, item)], self.pair_sems, t, item, self.w + 1 - 2 * self.side)

    def load(self, t, item):
        i = self.items[item][0]
        return pltpu.make_async_copy(self.sources[i].at[2 * t + self.side, self.at(t, item)[1]],
                                     self.owns[i].at[self.at(t, item)], self.load_sems.at[t, item])

    def right(self, t, item):
        i, at = self.items[item][0], self.at(t, item)
        return self.remote(self.owns[i].at[at], self.lines[i].at[at], self.right_sems, t, item, self.w + 2)

    def left(self, t, item, arriving=False):
        i, at = self.items[item][0], self.at(t, item)
        slot = jnp.where(t == self.place - (0 if arriving else 1), self.places, t)
        return self.remote(self.owns[i].at[at], self.lines[i].at[slot, at[1]], self.left_sems, t, item, self.w - 2)

    def start(self):
        for t in self.order:
            for item in range(len(self.items)):
                self.across(t, item).start()
                self.load(t, item).start()

    def events(self):
        return [(t, item) for t in self.order for item in range(len(self.items))]

    def run(self, event):
        t, item = event
        i, at = self.items[item][0], self.at(t, item)
        own, place, places = self.owns[i], self.place, self.places

        def add(other):
            own[at] = (own[at].astype(F32) + other[at].astype(F32)).astype(own.dtype)

        self.load(t, item).wait()
        self.across(t, item).wait_recv()
        add(self.pairs[i])

        @pl.when(t > place)
        def _():
            @pl.when(place > 0)
            def _():
                self.right(t, item).wait_recv()
                add(self.lines[i])

            self.right(t, item).start()

        @pl.when(t < place)
        def _():
            @pl.when(place < places - 1)
            def _():
                self.left(t, item, True).wait_recv()
                add(self.lines[i])

            self.left(t, item).start()

    def finish(self, outs):
        place = self.place
        for item in range(len(self.items)):
            i, at = self.items[item][0], self.at(place, item)
            out, own = outs[i], self.owns[i]
            out[at[1]] = own[at].astype(F32)

            @pl.when(place > 0)
            def _():
                self.right(place, item).wait_recv()
                out[at[1]] = out[at[1]] + self.lines[i][at].astype(F32)

            @pl.when(place < self.places - 1)
            def _():
                self.left(place, item, True).wait_recv()
                out[at[1]] = out[at[1]] + self.lines[i][self.places, at[1]].astype(F32)
        for t in range(self.places):
            for item in range(len(self.items)):
                self.across(t, item).wait_send()

                @pl.when(t > place)
                def _():
                    self.right(t, item).wait_send()

                @pl.when(t < place)
                def _():
                    self.left(t, item).wait_send()

    @staticmethod
    def scratch(places, cuts, values):
        buffers = [pltpu.VMEM((places,) + value.shape[1:], value.dtype) for value in values]
        lines = [pltpu.VMEM((places + 1,) + value.shape[1:], value.dtype) for value in values]
        items = sum(len(found) for found in cuts)
        return buffers * 2 + lines + [pltpu.SemaphoreType.DMA((places, items))] * 7


def scatter_kernel(places, cuts, *refs):
    m = len(cuts)
    sources, outs, owns, pairs, lines = [refs[m * g:m * (g + 1)] for g in range(5)]
    scatter = LineScatter(places, cuts, sources, owns, pairs, lines, *refs[5 * m:])
    greet_line(places, scatter.w, scatter.place, scatter.side, scatter.n)
    scatter.start()
    for event in scatter.events():
        scatter.run(event)
    scatter.finish(outs)


def line_scatter(values, call_id, chunks=4):
    count = values[0].shape[0]
    cuts = [row_cuts(value.shape[1], chunks if value.shape[1] > 64 else 1) for value in values]
    return pl.pallas_call(
        functools.partial(scatter_kernel, count // 2, cuts),
        out_shape=[jax.ShapeDtypeStruct(value.shape[1:], F32) for value in values],
        in_specs=[pl.BlockSpec(memory_space=pl.ANY)] * len(values),
        out_specs=[pl.BlockSpec(memory_space=pltpu.VMEM)] * len(values),
        scratch_shapes=LineScatter.scratch(count // 2, cuts, values),
        compiler_params=pltpu.CompilerParams(collective_id=call_id, has_side_effects=True, vmem_limit_bytes=56 * 2**20),
    )(*values)


def forward_gather_kernel(heads, nb, places, cuts, *refs):
    m = len(cuts)
    inputs, sources, refs = refs[:8], refs[8:8 + m], refs[8 + m:]
    outs, targets, refs = refs[:5], refs[5:5 + m], refs[5 + m:]
    gather = LineGather(places, cuts, sources, targets, *refs[2:])
    step = pl.program_id(0)

    @pl.when(step == 0)
    def _():
        greet_line(places, gather.w, gather.place, gather.side, gather.n)
        gather.start()

    forward_kernel(heads, *inputs, *outs, *refs[:2])
    events = gather.events()
    for i in range(nb):
        @pl.when(step == i)
        def _():
            for event in events[len(events) * i // nb:len(events) * (i + 1) // nb]:
                gather.run(event)

    @pl.when(step == nb - 1)
    def _():
        gather.finish()


def forward_gather(flags, mixed, taps, small, live, a_log, dt_bias, heads, blocks, call_id, chunks=2):
    rows, width = live.shape[0], mixed.shape[1]
    nb = rows // BLOCK
    count = lax.axis_size("wide")
    cuts = [row_cuts(block.shape[0], chunks) for block in blocks]
    row = lambda width: pl.BlockSpec((BLOCK, width), lambda i: (i, 0))
    same = lambda *shape: pl.BlockSpec(shape, lambda i: (0,) * len(shape))
    hbm = pl.BlockSpec(memory_space=pl.ANY)
    found = pl.pallas_call(
        functools.partial(forward_gather_kernel, heads, nb, count // 2, cuts),
        grid=(nb,),
        in_specs=[pl.BlockSpec(memory_space=pltpu.SMEM), row(width), pl.BlockSpec((16, width), lambda i: (rows // 16, 0)),
                  same(*taps.shape), row(small.shape[1]), row(1), same(1, heads), same(1, heads)]
                 + [hbm] * len(blocks),
        out_specs=[row(heads * DV), row(heads * DK),
                   pl.BlockSpec((1, heads, BLOCK, BLOCK), lambda i: (i, 0, 0, 0)),
                   pl.BlockSpec((1, heads, DK, DV + DK), lambda i: (i, 0, 0, 0)),
                   same(heads, DK, DV + DK)] + [hbm] * len(blocks),
        out_shape=[jax.ShapeDtypeStruct((rows, heads * DV), F32), jax.ShapeDtypeStruct((rows, heads * DK), BF),
                   jax.ShapeDtypeStruct((nb, heads, BLOCK, BLOCK), BF),
                   jax.ShapeDtypeStruct((nb, heads, DK, DV + DK), BF),
                   jax.ShapeDtypeStruct((heads, DK, DV + DK), F32)]
                  + [jax.ShapeDtypeStruct((count,) + block.shape, block.dtype) for block in blocks],
        scratch_shapes=[pltpu.VMEM((heads, DK, DV + DK), F32), pltpu.VMEM((8, width), F32)]
                       + LineGather.scratch(count, cuts),
        compiler_params=pltpu.CompilerParams(collective_id=call_id, has_side_effects=True, vmem_limit_bytes=48 * 2**20),
    )(flags, mixed, mixed, taps, small, live, a_log, dt_bias, *blocks)
    return found[:5], [g.reshape((count * g.shape[1],) + g.shape[2:]) for g in found[5:]]


def backward_scatter_kernel(heads, nb, places, cuts, *refs):
    m = len(cuts)
    inputs, sources, refs = refs[:14], refs[14:14 + m], refs[14 + m:]
    outs, sums, refs = refs[:4], refs[4:4 + m], refs[4 + m:]
    scratch, refs = refs[:2], refs[2:]
    owns, pairs, lines = (refs[m * g:m * (g + 1)] for g in range(3))
    scatter = LineScatter(places, cuts, sources, owns, pairs, lines, *refs[3 * m:])
    step = pl.program_id(0)

    @pl.when(step == 0)
    def _():
        greet_line(places, scatter.w, scatter.place, scatter.side, scatter.n)
        scatter.start()

    backward_kernel(heads, *inputs, *outs, *scratch)
    events = scatter.events()
    for i in range(nb):
        @pl.when(step == i)
        def _():
            for event in events[len(events) * i // nb:len(events) * (i + 1) // nb]:
                scatter.run(event)

    @pl.when(step == nb - 1)
    def _():
        scatter.finish(sums)


def backward_scatter(flags, mixed, taps, small, live, a_log, dt_bias, t, z, go, entry, leaving, heads, terms, call_id,
                     chunks=2):
    rows, width = live.shape[0], mixed.shape[1]
    nb = rows // BLOCK
    count = terms[0].shape[0]
    cuts = [row_cuts(term.shape[1], chunks) for term in terms]
    row = lambda width: pl.BlockSpec((BLOCK, width), lambda i: (nb - 1 - i, 0))
    same = lambda *shape: pl.BlockSpec(shape, lambda i: (0,) * len(shape))
    prev = pl.BlockSpec((16, width), lambda i: (jnp.maximum((nb - 1 - i) * (BLOCK // 16) - 1, 0), 0))
    found = pl.pallas_call(
        functools.partial(backward_scatter_kernel, heads, nb, count // 2, cuts),
        grid=(nb,),
        in_specs=[pl.BlockSpec(memory_space=pltpu.SMEM), row(width), prev,
                  pl.BlockSpec((16, width), lambda i: (rows // 16, 0)), same(*taps.shape), row(small.shape[1]), row(1),
                  same(1, heads), same(1, heads),
                  pl.BlockSpec((1, heads, BLOCK, BLOCK), lambda i: (nb - 1 - i, 0, 0, 0)),
                  pl.BlockSpec((1, heads, DK, DV + DK), lambda i: (nb - 1 - i, 0, 0, 0)),
                  row(heads * DV), same(heads, DK, DV), same(heads, DK, DV)]
                 + [pl.BlockSpec(memory_space=pl.ANY)] * len(terms),
        out_specs=[same(rows + 16, width), row(2 * heads), same(*taps.shape), same(8, heads)]
                  + [same(*term.shape[1:]) for term in terms],
        out_shape=[jax.ShapeDtypeStruct((rows + 16, width), BF), jax.ShapeDtypeStruct((rows, 2 * heads), F32),
                   jax.ShapeDtypeStruct(taps.shape, F32), jax.ShapeDtypeStruct((8, heads), F32)]
                  + [jax.ShapeDtypeStruct(term.shape[1:], F32) for term in terms],
        scratch_shapes=[pltpu.VMEM((heads, DK, DV), F32), pltpu.VMEM((8, width), F32)]
                       + LineScatter.scratch(count // 2, cuts, terms),
        compiler_params=pltpu.CompilerParams(collective_id=call_id, has_side_effects=True, vmem_limit_bytes=58 * 2**20),
    )(flags, mixed, mixed, mixed, taps, small, live, a_log, dt_bias, t, z, go, entry, leaving, *terms)
    return found[:4], found[4:]


def greet_places(places, w, place, side, n):
    barrier = pltpu.get_barrier_semaphore()
    pl.semaphore_signal(barrier, inc=1, device_id=(w + 1 - 2 * side, n), device_id_type=MESH)
    for k in range(1, places):
        @pl.when(place + k < places)
        def _():
            pl.semaphore_signal(barrier, inc=1, device_id=(w + 2 * k, n), device_id_type=MESH)

        @pl.when(place - k >= 0)
        def _():
            pl.semaphore_signal(barrier, inc=1, device_id=(w - 2 * k, n), device_id_type=MESH)

    pl.semaphore_wait(barrier, places)


def pass_kernel(places, heads, forward, *refs):
    if forward:
        end_ref, entry_ref, their_map_ref, joined_map_ref = refs[:4]
        refs = refs[4:]
    else:
        direct_ref, my_map_ref, their_map_ref, joined_map_ref, entry_ref = refs[:5]
        refs = refs[5:]
    mine, theirs, joined, turned, total, states, near_send, near_recv, far_send, far_recv = refs
    w, place, side, n = line_position()
    half = heads // 2
    partner = w + 1 - 2 * side
    my_half, other_half = pl.ds(side * half, half), pl.ds((1 - side) * half, half)
    mine[...] = (end_ref if forward else direct_ref)[...].astype(BF)
    greet_places(places, w, place, side, n)

    def near(source, target, part, which):
        return pltpu.make_async_remote_copy(
            src_ref=source.at[part], dst_ref=target.at[part], send_sem=near_send.at[which], recv_sem=near_recv.at[which],
            device_id=(partner, n), device_id_type=MESH)

    def far(k, step):
        return pltpu.make_async_remote_copy(
            src_ref=joined, dst_ref=turned.at[k], send_sem=far_send.at[k], recv_sem=far_recv.at[k],
            device_id=(w + 2 * step, n), device_id_type=MESH)

    ahead = 1 if forward else -1
    near(mine, theirs, other_half, 0).start()
    near(mine, theirs, my_half, 1).start()
    near(mine, theirs, my_half, 0).wait_recv()
    for i in range(half):
        own, other = mine[side * half + i], theirs[side * half + i]
        early, late = jnp.where(side == 0, own, other), jnp.where(side == 0, other, own)
        if forward:
            both = mm(late[:, DV:], early)
            joined[i, :, :DV] = (both[:, :DV] + late[:, :DV].astype(F32)).astype(BF)
            joined[i, :, DV:] = both[:, DV:].astype(BF)
            joined_map_ref[i] = both[:, DV:].astype(BF)
        else:
            early_map = jnp.where(side == 0, my_map_ref[side * half + i], their_map_ref[side * half + i])
            joined[i, :, :DV] = (mm_tn(early_map, late) + early.astype(F32)).astype(BF)
            joined[i, :, DV:] = joined_map_ref[i]
    for k in range(1, places):
        @pl.when((place + ahead * k >= 0) & (place + ahead * k < places))
        def _():
            far(k, ahead * k).start()

    total[...] = jnp.zeros_like(total)
    for k in range(places - 1, 0, -1):
        @pl.when((place - ahead * k >= 0) & (place - ahead * k < places))
        def _():
            far(k, ahead * k).wait_recv()
            for i in range(half):
                apply = mm if forward else mm_tn
                total[i] = apply(turned[k, i, :, DV:], total[i]) + turned[k, i, :, :DV].astype(F32)

    states[my_half] = total[...].astype(BF)
    near(states, states, my_half, 2).start()
    near(mine, theirs, other_half, 1).wait_recv()
    near(states, states, other_half, 2).wait_recv()
    through = 1 if forward else 0
    for h in range(heads):
        if forward:
            their_map_ref[h] = theirs[h, :, DV:]
        state = states[h]
        if forward:
            passed = mm(theirs[h, :, DV:], state) + theirs[h, :, :DV].astype(F32)
        else:
            passed = mm_tn(their_map_ref[h], state) + theirs[h].astype(F32)
        entry_ref[h] = jnp.where(side == through, passed, state.astype(F32)).astype(BF)
    near(mine, theirs, other_half, 0).wait_send()
    near(mine, theirs, my_half, 1).wait_send()
    near(states, states, my_half, 2).wait_send()
    for k in range(1, places):
        @pl.when((place + ahead * k >= 0) & (place + ahead * k < places))
        def _():
            far(k, ahead * k).wait_send()


def pass_states(operands, heads, forward, call_id):
    places = lax.axis_size("wide") // 2
    half = heads // 2
    width = DV + DK if forward else DV
    vmem = pl.BlockSpec(memory_space=pltpu.VMEM)
    out_shape = [jax.ShapeDtypeStruct((heads, DK, DV), BF)]
    if forward:
        out_shape += [jax.ShapeDtypeStruct((heads, DK, DK), BF), jax.ShapeDtypeStruct((half, DK, DK), BF)]
    return pl.pallas_call(
        functools.partial(pass_kernel, places, heads, forward),
        in_specs=[vmem] * len(operands),
        out_specs=[vmem] * len(out_shape),
        out_shape=out_shape,
        scratch_shapes=[pltpu.VMEM((heads, DK, width), BF), pltpu.VMEM((heads, DK, width), BF),
                        pltpu.VMEM((half, DK, DV + DK), BF), pltpu.VMEM((places, half, DK, DV + DK), BF),
                        pltpu.VMEM((half, DK, DV), F32), pltpu.VMEM((heads, DK, DV), BF),
                        pltpu.SemaphoreType.DMA((3,)), pltpu.SemaphoreType.DMA((3,)),
                        pltpu.SemaphoreType.DMA((places,)), pltpu.SemaphoreType.DMA((places,))],
        compiler_params=pltpu.CompilerParams(collective_id=call_id, has_side_effects=True, vmem_limit_bytes=32 * 2**20),
    )(*operands)


CONV = 4


def rms_norm(value, gain):
    return value * lax.rsqrt(jnp.mean(value * value, axis=-1, keepdims=True) + EPS) * gain


def after(value, *others):
    return lax.optimization_barrier((value,) + others)[0]


def from_behind(value, axis, steps):
    count = lax.axis_size(axis)
    initial, last = (max(0, -steps), min(count, count - steps))
    return lax.ppermute(value, axis, [(source, source + steps) for source in range(initial, last)])


def turn(value, k):
    count = lax.axis_size("wide")
    if k % (count // 2) == 0:
        return value
    return lax.ppermute(value, "wide", [(w, (w + 2 * k) % count) for w in range(count)])


def across(value, axis, bit):
    return lax.ppermute(value, axis, [(i, i ^ bit) for i in range(lax.axis_size(axis))])


def turn_gather(value):
    places = lax.axis_size("wide") // 2
    own = [turn(value, k) for k in range(places)]
    return assemble([piece for part in own for piece in (part, across(part, "wide", 1))])


def turn_scatter(value):
    places = value.shape[0] // 2
    me = lax.axis_index("wide")
    place, side = me // 2, me % 2
    paired = value.reshape((places, 2) + value.shape[1:])
    theirs = across(lax.dynamic_index_in_dim(paired, 1 - side, 1, keepdims=False), "wide", 1)
    total = None
    for k in list(range(1, places)) + [0]:
        at = (place + k) % places
        block = lax.dynamic_slice(paired, (at, side, 0, 0), (1, 1) + value.shape[1:])[0, 0].astype(F32)
        block = block + lax.dynamic_index_in_dim(theirs, at, 0, keepdims=False).astype(F32)
        if k:
            block = turn(block.astype(BF), k).astype(F32)
        total = block if total is None else total + block
    return total


def gather_narrow(value):
    near = across(value, "narrow", 1)
    return [value, near, across(value, "narrow", 2), across(near, "narrow", 2)]


def scatter_narrow(parts):
    first = parts[0].astype(F32) + across(parts[1], "narrow", 1).astype(F32)
    second = (parts[2].astype(F32) + across(parts[3], "narrow", 1).astype(F32)).astype(parts[2].dtype)
    return first + across(second, "narrow", 2).astype(F32)


def blocks_of(value, axis, count):
    me = lax.axis_index("narrow")
    size = value.shape[axis] // count
    return [lax.dynamic_slice_in_dim(value, (me ^ j) * size, size, axis) for j in range(count)]


def placed(pieces, axis):
    me = lax.axis_index("narrow")
    size = pieces[0].shape[axis]
    shape = list(pieces[0].shape)
    shape[axis] = size * len(pieces)
    whole = jnp.zeros(shape, pieces[0].dtype)
    for j, piece in enumerate(pieces):
        whole = lax.dynamic_update_slice_in_dim(whole, piece, (me ^ j) * size, axis)
    return whole


def sum_all(value, axis):
    bit = 1
    while bit < lax.axis_size(axis):
        value = value + across(value, axis, bit)
        bit *= 2
    return value


def sequence_tables(doc_lengths, first_row, row_count, block_size):
    padded = (doc_lengths + block_size - 1) // block_size * block_size
    seq_ends = jnp.cumsum(padded)
    seq_starts = seq_ends - padded
    row_places = first_row + jnp.arange(row_count, dtype=jnp.int32)
    inside_mask = (row_places[:, None] >= seq_starts[None, :]) & (row_places[:, None] < seq_ends[None, :])
    live_mask = jnp.any(inside_mask & (row_places[:, None] < (seq_starts + doc_lengths)[None, :]), axis=1, keepdims=True)
    fresh_block = jnp.any(row_places[::block_size][:, None] == seq_starts[None, :], axis=1)
    return live_mask.astype(F32), jnp.where(fresh_block, 0.0, 1.0).astype(F32)


def contract_rows(left, right):
    return lax.dot_general(left, right, (((0,), (0,)), ((), ())), preferred_element_type=F32)


def contract_cols(left, right):
    return lax.dot_general(left, right, (((1,), (1,)), ((), ())), preferred_element_type=F32)


def shards(block_input, gain_attn, w_query, w_key, w_value, w_gate_out, w_decay, w_beta, conv_query, conv_key,
           conv_value, a_log, dt_bias, out_gain, w_out, gain_mlp, w_gate, w_up, w_down, doc_lengths, cotangent):
    row_count, d_model = block_input.shape
    quarter = cotangent.shape[0]
    depth = w_query.shape[0]
    heads = a_log.shape[0]
    narrow = lax.axis_size("narrow")
    wide = lax.axis_size("wide")
    wide_index = lax.axis_index("wide")
    live, flags = sequence_tables(doc_lengths, wide_index * row_count, row_count, BLOCK)
    gain_row, a_row, dt_row = out_gain[None, :], a_log[None, :], dt_bias[None, :]
    key_width, value_width = heads * DK, heads * DV
    columns = 2 * key_width + value_width
    depth_blocks = lambda a: a.astype(BF).reshape(wide, depth, a.shape[1])
    row_blocks = lambda a: a.astype(BF).reshape(wide, quarter, a.shape[1])

    padded = lambda a: jnp.pad(a, ((0, 16 - 2 * heads), (0, 0)))
    small_shard = padded(jnp.concatenate([w_decay.T, w_beta.T], axis=0))
    rim_input = from_behind(block_input[row_count - 16:], "wide", 1)
    input_rows = jnp.concatenate([block_input, rim_input], axis=0).astype(F32)
    normed_low = rms_norm(input_rows, gain_attn).astype(BF)
    first, small_weight = line_gather([jnp.concatenate([w_query, w_key, w_value], axis=1), small_shard], 1)
    small_weight = small_weight.reshape(wide, 16, depth)[:, :2 * heads].transpose(1, 0, 2).reshape(2 * heads, d_model)
    taps = jnp.concatenate([conv_query, conv_key, conv_value], axis=1)
    mixed = jnp.dot(normed_low, first, preferred_element_type=F32).astype(BF)
    small = contract_cols(normed_low[:row_count], small_weight)

    (local_out, reach, inverses, states, end), (gate_weight, out_weight) = forward_gather(
        flags, mixed, taps, small, live, a_row, dt_row, heads, [w_gate_out, w_out], 7)
    entry, their_map, joined_map = pass_states((end,), heads, True, 2)
    gate_rows = jnp.dot(normed_low[:row_count], gate_weight, preferred_element_type=F32)
    mixer_low = finish(local_out, reach, entry, gate_rows, live, gain_row, heads)
    gathered_cot = lax.all_gather(after(cotangent, entry), "wide", axis=0, tiled=True)
    head_part = contract_cols(mixer_low, out_weight)
    own_rows = scatter_narrow(blocks_of(head_part, 0, narrow)) + lax.dynamic_slice_in_dim(
        block_input, lax.axis_index("narrow") * quarter, quarter, 0).astype(F32)
    mlp_normed, mlp_norm_back = jax.vjp(rms_norm, own_rows, gain_mlp)
    gathered_rows = line_gather([mlp_normed.astype(BF)], 3)[0]
    gate_pre = jnp.dot(gathered_rows, w_gate, preferred_element_type=F32)
    up_pre = jnp.dot(gathered_rows, w_up, preferred_element_type=F32)
    gate_sig = jax.nn.sigmoid(gate_pre)
    gate_act = gate_pre * gate_sig
    hidden_low = (gate_act * up_pre).astype(BF)
    grad_hidden = contract_cols(gathered_cot, w_down)
    grad_gate_low = (grad_hidden * up_pre * gate_sig * (1.0 + gate_pre * (1.0 - gate_sig))).astype(BF)
    grad_up_low = (grad_hidden * gate_act).astype(BF)
    grad_rows = contract_cols(grad_gate_low, w_gate) + contract_cols(grad_up_low, w_up)
    grad_mlp_normed = line_scatter([row_blocks(grad_rows)], 4)[0]
    grad_own_norm, grad_gain_mlp = mlp_norm_back(grad_mlp_normed)
    grad_own = cotangent.astype(F32) + grad_own_norm
    grad_attn = placed(gather_narrow(grad_own.astype(BF)), 0)

    hidden_late, cot_late, rows_late = after((hidden_low, gathered_cot, gathered_rows), grad_mlp_normed)
    down_rows = jnp.dot(hidden_late, w_down, preferred_element_type=F32)
    grad_w_down = contract_rows(hidden_late, cot_late).astype(BF)
    grad_w_gate = contract_rows(rows_late, grad_gate_low).astype(BF)
    grad_w_up = contract_rows(rows_late, grad_up_low).astype(BF)
    grad_w_down, grad_w_gate, grad_w_up = after((grad_w_down, grad_w_gate, grad_w_up), grad_attn)
    share_gate = scatter_narrow(blocks_of(grad_w_gate, 0, narrow))
    share_up = scatter_narrow(blocks_of(grad_w_up, 0, narrow))
    share_down = scatter_narrow(blocks_of(grad_w_down, 1, narrow))

    grad_mixer = jnp.dot(grad_attn, out_weight, preferred_element_type=F32)
    grad_outputs, grad_gate_rows, grad_out_gain, direct = unfinish(local_out, reach, entry, gate_rows, live, gain_row,
                                                                   grad_mixer, heads)
    leaving = pass_states((direct, end[:, :, DV:].astype(BF), their_map, joined_map), heads, False, 5)[0]
    leaving = after(leaving, share_gate, share_up, share_down)
    terms = [depth_blocks(contract_rows(grad_attn, mixer_low)),
             depth_blocks(contract_rows(normed_low[:row_count], grad_gate_rows)), row_blocks(down_rows)]
    (grad_mixed, grad_small, grad_taps, grad_scalars), (sum_w_out, sum_w_gate_out, sum_down) = backward_scatter(
        flags, mixed, taps, small, live, a_row, dt_row, inverses, states, grad_outputs, entry, leaving, heads, terms, 8)
    output = (own_rows + sum_down).astype(BF)
    grad_small = grad_small.astype(BF)
    grad_first = contract_rows(normed_low, grad_mixed)
    grad_small_weight = contract_rows(grad_small, normed_low[:row_count]).astype(BF)
    small_blocks = padded(grad_small_weight).reshape(16, wide, depth).transpose(1, 0, 2)
    grad_normed = contract_cols(grad_mixed, first)
    grad_next = from_behind(grad_normed[row_count:], "wide", -1)
    grad_normed = (grad_normed[:row_count] + contract_cols(grad_gate_rows, gate_weight)
                   + jnp.dot(grad_small, small_weight, preferred_element_type=F32))
    grad_normed = grad_normed.at[row_count - 16:].add(grad_next)
    _, attn_norm_back = jax.vjp(rms_norm, block_input.astype(F32), gain_attn)
    grad_input_part, grad_gain_attn = attn_norm_back(grad_normed)
    grad_input = scatter_narrow(blocks_of(grad_input_part.astype(BF), 0, narrow)) + grad_own

    head_sums = jnp.concatenate([grad_taps.reshape(-1), grad_scalars[0], grad_scalars[1]])
    whole_sums = jnp.concatenate([grad_gain_attn, grad_gain_mlp, grad_out_gain[0]])
    sums = sum_all(jnp.concatenate([head_sums, whole_sums]), "wide")
    whole_sums = sum_all(sums[head_sums.shape[0]:], "narrow")
    every = placed([p[None] for p in gather_narrow(sums[:head_sums.shape[0]])], 0)
    conv_all = every[:, :CONV * columns].reshape(narrow, CONV, columns).transpose(1, 0, 2)
    conv_parts = [conv_all[:, :, lo:hi].reshape(CONV, -1) for lo, hi in
                  ((0, key_width), (key_width, 2 * key_width), (2 * key_width, columns))]
    sum_first, sum_small = line_scatter([depth_blocks(grad_first), small_blocks], 6)
    return (
        output, grad_input, whole_sums[:d_model],
        sum_first[:, :key_width], sum_first[:, key_width:2 * key_width], sum_first[:, 2 * key_width:], sum_w_gate_out,
        sum_small[:heads].T, sum_small[heads:2 * heads].T, conv_parts[0], conv_parts[1], conv_parts[2],
        every[:, CONV * columns:CONV * columns + heads].reshape(-1), every[:, CONV * columns + heads:].reshape(-1),
        whole_sums[2 * d_model:], sum_w_out, whole_sums[d_model:2 * d_model], share_gate, share_up, share_down,
    )


def solution(mesh):
    both = P("wide", "narrow")
    rows = P(("wide", "narrow"), None)
    return jax.shard_map(
        shards,
        mesh=mesh,
        in_specs=(P("wide", None), P(), both, both, both, both, both, both, P(None, "narrow"), P(None, "narrow"),
                  P(None, "narrow"), P("narrow"), P("narrow"), P(), both, P(), P(None, "wide"), P(None, "wide"),
                  P("wide", None), P(), rows),
        out_specs=(rows, rows, P(), both, both, both, both, both, both, P(), P(), P(), P(), P(), P(), both, P(),
                   P("narrow", "wide"), P("narrow", "wide"), both),
        check_vma=False,
    )
```

```python
import functools
import jax
import jax.numpy as jnp
from jax import lax
from jax.experimental import pallas as pl
from jax.experimental.pallas import tpu as pltpu
from jax.sharding import PartitionSpec as P

DK, DV, BLOCK, EPS = 128, 256, 64, 1e-6
BF = jnp.bfloat16
F32 = jnp.float32


def mm(a, b):
    return jnp.dot(a.astype(BF), b.astype(BF), preferred_element_type=F32)


def mm_nt(a, b):
    return lax.dot_general(a.astype(BF), b.astype(BF), (((1,), (1,)), ((), ())), preferred_element_type=F32)


def mm_tn(a, b):
    return lax.dot_general(a.astype(BF), b.astype(BF), (((0,), (0,)), ((), ())), preferred_element_type=F32)


def split(a):
    high = a.astype(BF)
    return high, (a - high.astype(F32)).astype(BF)


def mm_fine(a, b):
    ah, al = split(a)
    bh, bl = split(b)
    return mm(ah, bh) + (mm(ah, bl) + mm(al, bh))


def unit_lower_inverses(systems, rows, cols):
    gap = rows ^ cols
    below = rows > cols
    unit = jnp.where(rows == cols, 1.0, 0.0)
    found = [unit - jnp.where(below & (gap < 2), a, 0.0) for a in systems]
    size = 2
    while size < systems[0].shape[0]:
        mask = below & (gap >= size) & (gap < 2 * size)
        inner = [mm_fine(jnp.where(mask, a, 0.0), t) for a, t in zip(systems, found)]
        found = [t - mm_fine(t, m) for t, m in zip(found, inner)]
        size *= 2
    return found


def block_tables(g_col, g_row, rows, cols):
    lower = rows >= cols
    return jnp.where(lower, jnp.exp(jnp.where(lower, g_col - g_row, 0.0)), 0.0)


def shifted(rows, before, back):
    if back == 0:
        return rows
    return jnp.concatenate([before[8 - back:], rows[:rows.shape[0] - back]], axis=0)


def conv_rows(rows, before, taps):
    count = taps.shape[0]
    total = taps[count - 1:count] * rows
    for back in range(1, count):
        total = total + taps[count - 1 - back:count - back] * shifted(rows, before, back)
    return total


def head_slices(heads, h):
    key = heads * DK
    return slice(h * DK, (h + 1) * DK), slice(key + h * DK, key + (h + 1) * DK), slice(2 * key + h * DV, 2 * key + (h + 1) * DV)


def unit_factor(rows):
    return lax.rsqrt(jnp.sum(rows * rows, axis=1, keepdims=True) + EPS)


def exact_tn(a, b):
    return lax.dot_general(a, b, (((0,), (0,)), ((), ())), precision=lax.Precision.HIGHEST, preferred_element_type=F32)


def softplus(x):
    return jnp.maximum(x, 0.0) + jnp.log(1.0 + jnp.exp(-jnp.abs(x)))


def decay_tables(heads, small, a_log, dt_bias, live, rows, cols):
    speed = -jnp.exp(a_log)
    biased = small[:, :heads] + dt_bias
    log_decay = speed * softplus(biased)
    sig = jax.nn.sigmoid(small[:, heads:2 * heads])
    upto = jnp.where(rows <= cols, 1.0, 0.0)
    run = exact_tn(upto, log_decay)
    run_row = exact_tn(log_decay, upto)
    return speed, biased, log_decay, sig, sig * live, run, run_row


def forward_kernel(heads, flag_ref, x_ref, rim_ref, taps_ref, small_ref, live_ref, alog_ref, dt_ref,
                   o_ref, e_ref, t_ref, z_ref, end_ref, carry, before_ref):
    step = pl.program_id(0)
    rows = lax.broadcasted_iota(jnp.int32, (BLOCK, BLOCK), 0)
    cols = lax.broadcasted_iota(jnp.int32, (BLOCK, BLOCK), 1)
    flag = flag_ref[step]

    @pl.when(step == 0)
    def _():
        before_ref[...] = rim_ref[8:16, :].astype(F32)
        unit = jnp.where(lax.broadcasted_iota(jnp.int32, (DK, DK), 0) == lax.broadcasted_iota(jnp.int32, (DK, DK), 1), 1.0, 0.0)
        for h in range(heads):
            carry[h, :, :DV] = jnp.zeros((DK, DV), F32)
            carry[h, :, DV:] = unit

    _, _, _, _, betas, run, run_row = decay_tables(heads, small_ref[...], alog_ref[...], dt_ref[...], live_ref[...], rows, cols)
    openings = flag * jnp.exp(run)
    closings = jnp.exp(run[BLOCK - 1:BLOCK] - run)

    def active(columns):
        c = conv_rows(x_ref[:, columns].astype(F32), before_ref[:, columns] * flag, taps_ref[:, columns])
        return c * jax.nn.sigmoid(c)

    tables, systems, parts = [], [], []
    for h in range(heads):
        qs, ks, vs = head_slices(heads, h)
        q, k, v = active(qs), active(ks), active(vs).astype(BF)
        q = (q * unit_factor(q) * DK ** (-0.5)).astype(BF)
        k = (k * unit_factor(k)).astype(BF)
        parts.append((q, k, v))
        table = block_tables(run[:, h:h + 1], run_row[h:h + 1, :], rows, cols)
        tables.append(table)
        systems.append(jnp.where(rows > cols, betas[:, h:h + 1] * table * mm_nt(k, k), 0.0))
    before_ref[...] = x_ref[BLOCK - 8:, :].astype(F32)
    inverses = unit_lower_inverses(systems, rows, cols)
    for h in range(heads):
        q, k, v = parts[h]
        beta, opening, closing = betas[:, h:h + 1], openings[:, h:h + 1], closings[:, h:h + 1]
        low_t = inverses[h].astype(BF)
        t_ref[0, h] = low_t
        u = mm(low_t, beta * v.astype(F32))
        w = mm(low_t, (beta * opening) * k.astype(F32))
        scores = mm_nt(q, k) * tables[h]
        state = carry[h]
        low_state = state.astype(BF)
        z_ref[0, h] = low_state
        reach = mm(jnp.concatenate([w.astype(BF), (opening * q.astype(F32)).astype(BF)], axis=0), low_state)
        c = jnp.concatenate([u, jnp.zeros((BLOCK, DK), F32)], axis=1) - reach[:BLOCK]
        low_c = c.astype(BF)
        out = reach[BLOCK:] + mm(scores, low_c)
        o_ref[:, h * DV:(h + 1) * DV] = out[:, :DV]
        e_ref[:, h * DK:(h + 1) * DK] = out[:, DV:].astype(BF)
        new = opening[BLOCK - 1:BLOCK] * state + mm_tn(closing * k.astype(F32), low_c)
        carry[h] = new
        end_ref[h] = new


def unfinish_kernel(heads, o_ref, e_ref, s_ref, gate_ref, live_ref, gain_ref, gm_ref, go_ref, gg_ref, ggain_ref, direct_ref):
    @pl.when(pl.program_id(0) == 0)
    def _():
        ggain_ref[...] = jnp.zeros_like(ggain_ref)
        direct_ref[...] = jnp.zeros_like(direct_ref)

    live = live_ref[...]
    gain = gain_ref[...]
    total = jnp.zeros((1, DV), F32)
    for h in range(heads):
        vs = slice(h * DV, (h + 1) * DV)
        e = e_ref[:, h * DK:(h + 1) * DK]
        y = (o_ref[:, vs] + mm(e, s_ref[h])) * live
        r = lax.rsqrt(jnp.mean(y * y, axis=1, keepdims=True) + EPS)
        gate = gate_ref[:, vs]
        sig = jax.nn.sigmoid(gate)
        act = gate * sig
        gm = gm_ref[:, vs]
        unit = y * r
        gn = gm * act
        total = total + jnp.sum(gn * unit, axis=0, keepdims=True)
        gn = gn * gain
        gg_ref[:, vs] = (gm * unit * gain * (sig * (1.0 + gate * (1.0 - sig)))).astype(BF)
        go = (r * (gn - unit * jnp.mean(gn * unit, axis=1, keepdims=True)) * live).astype(BF)
        go_ref[:, vs] = go
        direct_ref[h] += mm_tn(e, go)
    ggain_ref[...] += total


def unfinish(o, e, entry, gate, live, gain, gm, heads, tile=256):
    rows = o.shape[0]
    row = lambda width: pl.BlockSpec((tile, width), lambda i: (i, 0))
    return pl.pallas_call(
        functools.partial(unfinish_kernel, heads),
        grid=(rows // tile,),
        in_specs=[row(heads * DV), row(heads * DK), pl.BlockSpec((heads, DK, DV), lambda i: (0, 0, 0)), row(heads * DV),
                  row(1), pl.BlockSpec((1, DV), lambda i: (0, 0)), row(heads * DV)],
        out_specs=[row(heads * DV), row(heads * DV), pl.BlockSpec((1, DV), lambda i: (0, 0)),
                   pl.BlockSpec((heads, DK, DV), lambda i: (0, 0, 0))],
        out_shape=[jax.ShapeDtypeStruct((rows, heads * DV), BF), jax.ShapeDtypeStruct((rows, heads * DV), BF),
                   jax.ShapeDtypeStruct((1, DV), F32), jax.ShapeDtypeStruct((heads, DK, DV), F32)],
        compiler_params=pltpu.CompilerParams(vmem_limit_bytes=48 * 2**20),
    )(o, e, entry, gate, live, gain, gm)


def silu_back(c, grad):
    sig = jax.nn.sigmoid(c)
    return grad * (sig * (1.0 + c * (1.0 - sig)))


def backward_kernel(heads, flag_ref, x_ref, prev_ref, rim_ref, taps_ref, small_ref, live_ref, alog_ref, dt_ref, t_ref, z_ref,
                    go_ref, s_ref, exit_ref, gx_ref, gsmall_ref, gtaps_ref, gscalar_ref, carry, after_ref):
    step = pl.program_id(0)
    nb = pl.num_programs(0)
    at = nb - 1 - step
    rows = lax.broadcasted_iota(jnp.int32, (BLOCK, BLOCK), 0)
    cols = lax.broadcasted_iota(jnp.int32, (BLOCK, BLOCK), 1)
    last = lax.broadcasted_iota(jnp.int32, (BLOCK, 1), 0) == BLOCK - 1
    flag = flag_ref[at]
    taps_count = taps_ref.shape[0]

    @pl.when(step == 0)
    def _():
        carry[...] = exit_ref[...].astype(F32)
        after_ref[...] = jnp.zeros_like(after_ref)
        gtaps_ref[...] = jnp.zeros_like(gtaps_ref)
        gscalar_ref[...] = jnp.zeros_like(gscalar_ref)

    live = live_ref[...]
    speed, biased, log_decay, sig, betas, run, run_row = decay_tables(
        heads, small_ref[...], alog_ref[...], dt_ref[...], live, rows, cols)
    openings = flag * jnp.exp(run)
    closings = jnp.exp(run[BLOCK - 1:BLOCK] - run)
    row_block = pl.ds(pl.multiple_of(at * BLOCK, BLOCK), BLOCK)

    def inputs(columns):
        x = x_ref[:, columns].astype(F32)
        before = jnp.where(at == 0, rim_ref[8:16, columns].astype(F32), prev_ref[8:16, columns].astype(F32)) * flag
        return x, before, conv_rows(x, before, taps_ref[:, columns])

    def conv_back(columns, x, before, grad):
        taps = taps_ref[:, columns]
        later = after_ref[:, columns]
        longer = jnp.concatenate([grad, later], axis=0)
        gx = taps[taps_count - 1:taps_count] * grad
        sums = [jnp.sum(grad * x, axis=0, keepdims=True)]
        for back in range(1, taps_count):
            gx = gx + taps[taps_count - 1 - back:taps_count - back] * longer[back:back + BLOCK]
            sums.append(jnp.sum(grad * shifted(x, before, back), axis=0, keepdims=True))
        gx_ref[row_block, columns] = gx.astype(BF)
        gtaps_ref[:, columns] += jnp.concatenate(sums[::-1], axis=0)
        after_ref[:, columns] = grad[:8] * flag

    grad_runs, grad_betas = [], []
    for h in range(heads):
        qs, ks, vs = head_slices(heads, h)
        xq, bq, cq = inputs(qs)
        xk, bk, ck = inputs(ks)
        xv, bv, cv = inputs(vs)
        aq, ak = cq * jax.nn.sigmoid(cq), ck * jax.nn.sigmoid(ck)
        rq, rk_unit = unit_factor(aq), unit_factor(ak)
        uq, uk = aq * rq, ak * rk_unit
        q, k = (uq * DK ** (-0.5)).astype(BF), uk.astype(BF)
        v = (cv * jax.nn.sigmoid(cv)).astype(BF)
        qf, kf, vf = q.astype(F32), k.astype(F32), v.astype(F32)
        beta, opening, closing = betas[:, h:h + 1], openings[:, h:h + 1], closings[:, h:h + 1]
        gamma = opening[BLOCK - 1:BLOCK]
        table = block_tables(run[:, h:h + 1], run_row[h:h + 1, :], rows, cols)
        kk = mm_nt(k, k)
        scores = mm_nt(q, k) * table
        low_t = t_ref[0, h]
        u = mm(low_t, beta * vf)
        w = mm(low_t, (beta * opening) * kf)
        low_w = w.astype(BF)
        state = z_ref[0, h, :, :DV].astype(F32) + mm(z_ref[0, h, :, DV:], s_ref[h])
        low_s = state.astype(BF)
        c = u - mm(low_w, low_s)
        low_c = c.astype(BF)
        go = go_ref[:, h * DV:(h + 1) * DV]
        g = carry[h]
        low_g = g.astype(BF)
        low_ck = (closing * kf).astype(BF)
        low_oq = (opening * qf).astype(BF)
        dc = mm_tn(scores, go) + mm(low_ck, low_g)
        low_dc = dc.astype(BF)
        both = jnp.concatenate([go, low_dc], axis=0)
        carry[h] = gamma * g + mm_tn(jnp.concatenate([low_oq, -low_w], axis=0), both)
        dkeyed = mm_nt(low_c, low_g)
        dgamma = jnp.sum(jnp.sum(state * g, axis=1, keepdims=True), axis=0, keepdims=True)
        dscore = jnp.where(rows >= cols, mm_nt(go, low_c), 0.0)
        back = mm_nt(both, low_s)
        doq, dw = back[:BLOCK], -back[BLOCK:]
        drv = mm_tn(low_t, low_dc)
        drw = mm_tn(low_t, dw)
        low_drv, low_drw = drv.astype(BF), drw.astype(BF)
        da = jnp.where(rows > cols, -(mm_nt(low_drv, u) + mm_nt(low_drw, low_w)), 0.0)
        dat = da * table
        dkk = (beta * dat).astype(BF)
        dqk = (dscore * table).astype(BF)
        gq = (opening * doq + mm(dqk, k)) * DK ** (-0.5)
        gk = mm_tn(dqk, q) + mm(dkk, k) + mm_tn(dkk, k) + closing * dkeyed + (beta * opening) * drw
        gq = rq * (gq - uq * jnp.sum(gq * uq, axis=1, keepdims=True))
        gk = rk_unit * (gk - uk * jnp.sum(gk * uk, axis=1, keepdims=True))
        conv_back(qs, xq, bq, silu_back(cq, gq))
        conv_back(ks, xk, bk, silu_back(ck, gk))
        conv_back(vs, xv, bv, silu_back(cv, beta * drv))
        rk = jnp.sum(drw * kf, axis=1, keepdims=True)
        atk = dat * kk
        grad_betas.append(jnp.sum(drv * vf, axis=1, keepdims=True) + opening * rk + jnp.sum(atk, axis=1, keepdims=True))
        dopen = opening * (jnp.sum(doq * qf, axis=1, keepdims=True) + beta * rk)
        dclose = closing * jnp.sum(dkeyed * kf, axis=1, keepdims=True)
        e = dscore * scores + beta * atk
        by_col = exact_tn(e, jnp.ones((BLOCK, 8), F32))[:, :1]
        dg = jnp.sum(e, axis=1, keepdims=True) - by_col + dopen - dclose
        grad_runs.append(dg + jnp.where(last, jnp.sum(dclose, axis=0, keepdims=True) + dgamma * gamma, 0.0))

    lane = lax.broadcasted_iota(jnp.int32, (BLOCK, heads), 1)
    grad_run = sum(jnp.where(lane == h, grad_runs[h], 0.0) for h in range(heads))
    grad_beta = sum(jnp.where(lane == h, grad_betas[h], 0.0) for h in range(heads))
    grad_log = exact_tn(jnp.where(cols <= rows, 1.0, 0.0), grad_run)
    grad_biased = grad_log * speed * jax.nn.sigmoid(biased)
    gsmall_ref[:, :heads] = grad_biased
    gsmall_ref[:, heads:] = grad_beta * live * sig * (1.0 - sig)
    gscalar_ref[0:1, :] += jnp.sum(grad_log * log_decay, axis=0, keepdims=True)
    gscalar_ref[1:2, :] += jnp.sum(grad_biased, axis=0, keepdims=True)

    @pl.when(step == nb - 1)
    def _():
        longer = jnp.concatenate([jnp.zeros((16, taps_ref.shape[1]), F32), after_ref[...]], axis=0)
        gx = jnp.zeros((16, taps_ref.shape[1]), F32)
        for back in range(1, taps_count):
            gx = gx + taps_ref[taps_count - 1 - back:taps_count - back, :] * longer[back:back + 16]
        gx_ref[pl.ds(nb * BLOCK, 16), :] = gx.astype(BF)


MESH = pl.DeviceIdType.MESH


def position():
    w = lax.axis_index("wide")
    return w, w // 2, w % 2, lax.axis_index("narrow")


def greet(line=0, pair=False, cube=False, bits=(), places=0, rim=False):
    w, place, side, n = position()
    barrier = pltpu.get_barrier_semaphore()

    def signal(*device):
        pl.semaphore_signal(barrier, inc=1, device_id=device, device_id_type=MESH)

    count = 0
    if pair:
        signal(w + 1 - 2 * side, n)
        count += 1
    if cube:
        signal(w, n ^ 1)
        signal(w, n ^ 2)
        count += 2
    for bit in bits:
        signal(w ^ bit, n)
        count += 1
    if line:
        @pl.when(place > 0)
        def _():
            signal(w - 2, n)

        @pl.when(place < line - 1)
        def _():
            signal(w + 2, n)

        count = count + jnp.where(place > 0, 1, 0) + jnp.where(place < line - 1, 1, 0)
    if rim:
        @pl.when((side == 0) & (place > 0))
        def _():
            signal(w - 1, n)

        @pl.when((side == 1) & (place < line - 1))
        def _():
            signal(w + 1, n)

        count = count + jnp.where(side == 0, jnp.where(place > 0, 1, 0), jnp.where(place < line - 1, 1, 0))
    for k in range(1, places):
        for there in (place + k, place - k):
            @pl.when((there >= 0) & (there < places))
            def _():
                signal(2 * there + side, n)

    pl.semaphore_wait(barrier, count + max(places - 1, 0))


def row_cuts(rows, chunks):
    units = rows // 16
    chunks = min(chunks, units)
    edges = [16 * (units * c // chunks) for c in range(chunks + 1)]
    return [(edges[c], edges[c + 1] - edges[c]) for c in range(chunks)]


class LineGather:
    def __init__(self, places, cuts, sources, others, targets, local_sems, send_sems, recv_sems):
        self.places, self.sources, self.others, self.targets = places, sources, others, targets
        self.local_sems, self.send_sems, self.recv_sems = local_sems, send_sems, recv_sems
        self.w, self.place, self.side, self.n = position()
        self.items = [(i,) + cut for i, found in enumerate(cuts) for cut in found]

    def both(self, item):
        return self.others[self.items[item][0]] is not None

    def copy(self, item, slot, way, own=False):
        i, start, size = self.items[item]
        rows = pl.ds(start, size)
        source = self.targets[i].at[slot, rows]
        if own:
            source = (self.others if way == 0 and self.both(item) else self.sources)[i].at[rows]
        device = [self.w + 1 - 2 * self.side, self.w + 2, self.w - 2][way]
        return pltpu.make_async_remote_copy(
            src_ref=source, dst_ref=self.targets[i].at[slot, rows], send_sem=self.send_sems.at[way, slot, item],
            recv_sem=self.recv_sems.at[slot, item], device_id=(device, self.n), device_id_type=MESH)

    def start(self):
        for i, source in enumerate(self.sources):
            pltpu.make_async_copy(source, self.targets[i].at[self.w], self.local_sems.at[i]).start()
        for item in range(len(self.items)):
            self.copy(item, self.w, 0, True).start()
            self.along(item, self.w, 1, True)
            self.along(item, self.w, 2, True)

    def along(self, item, slot, way, own=False):
        @pl.when(self.place < self.places - 1 if way == 1 else self.place > 0)
        def _():
            self.copy(item, slot, way, own).start()

    def events(self):
        items = range(len(self.items))
        found = [(item, 0, 1) for item in items if self.both(item)]
        return found + [(item, t, s) for t in range(1, self.places) for item in items
                        for s in ((0, 1) if self.both(item) else (0,))]

    def run(self, event):
        item, t, s = event
        if t == 0:
            slot = self.w + 1 - 2 * self.side
            self.copy(item, slot, 0).wait_recv()
            self.along(item, slot, 1)
            self.along(item, slot, 2)
            return

        for way, there in ((1, self.place - t), (2, self.place + t)):
            slot = 2 * there + (self.side if s == 0 else 1 - self.side)

            @pl.when((there >= 0) & (there < self.places))
            def _():
                self.copy(item, slot, way).wait_recv()
                self.along(item, slot, way)
                if not self.both(item):
                    self.copy(item, slot, 0).start()

    def finish(self):
        for item in range(len(self.items)):
            if not self.both(item):
                for t in range(self.places):
                    self.copy(item, 2 * t + 1 - self.side, 0).wait_recv()
        for i, source in enumerate(self.sources):
            pltpu.make_async_copy(source, self.targets[i].at[self.w], self.local_sems.at[i]).wait()
        for item in range(len(self.items)):
            both = self.both(item)
            if both:
                self.copy(item, self.w, 0, True).wait_send()
            for t in range(self.places):
                if not both:
                    self.copy(item, 2 * t + self.side, 0).wait_send()
                for s in ((0, 1) if both else (0,)):
                    slot = 2 * t + (self.side if s == 0 else 1 - self.side)

                    @pl.when((self.place < self.places - 1) & (t <= self.place))
                    def _():
                        self.copy(item, slot, 1).wait_send()

                    @pl.when((self.place > 0) & (t >= self.place))
                    def _():
                        self.copy(item, slot, 2).wait_send()

    @staticmethod
    def scratch(count, cuts):
        items = sum(len(found) for found in cuts)
        return [pltpu.SemaphoreType.DMA((len(cuts),)), pltpu.SemaphoreType.DMA((3, count, items)),
                pltpu.SemaphoreType.DMA((count, items))]


class PairRows:
    def __init__(self, places, source, target, rim, send_sems, recv_sems, rim_send, rim_recv):
        self.places, self.source, self.target, self.rim = places, source, target, rim
        self.send_sems, self.recv_sems, self.rim_sems = send_sems, recv_sems, (rim_send, rim_recv)
        self.w, self.place, self.side, self.n = position()

    def copy(self, number, part):
        size = self.target.shape[1]
        device = [(self.w + 1 - 2 * self.side, self.n), (self.w, self.n ^ 2), (self.w, self.n ^ 1), (self.w, self.n ^ 1)][number]
        source = self.source.at[pl.ds(part * size, size)] if number == 0 else self.target.at[part]
        return pltpu.make_async_remote_copy(
            src_ref=source, dst_ref=self.target.at[part], send_sem=self.send_sems.at[number],
            recv_sem=self.recv_sems.at[part], device_id=device, device_id_type=MESH)

    def rim_copy(self, side):
        size = self.rim.shape[0]
        return pltpu.make_async_remote_copy(
            src_ref=self.source.at[pl.ds(self.source.shape[0] - size, size)], dst_ref=self.rim,
            send_sem=self.rim_sems[0].at[side], recv_sem=self.rim_sems[1],
            device_id=(2 * self.place + 2 + side, self.n), device_id_type=MESH)

    def sends_rim(self):
        return (self.side == 1) & (self.place < self.places - 1)

    def start(self):
        self.copy(0, self.n).start()

        @pl.when(self.sends_rim())
        def _():
            self.rim_copy(0).start()
            self.rim_copy(1).start()

    def events(self):
        return [0, 1]

    def run(self, event):
        if event == 0:
            self.copy(0, self.n).wait_recv()
            self.copy(1, self.n).start()
            self.copy(2, self.n).start()
        else:
            self.copy(1, self.n ^ 2).wait_recv()
            self.copy(3, self.n ^ 2).start()

    def finish(self):
        self.copy(2, self.n ^ 1).wait_recv()
        self.copy(3, self.n ^ 3).wait_recv()
        for number in range(4):
            self.copy(number, self.n ^ 2 if number == 3 else self.n).wait_send()

        @pl.when(self.place > 0)
        def _():
            self.rim_copy(0).wait_recv()

        @pl.when(self.sends_rim())
        def _():
            self.rim_copy(0).wait_send()
            self.rim_copy(1).wait_send()


def gather_kernel(places, cuts, halved, rows, *refs):
    m = len(cuts)
    sources, refs = refs[:m], refs[m:]
    others, refs = iter(refs[:sum(halved)]), refs[sum(halved):]
    others = [next(others) if h else None for h in halved]
    rows_in, refs = refs[:rows], refs[rows:]
    targets, rows_out, refs = refs[:m], refs[m:m + 2 * rows], refs[m + 2 * rows:]
    groups = [LineGather(places, cuts, sources, others, targets, *refs[:3])]
    if rows:
        groups.append(PairRows(places, rows_in[0], *rows_out, *refs[3:]))
    greet(line=places, pair=True, cube=bool(rows), rim=bool(rows))
    for group in groups[::-1]:
        group.start()
    for group, event in merged(groups):
        group.run(event)
    for group in groups[::-1]:
        group.finish()


def flat_blocks(gathered):
    return [g.reshape((g.shape[0] * g.shape[1],) + g.shape[2:]) for g in gathered]


def line_gather(values, call_id, chunks=4, rows=None):
    count = lax.axis_size("wide")
    halved = [isinstance(value, tuple) for value in values]
    sources = [value[0] if h else value for value, h in zip(values, halved)]
    others = [value[1] for value, h in zip(values, halved) if h]
    cuts = [row_cuts(value.shape[0], chunks if value.shape[0] > 64 else 1) for value in sources]
    hbm = pl.BlockSpec(memory_space=pl.ANY)
    shapes = [jax.ShapeDtypeStruct((count,) + value.shape, value.dtype) for value in sources]
    scratch = LineGather.scratch(count, cuts)
    if rows is not None:
        narrow = lax.axis_size("narrow")
        others.append(rows)
        shapes.append(jax.ShapeDtypeStruct((narrow, rows.shape[0] // narrow, rows.shape[1]), rows.dtype))
        shapes.append(jax.ShapeDtypeStruct((16, rows.shape[1]), rows.dtype))
        scratch += [pltpu.SemaphoreType.DMA((4,)), pltpu.SemaphoreType.DMA((narrow,)), pltpu.SemaphoreType.DMA((2,)),
                    pltpu.SemaphoreType.DMA]
    found = pl.pallas_call(
        functools.partial(gather_kernel, count // 2, cuts, halved, 0 if rows is None else 1),
        out_shape=shapes,
        in_specs=[hbm] * (len(sources) + len(others)),
        out_specs=[hbm] * len(shapes),
        scratch_shapes=scratch,
        compiler_params=pltpu.CompilerParams(collective_id=call_id, has_side_effects=True),
    )(*sources, *others)
    return flat_blocks(found[:-1]) + [found[-1]] if rows is not None else flat_blocks(found)


class LineScatter:
    def __init__(self, places, cuts, paired, sources, owns, pairs, lines, load_sems, pair_send, pair_recv, right_send,
                 right_recv, left_send, left_recv):
        self.places, self.paired = places, paired
        self.sources, self.owns, self.pairs, self.lines = sources, owns, pairs, lines
        self.load_sems, self.pair_sems = load_sems, (pair_send, pair_recv)
        self.right_sems, self.left_sems = (right_send, right_recv), (left_send, left_recv)
        self.w, self.place, self.side, self.n = position()
        self.items = [(i,) + cut for i, found in enumerate(cuts) for cut in found]
        self.order = [(t, item) for j in range(places // 2) for item in range(len(self.items)) for t in (places - 1 - j, j)]

    def remote(self, source, target, sems, t, item, device):
        return pltpu.make_async_remote_copy(src_ref=source, dst_ref=target, send_sem=sems[0].at[t, item],
                                            recv_sem=sems[1].at[t, item], device_id=(device, self.n), device_id_type=MESH)

    def at(self, t, item):
        i, start, size = self.items[item]
        return (t, pl.ds(start, size)) if self.paired else (t, slice(None), pl.ds(start, size))

    def across(self, t, item):
        i = self.items[item][0]
        source = self.sources[i].at[2 * t + 1 - self.side, self.at(t, item)[1]]
        return self.remote(source, self.pairs[i].at[self.at(t, item)], self.pair_sems, t, item, self.w + 1 - 2 * self.side)

    def load(self, t, item):
        i = self.items[item][0]
        slot = 2 * t + self.side if self.paired else t
        return pltpu.make_async_copy(self.sources[i].at[self.at(slot, item)], self.owns[i].at[self.at(t, item)],
                                     self.load_sems.at[t, item])

    def right(self, t, item):
        i, at = self.items[item][0], self.at(t, item)
        return self.remote(self.owns[i].at[at], self.lines[i].at[at], self.right_sems, t, item, self.w + 2)

    def left(self, t, item, arriving=False):
        i, at = self.items[item][0], self.at(t, item)
        slot = jnp.where(t == self.place - (0 if arriving else 1), self.places, t)
        return self.remote(self.owns[i].at[at], self.lines[i].at[(slot,) + at[1:]], self.left_sems, t, item, self.w - 2)

    ahead = 4

    def start(self):
        if self.sources is not None:
            for t, item in self.order:
                self.load(t, item).start()
        if self.paired:
            for t, item in self.order[:self.ahead]:
                self.across(t, item).start()

    def events(self):
        return self.order

    def run(self, event):
        t, item = event
        i, at = self.items[item][0], self.at(t, item)
        own, place, places = self.owns[i], self.place, self.places

        def add(other):
            own[at] = (own[at].astype(F32) + other[at].astype(F32)).astype(own.dtype)

        if self.sources is not None:
            self.load(t, item).wait()
        if self.paired:
            following = self.order.index(event) + self.ahead
            if following < len(self.order):
                self.across(*self.order[following]).start()
            self.across(t, item).wait_recv()
            add(self.pairs[i])

        @pl.when(t > place)
        def _():
            @pl.when(place > 0)
            def _():
                self.right(t, item).wait_recv()
                add(self.lines[i])

            self.right(t, item).start()

        @pl.when(t < place)
        def _():
            @pl.when(place < places - 1)
            def _():
                self.left(t, item, True).wait_recv()
                add(self.lines[i])

            self.left(t, item).start()

    def finish(self, outs, theirs=None):
        place, copies = self.place, []
        for item in range(len(self.items)):
            i, start, size = self.items[item]
            own, line, at, rows = self.owns[i], self.lines[i], self.at(place, item), pl.ds(start, size)

            @pl.when(place > 0)
            def _():
                self.right(place, item).wait_recv()
                own[at] = (own[at].astype(F32) + line[at].astype(F32)).astype(own.dtype)

            @pl.when(place < self.places - 1)
            def _():
                self.left(place, item, True).wait_recv()
                own[at] = (own[at].astype(F32) + line[(self.places,) + at[1:]].astype(F32)).astype(own.dtype)

            if self.paired:
                outs[i][rows] = own[at].astype(F32)
            else:
                copy = self.remote(own.at[place, 1 - self.side, rows], self.pairs[i].at[rows], self.pair_sems, 0, item,
                                   self.w + 1 - 2 * self.side)
                copy.start()
                copies.append((i, rows, copy))
                outs[i][rows] = own[place, self.side, rows].astype(F32)
        for i, rows, copy in copies:
            copy.wait()
            theirs[i][rows] = self.pairs[i][rows].astype(F32)
        for t in range(self.places):
            for item in range(len(self.items)):
                if self.paired:
                    self.across(t, item).wait_send()

                @pl.when(t > place)
                def _():
                    self.right(t, item).wait_send()

                @pl.when(t < place)
                def _():
                    self.left(t, item).wait_send()

    @staticmethod
    def scratch(places, cuts, paired, values):
        owns = [pltpu.VMEM((places,) + value.shape[1:], value.dtype) for value in values]
        pairs = owns if paired else [pltpu.VMEM(value.shape[2:], value.dtype) for value in values]
        lines = [pltpu.VMEM((places + 1,) + value.shape[1:], value.dtype) for value in values]
        items = sum(len(found) for found in cuts)
        return owns + pairs + lines + [pltpu.SemaphoreType.DMA((places, items))] * 7

    @staticmethod
    def take(places, cuts, paired, sources, refs):
        m = len(cuts)
        amount = 3 * m + 7
        groups = [refs[m * g:m * (g + 1)] for g in range(3)]
        return LineScatter(places, cuts, paired, sources, *groups, *refs[3 * m:amount]), refs[amount:]


class CubeScatter:
    def __init__(self, source, own, near, second, third, load_sems, send_sems, recv_sems):
        self.source, self.own, self.near, self.second, self.third = source, own, near, second, third
        self.load_sems, self.send_sems, self.recv_sems = load_sems, send_sems, recv_sems
        self.w, self.place, self.side, self.n = position()
        self.half = own.shape[2] // 2
        self.order = (3, 1, 2, 0)

    def block(self, s, m):
        return (self.side ^ s) * 4 + (self.n ^ m)

    def remote(self, number, source, target, device):
        return pltpu.make_async_remote_copy(src_ref=source, dst_ref=target, send_sem=self.send_sems.at[number],
                                            recv_sem=self.recv_sems.at[number], device_id=device, device_id_type=MESH)

    def cut(self, part):
        return pl.ds(part * self.half, self.half)

    def first(self, j):
        return self.remote(j, self.source.at[self.block(j // 2, 1 + 2 * (j % 2))], self.near.at[j], (self.w, self.n ^ 1))

    def load(self, j):
        return pltpu.make_async_copy(self.source.at[self.block(j // 2, 2 * (j % 2))], self.own.at[j], self.load_sems.at[j])

    def device(self, part, stage):
        return (self.w, self.n ^ 2) if part == stage else (self.w + 1 - 2 * self.side, self.n)

    def middle(self, part, k):
        j = 2 * k + 1 if part == 0 else 2 + k
        return self.remote(4 + 2 * part + k, self.own.at[j, :, self.cut(part)], self.second.at[part, k], self.device(part, 0))

    def end(self, part):
        j = 2 if part == 0 else 1
        return self.remote(8 + part, self.own.at[j, :, self.cut(part)], self.third.at[part], self.device(part, 1))

    def start(self):
        for j in self.order:
            self.load(j).start()
        for j in self.order:
            self.first(j).start()

    def events(self):
        return [("near", j) for j in self.order] + [("middle", k) for k in (1, 0)]

    def run(self, event):
        kind, j = event
        if kind == "near":
            self.load(j).wait()
            self.first(j).wait_recv()
            self.own[j] = (self.own[j].astype(F32) + self.near[j].astype(F32)).astype(self.own.dtype)
            if j % 2 == 1:
                self.middle(0, j // 2).start()
            if j // 2 == 1:
                self.middle(1, j % 2).start()
            return
        for part in (0, 1):
            self.middle(part, j).wait_recv()
            target = (2 * j if part == 0 else j, slice(None), self.cut(part))
            self.own[target] = (self.own[target].astype(F32) + self.second[part, j].astype(F32)).astype(self.own.dtype)
            if j == 1:
                self.end(part).start()

    def finish(self, out):
        for part in (0, 1):
            self.end(part).wait_recv()
            out[:, self.cut(part)] = self.own[0, :, self.cut(part)].astype(F32) + self.third[part].astype(F32)
        for j in range(4):
            self.first(j).wait_send()
        for part in (0, 1):
            for k in (0, 1):
                self.middle(part, k).wait_send()
            self.end(part).wait_send()

    @staticmethod
    def scratch(value):
        rows, columns = value.shape[1:]
        block = pltpu.VMEM((4, rows, columns), value.dtype)
        return [block, block, pltpu.VMEM((2, 2, rows, columns // 2), value.dtype),
                pltpu.VMEM((2, rows, columns // 2), value.dtype), pltpu.SemaphoreType.DMA((4,)),
                pltpu.SemaphoreType.DMA((10,)), pltpu.SemaphoreType.DMA((10,))]


class NarrowScatter:
    def __init__(self, sources, owns, nears, fars, load_sems, send_sems, recv_sems):
        self.sources, self.owns, self.nears, self.fars = sources, owns, nears, fars
        self.load_sems, self.send_sems, self.recv_sems = load_sems, send_sems, recv_sems
        self.w, self.place, self.side, self.n = position()

    def cut(self, i, m):
        size = self.owns[i].shape[2]
        return self.sources[i].at[:, pl.ds(pl.multiple_of((self.n ^ m) * size, size), size)]

    def remote(self, i, number, source, target, bit):
        return pltpu.make_async_remote_copy(
            src_ref=source, dst_ref=target, send_sem=self.send_sems.at[i, number], recv_sem=self.recv_sems.at[i, number],
            device_id=(self.w, self.n ^ bit), device_id_type=MESH)

    def near(self, i, m):
        return self.remote(i, m, self.cut(i, 1 + 2 * m), self.nears[i].at[m], 1)

    def far(self, i):
        return self.remote(i, 2, self.owns[i].at[1], self.fars[i], 2)

    def load(self, i, m):
        return pltpu.make_async_copy(self.cut(i, 2 * m), self.owns[i].at[m], self.load_sems.at[i, m])

    def start(self):
        for i in range(len(self.owns)):
            for m in (1, 0):
                self.load(i, m).start()
        for i in range(len(self.owns)):
            for m in (1, 0):
                self.near(i, m).start()

    def events(self):
        return [(kind, i) for i in range(len(self.owns)) for kind in ("high", "low")]

    def run(self, event):
        kind, i = event
        m = 1 if kind == "high" else 0
        self.load(i, m).wait()
        self.near(i, m).wait_recv()
        self.owns[i][m] = (self.owns[i][m].astype(F32) + self.nears[i][m].astype(F32)).astype(self.owns[i].dtype)
        if m == 1:
            self.far(i).start()

    def finish(self, outs):
        for i, out in enumerate(outs):
            self.far(i).wait_recv()
            out[...] = self.owns[i][0].astype(F32) + self.fars[i][...].astype(F32)
            for m in (0, 1):
                self.near(i, m).wait_send()
            self.far(i).wait_send()

    @staticmethod
    def scratch(values, narrow):
        shapes = [(value.shape[0], value.shape[1] // narrow) for value in values]
        pairs = [pltpu.VMEM((2,) + shape, value.dtype) for shape, value in zip(shapes, values)]
        m = len(values)
        return (pairs * 2 + [pltpu.VMEM(shape, value.dtype) for shape, value in zip(shapes, values)]
                + [pltpu.SemaphoreType.DMA((m, 2)), pltpu.SemaphoreType.DMA((m, 3)), pltpu.SemaphoreType.DMA((m, 3))])

    @staticmethod
    def take(sources, refs):
        m = len(sources)
        amount = 3 * m + 3
        return NarrowScatter(sources, refs[:m], refs[m:2 * m], refs[2 * m:3 * m], *refs[3 * m:amount]), refs[amount:]


def cube_scatter_kernel(x_ref, o_ref, *refs):
    cube = CubeScatter(x_ref, *refs)
    greet(pair=True, cube=True)
    cube.start()
    for event in cube.events():
        cube.run(event)
    cube.finish(o_ref)


def cube_scatter(value, call_id):
    return pl.pallas_call(
        cube_scatter_kernel,
        out_shape=jax.ShapeDtypeStruct(value.shape[1:], F32),
        in_specs=[pl.BlockSpec(memory_space=pl.ANY)],
        out_specs=pl.BlockSpec(memory_space=pltpu.VMEM),
        scratch_shapes=CubeScatter.scratch(value),
        compiler_params=pltpu.CompilerParams(collective_id=call_id, has_side_effects=True, vmem_limit_bytes=32 * 2**20),
    )(value)


def cube_gather_kernel(x_ref, o_ref, local_sem, send_sems, recv_sems):
    w, place, side, n = position()
    half = x_ref.shape[1] // 2
    devices = [(w + 1 - 2 * side, n), (w, n ^ 2), (w, n ^ 1)]

    def copy(s, m, part, way, own=False):
        slot = (side ^ s) * 4 + (n ^ m)
        columns = pl.ds(part * half, half)
        source = x_ref.at[:, columns] if own else o_ref.at[slot, :, columns]
        return pltpu.make_async_remote_copy(
            src_ref=source, dst_ref=o_ref.at[slot, :, columns], send_sem=send_sems.at[way, slot, part],
            recv_sem=recv_sems.at[slot, part], device_id=devices[way], device_id_type=MESH)

    greet(pair=True, cube=True)
    local = pltpu.make_async_copy(x_ref, o_ref.at[side * 4 + n], local_sem)
    local.start()
    sent = []

    def send(s, m, part, way, own=False):
        found = copy(s, m, part, way, own)
        found.start()
        sent.append(found)

    for way in (0, 1, 2):
        for part in (0, 1):
            send(0, 0, part, way, True)
    copy(1, 0, 0, 0).wait_recv()
    send(1, 0, 0, 1)
    copy(0, 2, 1, 1).wait_recv()
    send(0, 2, 1, 0)
    send(1, 0, 0, 2)
    send(0, 2, 1, 2)
    copy(0, 2, 0, 1).wait_recv()
    send(0, 2, 0, 2)
    copy(1, 0, 1, 0).wait_recv()
    send(1, 0, 1, 2)
    copy(1, 2, 0, 1).wait_recv()
    send(1, 2, 0, 2)
    copy(1, 2, 1, 0).wait_recv()
    send(1, 2, 1, 2)
    for s in (0, 1):
        for m in (1, 3):
            for part in (0, 1):
                copy(s, m, part, 2).wait_recv()
    local.wait()
    for found in sent:
        found.wait_send()


def cube_gather(value, call_id):
    return pl.pallas_call(
        cube_gather_kernel,
        out_shape=jax.ShapeDtypeStruct((8,) + value.shape, value.dtype),
        in_specs=[pl.BlockSpec(memory_space=pltpu.VMEM)],
        out_specs=pl.BlockSpec(memory_space=pl.ANY),
        scratch_shapes=[pltpu.SemaphoreType.DMA, pltpu.SemaphoreType.DMA((3, 8, 2)), pltpu.SemaphoreType.DMA((8, 2))],
        compiler_params=pltpu.CompilerParams(collective_id=call_id, has_side_effects=True, vmem_limit_bytes=16 * 2**20),
    )(value).reshape(8 * value.shape[0], value.shape[1])


class SmallSums:
    def __init__(self, steps, value, stages, inbox, cube, place_send, place_recv, cube_send, cube_recv):
        self.steps, self.value, self.stages, self.inbox, self.cube = steps, value, stages, inbox, cube
        self.place_sems, self.cube_sems = (place_send, place_recv), (cube_send, cube_recv)
        self.w, self.place, self.side, self.n = position()

    def step(self, i):
        return pltpu.make_async_remote_copy(
            src_ref=self.stages.at[i], dst_ref=self.inbox.at[i], send_sem=self.place_sems[0].at[i],
            recv_sem=self.place_sems[1].at[i], device_id=(self.w ^ (2 << i), self.n), device_id_type=MESH)

    def spread(self, way, s, m):
        slot = (self.side ^ s) * 4 + (self.n ^ m)
        device = [(self.w + 1 - 2 * self.side, self.n), (self.w, self.n ^ 2), (self.w, self.n ^ 1)][way]
        return pltpu.make_async_remote_copy(
            src_ref=self.cube.at[slot], dst_ref=self.cube.at[slot], send_sem=self.cube_sems[0].at[way, slot],
            recv_sem=self.cube_sems[1].at[slot], device_id=device, device_id_type=MESH)

    sent = {0: [(0, 0)], 1: [(0, 0), (1, 0)], 2: [(0, 0), (1, 0), (0, 2), (1, 2)]}
    arriving = {0: [(1, 0)], 1: [(0, 2), (1, 2)], 2: [(0, 1), (1, 1), (0, 3), (1, 3)]}

    def send(self, way):
        for s, m in self.sent[way]:
            self.spread(way, s, m).start()

    def start(self):
        self.stages[0] = self.value[...]
        self.step(0).start()

    def events(self):
        return [("place", i) for i in range(self.steps)] + [("cube", way) for way in range(3)]

    def run(self, event):
        kind, i = event
        if kind == "place":
            self.step(i).wait_recv()
            self.stages[i + 1] = self.stages[i] + self.inbox[i]
            if i + 1 < self.steps:
                self.step(i + 1).start()
            else:
                self.cube[self.side * 4 + self.n] = self.stages[i + 1]
                self.send(0)
            return
        for s, m in self.arriving[i]:
            self.spread(i, s, m).wait_recv()
        if i < 2:
            self.send(i + 1)

    def finish(self, out):
        out[...] = self.cube[...]
        for i in range(self.steps):
            self.step(i).wait_send()
        for way in range(3):
            for s, m in self.sent[way]:
                self.spread(way, s, m).wait_send()

    @staticmethod
    def scratch(steps, value):
        rows = pltpu.VMEM((steps + 1,) + value.shape, value.dtype)
        return [rows, rows, pltpu.VMEM((8,) + value.shape, value.dtype), pltpu.SemaphoreType.DMA((steps,)),
                pltpu.SemaphoreType.DMA((steps,)), pltpu.SemaphoreType.DMA((3, 8)), pltpu.SemaphoreType.DMA((8,))]


def place_bits(places):
    return [2 << i for i in range(places.bit_length() - 1)]


def scatter_kernel(places, half_cuts, pair_cuts, cubes, small, narrow, *refs):
    hm, pm = len(half_cuts), len(pair_cuts)

    def take(count):
        nonlocal refs
        found, refs = refs[:count], refs[count:]
        return found

    halves, pairs, cube_in, small_in = take(hm), take(pm), take(cubes), take(small)
    half_outs, half_theirs, pair_outs, cube_outs, small_outs = take(hm), take(hm), take(pm), take(cubes), take(small)
    groups, ends = [], []
    if hm:
        half, refs = LineScatter.take(places, half_cuts, False, halves, refs)
        groups.append(half)
        ends.append(lambda: half.finish(half_outs, half_theirs))
    if pm:
        pair, refs = LineScatter.take(places, pair_cuts, True, pairs, refs)
        groups.append(pair)
        ends.append(lambda: pair.finish(pair_outs))
    for source, out in zip(cube_in, cube_outs):
        cube = CubeScatter(source, *take(7))
        groups.append(cube)
        ends.append(lambda cube=cube, out=out: cube.finish(out))
    if small:
        sums = SmallSums(len(place_bits(places)), small_in[0], *take(7))
        groups.append(sums)
        ends.append(lambda: sums.finish(small_outs[0]))
    greet(line=places, pair=True, cube=bool(cubes), bits=place_bits(places) if small else ())
    for group in groups[::-1]:
        group.start()
    for group, event in merged(groups):
        group.run(event)
    for end in ends[:0:-1]:
        end()
    if cubes == 2:
        w, place, side, n = position()
        rim_in, rim_send, rim_recv = take(3)
        rim = pltpu.make_async_remote_copy(src_ref=cube_outs[1], dst_ref=rim_in, send_sem=rim_send, recv_sem=rim_recv,
                                           device_id=(w - 2, n), device_id_type=MESH)
        last = (side == 1) & (n == narrow - 1)

        @pl.when(last & (place > 0))
        def _():
            rim.start()

        @pl.when(last & (place < places - 1))
        def _():
            rim.wait_recv()
            rows = pl.ds(cube_outs[0].shape[0] - rim_in.shape[0], rim_in.shape[0])
            cube_outs[0][rows] = cube_outs[0][rows] + rim_in[...]

        @pl.when(last & (place > 0))
        def _():
            rim.wait_send()
    ends[0]()


def merged(groups):
    found = []
    for order, group in enumerate(groups):
        events = group.events()
        found += [((i + 0.5) / len(events), order, i, group, event) for i, event in enumerate(events)]
    return [(group, event) for _, _, _, group, event in sorted(found, key=lambda e: e[:3])]


def place_blocks(term, places):
    return term.reshape(places, 2, term.shape[0] // (2 * places), term.shape[1])


def line_scatter(halves, pairs, cubes, small, call_id, chunks=4):
    places = lax.axis_size("wide") // 2
    halves = [place_blocks(term, places) for term in halves]
    half_cuts = [row_cuts(term.shape[2], chunks) for term in halves]
    pair_cuts = [row_cuts(term.shape[1], chunks if term.shape[1] > 64 else 1) for term in pairs]
    shapes = [term.shape[2:] for term in halves] * 2 + [term.shape[1:] for term in list(pairs) + list(cubes)]
    shapes += [(8,) + term.shape for term in small]
    scratch = []
    if halves:
        scratch += LineScatter.scratch(places, half_cuts, False, halves)
    if pairs:
        scratch += LineScatter.scratch(places, pair_cuts, True, pairs)
    for term in cubes:
        scratch += CubeScatter.scratch(term)
    for term in small:
        scratch += SmallSums.scratch(len(place_bits(places)), term)
    if cubes:
        scratch += [pltpu.VMEM(cubes[1].shape[1:], F32), pltpu.SemaphoreType.DMA, pltpu.SemaphoreType.DMA]
    vmem = pl.BlockSpec(memory_space=pltpu.VMEM)
    found = pl.pallas_call(
        functools.partial(scatter_kernel, places, half_cuts, pair_cuts, len(cubes), len(small), lax.axis_size("narrow")),
        out_shape=[jax.ShapeDtypeStruct(shape, F32) for shape in shapes],
        in_specs=[pl.BlockSpec(memory_space=pl.ANY)] * (len(halves) + len(pairs) + len(cubes)) + [vmem] * len(small),
        out_specs=[vmem] * len(shapes),
        scratch_shapes=scratch,
        compiler_params=pltpu.CompilerParams(collective_id=call_id, has_side_effects=True, vmem_limit_bytes=56 * 2**20),
    )(*halves, *pairs, *cubes, *small)
    h, p, c = len(halves), len(pairs), len(cubes)
    return list(zip(found[:h], found[h:2 * h])), found[2 * h:2 * h + p], found[2 * h + p:2 * h + p + c], found[2 * h + p + c:]


class PassStates:
    def __init__(self, places, forward, mine, turned, total, send_sems, recv_sems):
        self.places, self.forward, self.ahead = places, forward, 1 if forward else -1
        self.mine, self.turned, self.total = mine, turned, total
        self.send_sems, self.recv_sems = send_sems, recv_sems
        self.w, self.place, self.side, self.n = position()

    def copy(self, k):
        return pltpu.make_async_remote_copy(
            src_ref=self.mine, dst_ref=self.turned.at[k], send_sem=self.send_sems.at[k], recv_sem=self.recv_sems.at[k],
            device_id=(self.w + 2 * self.ahead * k, self.n), device_id_type=MESH)

    def inside(self, there):
        return (there >= 0) & (there < self.places)

    def start(self, state, maps):
        self.mine[:, :, :DV] = state.astype(BF)
        self.mine[:, :, DV:] = maps.astype(BF)
        for k in range(1, self.places):
            @pl.when(self.inside(self.place + self.ahead * k))
            def _():
                self.copy(k).start()

    def finish(self, out):
        total, turned = self.total, self.turned
        total[...] = jnp.zeros_like(total)
        for k in range(self.places - 1, 0, -1):
            @pl.when(self.inside(self.place - self.ahead * k))
            def _():
                self.copy(k).wait_recv()
                for h in range(total.shape[0]):
                    apply = mm if self.forward else mm_tn
                    total[h] = apply(turned[k, h, :, DV:], total[h]) + turned[k, h, :, :DV].astype(F32)

        out[...] = total[...].astype(out.dtype)
        for k in range(1, self.places):
            @pl.when(self.inside(self.place + self.ahead * k))
            def _():
                self.copy(k).wait_send()

    @staticmethod
    def scratch(places, heads):
        return [pltpu.VMEM((heads, DK, DV + DK), BF), pltpu.VMEM((places, heads, DK, DV + DK), BF),
                pltpu.VMEM((heads, DK, DV), F32), pltpu.SemaphoreType.DMA((places,)), pltpu.SemaphoreType.DMA((places,))]


def forward_gather_kernel(heads, nb, places, cuts, halved, *refs):
    m = len(cuts)
    inputs, sources, refs = refs[:8], refs[8:8 + m], refs[8 + m:]
    others, refs = iter(refs[:sum(halved)]), refs[sum(halved):]
    others = [next(others) if h else None for h in halved]
    outs, entry_ref, targets, refs = refs[:5], refs[5], refs[6:6 + m], refs[6 + m:]
    gather = LineGather(places, cuts, sources, others, targets, *refs[2:5])
    states = PassStates(places, True, *refs[5:])
    step = pl.program_id(0)

    @pl.when(step == 0)
    def _():
        greet(line=places, pair=True, places=places)
        gather.start()

    forward_kernel(heads, *inputs, *outs, *refs[:2])
    events = gather.events()
    early = min(len(events) // 2, nb)
    for i in range(nb):
        @pl.when(step == i)
        def _():
            for event in events[early * i // nb:early * (i + 1) // nb]:
                gather.run(event)

    @pl.when(step == nb - 1)
    def _():
        states.start(outs[4][:, :, :DV], outs[4][:, :, DV:])
        for event in events[early:(early + len(events)) // 2]:
            gather.run(event)
        states.finish(entry_ref)
        for event in events[(early + len(events)) // 2:]:
            gather.run(event)
        gather.finish()


def forward_gather(flags, mixed, taps, small, live, a_log, dt_bias, heads, blocks, call_id, chunks=2):
    rows, width = live.shape[0], mixed.shape[1]
    nb = rows // BLOCK
    count = lax.axis_size("wide")
    halved = [isinstance(block, tuple) for block in blocks]
    others = [b[1] for b, h in zip(blocks, halved) if h]
    blocks = [b[0] if h else b for b, h in zip(blocks, halved)]
    cuts = [row_cuts(block.shape[0], chunks) for block in blocks]
    row = lambda width: pl.BlockSpec((BLOCK, width), lambda i: (i, 0))
    same = lambda *shape: pl.BlockSpec(shape, lambda i: (0,) * len(shape))
    hbm = pl.BlockSpec(memory_space=pl.ANY)
    found = pl.pallas_call(
        functools.partial(forward_gather_kernel, heads, nb, count // 2, cuts, halved),
        grid=(nb,),
        in_specs=[pl.BlockSpec(memory_space=pltpu.SMEM), row(width), pl.BlockSpec((16, width), lambda i: (rows // 16, 0)),
                  same(*taps.shape), row(small.shape[1]), row(1), same(1, heads), same(1, heads)]
                 + [hbm] * (len(blocks) + len(others)),
        out_specs=[row(heads * DV), row(heads * DK),
                   pl.BlockSpec((1, heads, BLOCK, BLOCK), lambda i: (i, 0, 0, 0)),
                   pl.BlockSpec((1, heads, DK, DV + DK), lambda i: (i, 0, 0, 0)),
                   same(heads, DK, DV + DK), same(heads, DK, DV)] + [hbm] * len(blocks),
        out_shape=[jax.ShapeDtypeStruct((rows, heads * DV), F32), jax.ShapeDtypeStruct((rows, heads * DK), BF),
                   jax.ShapeDtypeStruct((nb, heads, BLOCK, BLOCK), BF),
                   jax.ShapeDtypeStruct((nb, heads, DK, DV + DK), BF),
                   jax.ShapeDtypeStruct((heads, DK, DV + DK), F32), jax.ShapeDtypeStruct((heads, DK, DV), BF)]
                  + [jax.ShapeDtypeStruct((count,) + block.shape, block.dtype) for block in blocks],
        scratch_shapes=[pltpu.VMEM((heads, DK, DV + DK), F32), pltpu.VMEM((8, width), F32)]
                       + LineGather.scratch(count, cuts) + PassStates.scratch(count // 2, heads),
        compiler_params=pltpu.CompilerParams(collective_id=call_id, has_side_effects=True, vmem_limit_bytes=48 * 2**20),
    )(flags, mixed, mixed, taps, small, live, a_log, dt_bias, *blocks, *others)
    return found[:6], flat_blocks(found[6:])


def backward_scatter_kernel(heads, nb, places, half_cuts, pair_cuts, shares, *refs):
    hm, pm = len(half_cuts), len(pair_cuts)

    def take(count):
        nonlocal refs
        found, refs = refs[:count], refs[count:]
        return found

    inputs, halves, pairs, share_in = tuple(take(15)), take(hm), take(pm), take(shares)
    outs, half_outs, half_theirs, pair_outs, share_outs = take(4), take(hm), take(hm), take(pm), take(shares)
    scratch = take(2)
    states, exit_ref = PassStates(places, False, *take(5)), take(1)[0]
    direct_ref, end_ref = inputs[-2:]
    inputs = inputs[:-2] + (exit_ref,)
    half, refs = LineScatter.take(places, half_cuts, False, halves, refs)
    groups = [half]
    if pm:
        pair, refs = LineScatter.take(places, pair_cuts, True, pairs, refs)
        groups.append(pair)
    share, refs = NarrowScatter.take(share_in, refs)
    groups.append(share)
    step = pl.program_id(0)

    @pl.when(step == 0)
    def _():
        greet(line=places, pair=True, cube=True, places=places)
        states.start(direct_ref[...], end_ref[:, :, DV:])
        for group in groups:
            group.start()
        states.finish(exit_ref)

    backward_kernel(heads, *inputs, *outs, *scratch)
    events = merged(groups)
    for i in range(nb):
        @pl.when(step == i)
        def _():
            for group, event in events[len(events) * i // nb:len(events) * (i + 1) // nb]:
                group.run(event)

    @pl.when(step == nb - 1)
    def _():
        share.finish(share_outs)
        if pm:
            pair.finish(pair_outs)
        half.finish(half_outs, half_theirs)


def backward_scatter(flags, mixed, taps, small, live, a_log, dt_bias, t, z, go, entry, direct, end, heads, halves, pairs, shares, call_id,
                     chunks=2):
    rows, width = live.shape[0], mixed.shape[1]
    nb = rows // BLOCK
    places = lax.axis_size("wide") // 2
    halves = [place_blocks(term, places) for term in halves]
    half_cuts = [row_cuts(term.shape[2], chunks) for term in halves]
    pair_cuts = [row_cuts(term.shape[1], chunks) for term in pairs]
    h = len(halves)
    narrow = lax.axis_size("narrow")
    sums = [term.shape[2:] for term in halves] * 2 + [term.shape[1:] for term in pairs]
    sums += [(term.shape[0], term.shape[1] // narrow) for term in shares]
    row = lambda width: pl.BlockSpec((BLOCK, width), lambda i: (nb - 1 - i, 0))
    same = lambda *shape: pl.BlockSpec(shape, lambda i: (0,) * len(shape))
    prev = pl.BlockSpec((16, width), lambda i: (jnp.maximum((nb - 1 - i) * (BLOCK // 16) - 1, 0), 0))
    found = pl.pallas_call(
        functools.partial(backward_scatter_kernel, heads, nb, places, half_cuts, pair_cuts, len(shares)),
        grid=(nb,),
        in_specs=[pl.BlockSpec(memory_space=pltpu.SMEM), row(width), prev,
                  pl.BlockSpec((16, width), lambda i: (rows // 16, 0)), same(*taps.shape), row(small.shape[1]), row(1),
                  same(1, heads), same(1, heads),
                  pl.BlockSpec((1, heads, BLOCK, BLOCK), lambda i: (nb - 1 - i, 0, 0, 0)),
                  pl.BlockSpec((1, heads, DK, DV + DK), lambda i: (nb - 1 - i, 0, 0, 0)),
                  row(heads * DV), same(heads, DK, DV), same(heads, DK, DV), same(heads, DK, DV + DK)]
                 + [pl.BlockSpec(memory_space=pl.ANY)] * (len(halves) + len(pairs) + len(shares)),
        out_specs=[same(rows + 16, width), row(2 * heads), same(*taps.shape), same(8, heads)]
                  + [pl.BlockSpec(shape, lambda i: (0, 0), pipeline_mode=pl.Buffered(1)) for shape in sums],
        out_shape=[jax.ShapeDtypeStruct((rows + 16, width), BF), jax.ShapeDtypeStruct((rows, 2 * heads), F32),
                   jax.ShapeDtypeStruct(taps.shape, F32), jax.ShapeDtypeStruct((8, heads), F32)]
                  + [jax.ShapeDtypeStruct(shape, F32) for shape in sums],
        scratch_shapes=[pltpu.VMEM((heads, DK, DV), F32), pltpu.VMEM((8, width), F32)]
                       + PassStates.scratch(places, heads) + [pltpu.VMEM((heads, DK, DV), F32)]
                       + LineScatter.scratch(places, half_cuts, False, halves)
                       + (LineScatter.scratch(places, pair_cuts, True, pairs) if pairs else [])
                       + NarrowScatter.scratch(shares, narrow),
        compiler_params=pltpu.CompilerParams(collective_id=call_id, has_side_effects=True, vmem_limit_bytes=58 * 2**20),
    )(flags, mixed, mixed, mixed, taps, small, live, a_log, dt_bias, t, z, go, entry, direct, end, *halves, *pairs, *shares)
    p = len(pairs)
    return (found[:4], list(zip(found[4:4 + h], found[4 + h:4 + 2 * h])), found[4 + 2 * h:4 + 2 * h + p],
            found[4 + 2 * h + p:])


TILE = 256


def place_rows(side_ref, own_ref, their_ref):
    return jnp.where(pl.program_id(0) // (pl.num_programs(0) // 2) == side_ref[0], own_ref[...], their_ref[...]).astype(F32)


def project_kernel(side_ref, own_ref, their_ref, rim_ref, gain_ref, w_ref, sw_ref, normed_ref, mixed_ref, small_ref):
    step = pl.program_id(0)

    def normal(x):
        return (x * lax.rsqrt(jnp.mean(x * x, axis=1, keepdims=True) + EPS) * gain_ref[...]).astype(BF)

    @pl.when(step < pl.num_programs(0) - 1)
    def _():
        normed = normal(place_rows(side_ref, own_ref, their_ref))
        normed_ref[...] = normed
        mixed_ref[...] = mm(normed, w_ref[...]).astype(BF)
        small_ref[...] = mm_nt(normed, sw_ref[...])

    @pl.when(step == pl.num_programs(0) - 1)
    def _():
        normed = normal(rim_ref[...].astype(F32))
        normed_ref[:16] = normed
        mixed_ref[:16] = mm(normed, w_ref[...]).astype(BF)


def row_specs(rows):
    tiles = 2 * rows // TILE
    held = lambda width: pl.BlockSpec((TILE, width), lambda i: (jnp.minimum(i, tiles - 1) % (tiles // 2), 0))
    tile = lambda width: pl.BlockSpec((TILE, width), lambda i: (jnp.minimum(i, tiles - 1), 0))
    every = lambda width: pl.BlockSpec((TILE, width), lambda i: (i, 0))
    same = lambda *shape: pl.BlockSpec(shape, lambda i: (0,) * len(shape))
    return tiles + 1, held, tile, every, same


def project(side, own, their, rim, gain, weight, small_weight):
    rows, width = own.shape
    steps, held, tile, every, same = row_specs(rows)
    columns = weight.shape[1]
    return pl.pallas_call(
        project_kernel,
        grid=(steps,),
        in_specs=[pl.BlockSpec(memory_space=pltpu.SMEM), held(width), held(width), same(16, width), same(1, width),
                  same(*weight.shape), same(*small_weight.shape)],
        out_specs=[every(width), every(columns), tile(small_weight.shape[0])],
        out_shape=[jax.ShapeDtypeStruct((2 * rows + 16, width), BF), jax.ShapeDtypeStruct((2 * rows + 16, columns), BF),
                   jax.ShapeDtypeStruct((2 * rows, small_weight.shape[0]), F32)],
        compiler_params=pltpu.CompilerParams(vmem_limit_bytes=48 * 2**20),
    )(side, own, their, rim, gain, weight, small_weight)


def unproject_kernel(side_ref, own_ref, their_ref, rim_ref, gain_ref, gm_ref, gg_ref, gs_ref, w_ref, gw_ref, sw_ref, back_ref,
                     rim_back_ref, grad_gain_ref):
    step = pl.program_id(0)

    @pl.when(step == 0)
    def _():
        grad_gain_ref[...] = jnp.zeros_like(grad_gain_ref)

    def norm_back(x, grad):
        factor = lax.rsqrt(jnp.mean(x * x, axis=1, keepdims=True) + EPS)
        unit = x * factor
        grad_gain_ref[...] += jnp.sum(grad * unit, axis=0, keepdims=True)
        scaled = grad * gain_ref[...]
        return (factor * (scaled - unit * jnp.mean(scaled * unit, axis=1, keepdims=True))).astype(BF)

    @pl.when(step < pl.num_programs(0) - 1)
    def _():
        grad = mm_nt(gm_ref[...], w_ref[...]) + mm_nt(gg_ref[...], gw_ref[...])
        for i in range(sw_ref.shape[0]):
            grad = grad + gs_ref[:, i:i + 1] * sw_ref[i:i + 1]
        back_ref[...] = norm_back(place_rows(side_ref, own_ref, their_ref), grad)

    @pl.when(step == pl.num_programs(0) - 1)
    def _():
        rim_back_ref[...] = norm_back(rim_ref[...].astype(F32), mm_nt(gm_ref[:16], w_ref[...]))


def unproject(side, own, their, rim, gain, grad_mixed, grad_gate, grad_small, weight, gate_weight, small_weight):
    rows, width = own.shape
    steps, held, tile, every, same = row_specs(rows)
    return pl.pallas_call(
        unproject_kernel,
        grid=(steps,),
        in_specs=[pl.BlockSpec(memory_space=pltpu.SMEM), held(width), held(width), same(16, width), same(1, width),
                  every(weight.shape[1]), tile(gate_weight.shape[1]), tile(grad_small.shape[1]), same(*weight.shape),
                  same(*gate_weight.shape), same(*small_weight.shape)],
        out_specs=[tile(width), same(16, width), same(1, width)],
        out_shape=[jax.ShapeDtypeStruct((2 * rows, width), BF), jax.ShapeDtypeStruct((16, width), BF),
                   jax.ShapeDtypeStruct((1, width), F32)],
        compiler_params=pltpu.CompilerParams(vmem_limit_bytes=56 * 2**20),
    )(side, own, their, rim, gain, grad_mixed, grad_gate, grad_small, weight, gate_weight, small_weight)


def mix_kernel(heads, x_ref, gw_ref, ow_ref, o_ref, e_ref, s_ref, live_ref, gain_ref, gate_ref, m_ref, out_ref):
    live = live_ref[...]
    gain = gain_ref[...]
    gates = mm(x_ref[...], gw_ref[...])
    gate_ref[...] = gates
    for h in range(heads):
        vs = slice(h * DV, (h + 1) * DV)
        y = (o_ref[:, vs] + mm(e_ref[:, h * DK:(h + 1) * DK], s_ref[h])) * live
        r = lax.rsqrt(jnp.mean(y * y, axis=1, keepdims=True) + EPS)
        gate = gates[:, vs]
        m_ref[:, vs] = (y * r * gain * (gate * jax.nn.sigmoid(gate))).astype(BF)
    out_ref[...] = mm_nt(m_ref[...], ow_ref[...]).astype(BF)


def mix(normed, gate_weight, out_weight, o, e, entry, live, gain, heads):
    rows, width = o.shape[0], normed.shape[1]
    row = lambda width: pl.BlockSpec((TILE, width), lambda i: (i, 0))
    same = lambda *shape: pl.BlockSpec(shape, lambda i: (0,) * len(shape))
    return pl.pallas_call(
        functools.partial(mix_kernel, heads),
        grid=(rows // TILE,),
        in_specs=[row(width), same(*gate_weight.shape), same(*out_weight.shape), row(heads * DV), row(heads * DK),
                  same(heads, DK, DV), row(1), same(1, DV)],
        out_specs=[row(heads * DV), row(heads * DV), row(width)],
        out_shape=[jax.ShapeDtypeStruct((rows, heads * DV), F32), jax.ShapeDtypeStruct((rows, heads * DV), BF),
                   jax.ShapeDtypeStruct((rows, width), BF)],
        compiler_params=pltpu.CompilerParams(vmem_limit_bytes=48 * 2**20),
    )(normed, gate_weight, out_weight, o, e, entry, live, gain)


def feed_kernel(places, chunks, own_ref, cot_hbm, wg_hbm, wu_hbm, wd_hbm, sum_ref, down_hbm, dwd_hbm, dwg_hbm, dwu_hbm,
                rows, cot, wg, wu, wd, hid, gg, gu, gr, pair, line, dn, dwd, dwg, dwu, load_sems, out_sems, own_sem,
                ag_send, ag_recv, pair_send, pair_recv, right_send, right_recv, left_send, left_recv):
    w, place, side, n = position()
    partner = w + 1 - 2 * side
    quarter, width = own_ref.shape
    size = quarter // chunks
    part = lambda c: pl.ds(c * size, size)
    devices = [(partner, n), (w + 2, n), (w - 2, n)]
    loads = [pltpu.make_async_copy(source, target, load_sems.at[i]) for i, (source, target) in enumerate(
        ((wg_hbm, wg), (wu_hbm, wu), (cot_hbm, cot), (wd_hbm, wd)))]

    def remote(source, target, send, recv, device):
        return pltpu.make_async_remote_copy(src_ref=source, dst_ref=target, send_sem=send, recv_sem=recv, device_id=device,
                                            device_id_type=MESH)

    def move(slot, way, c, own=False):
        source = own_ref.at[part(c)] if own else rows.at[slot, part(c)]
        return remote(source, rows.at[slot, part(c)], ag_send.at[way, slot, c], ag_recv.at[slot, c], devices[way])

    def along(slot, way, c, own=False):
        @pl.when(place < places - 1 if way == 1 else place > 0)
        def _():
            move(slot, way, c, own).start()

    def across(t, c):
        return remote(gr.at[2 * t + 1 - side, part(c)], pair.at[t, part(c)], pair_send.at[t, c], pair_recv.at[t, c], devices[0])

    def right(t, c):
        return remote(gr.at[2 * t + side, part(c)], line.at[t, part(c)], right_send.at[t, c], right_recv.at[t, c], devices[1])

    def left(t, c, arriving=False):
        slot = jnp.where(t == place - (0 if arriving else 1), places, t)
        return remote(gr.at[2 * t + side, part(c)], line.at[slot, part(c)], left_send.at[t, c], left_recv.at[t, c], devices[2])

    def inside(there):
        return (there >= 0) & (there < places)

    def arrive(s):
        for way, there in ((1, place - s), (2, place + s)):
            @pl.when(inside(there))
            def _():
                for c in range(chunks):
                    move(2 * there + side, way, c).wait_recv()
                    along(2 * there + side, way, c)
                    move(2 * there + side, 0, c).start()

    def work(there):
        for c in range(chunks):
            move(2 * there + 1 - side, 0, c).wait_recv()
        both = pl.ds(2 * there, 2)
        flat = lambda ref: ref[both].reshape(2 * quarter, ref.shape[2])
        x = flat(rows)
        gate = mm_nt(x, wg[...])
        up = mm_nt(x, wu[...])
        grad = mm_nt(flat(cot), wd[...])
        sig = jax.nn.sigmoid(gate)
        act = gate * sig
        hid[both] = (act * up).astype(BF).reshape(2, quarter, -1)
        low_gate = (grad * up * (sig + act * (1.0 - sig))).astype(BF)
        low_up = (grad * act).astype(BF)
        gg[both] = low_gate.reshape(2, quarter, -1)
        gu[both] = low_up.reshape(2, quarter, -1)
        gr[both] = (mm(low_gate, wg[...]) + mm(low_up, wu[...])).astype(BF).reshape(2, quarter, width)
        for c in range(chunks):
            across(there, c).start()

    def add(t, c, other, slot):
        at = (2 * t + side, part(c))
        gr[at] = (gr[at].astype(F32) + other[slot, part(c)].astype(F32)).astype(BF)

    def pass_on(s):
        t = s

        @pl.when(place < t)
        def _():
            for c in range(chunks):
                across(t, c).wait_recv()
                add(t, c, pair, t)

                @pl.when(place > 0)
                def _():
                    right(t, c).wait_recv()
                    add(t, c, line, t)

                right(t, c).start()

        t_left = places - 1 - s

        @pl.when(place > t_left)
        def _():
            for c in range(chunks):
                across(t_left, c).wait_recv()
                add(t_left, c, pair, t_left)

                @pl.when(place < places - 1)
                def _():
                    left(t_left, c, True).wait_recv()
                    add(t_left, c, line, t_left)

                left(t_left, c).start()

    greet(line=places, pair=True)
    for load in loads:
        load.start()
    for c in range(chunks):
        move(w, 0, c, True).start()
        along(w, 1, c, True)
        along(w, 2, c, True)
    own = pltpu.make_async_copy(own_ref, rows.at[w], own_sem)
    own.start()
    own.wait()
    for load in loads:
        load.wait()

    def rows_work(s, _):
        @pl.when(inside(place - s))
        def _():
            work(place - s)

        @pl.when(inside(place + s) & (s > 0))
        def _():
            work(place + s)
        return 0

    def advance(s, _):
        arrive(s)
        rows_work(s - 1, 0)

        @pl.when(s > 1)
        def _():
            pass_on(s - 1)
        return 0

    lax.fori_loop(1, places, advance, 0)
    rows_work(places - 1, 0)

    columns = width // 4

    def weights(i, _):
        cut = pl.ds(pl.multiple_of(i * columns, columns), columns)
        everything = lambda ref: ref[...].reshape(2 * places * quarter, ref.shape[2])
        slot = lax.rem(i, 2)

        @pl.when(i >= 2)
        def _():
            pltpu.make_async_copy(dn.at[slot], down_hbm.at[pl.ds(0, 2)], out_sems.at[3 + slot]).wait()

        dwd[:, cut] = mm_tn(everything(hid), cot[:, :, cut].reshape(2 * places * quarter, columns)).astype(BF)
        x = rows[:, :, cut].reshape(2 * places * quarter, columns)
        dwg[:, cut] = mm_tn(everything(gg), x).astype(BF)
        dwu[:, cut] = mm_tn(everything(gu), x).astype(BF)
        both = pl.ds(2 * i, 2)
        dn[slot] = jnp.dot(hid[both].reshape(2 * quarter, hid.shape[2]), wd[...],
                           preferred_element_type=F32).astype(BF).reshape(2, quarter, width)
        pltpu.make_async_copy(dn.at[slot], down_hbm.at[both], out_sems.at[3 + slot]).start()
        return 0

    before = jnp.where((place > 0) & (place < places - 1), 2, 0)
    lax.fori_loop(0, before, weights, 0)
    pass_on(places - 1)
    lax.fori_loop(before, 4, weights, 0)
    outs = [pltpu.make_async_copy(source, target, out_sems.at[i]) for i, (source, target) in enumerate(
        ((dwd, dwd_hbm), (dwg, dwg_hbm), (dwu, dwu_hbm)))]
    for out in outs:
        out.start()
    for c in range(chunks):
        across(place, c).wait_recv()
        add(place, c, pair, place)

        @pl.when(place > 0)
        def _():
            right(place, c).wait_recv()
            add(place, c, line, place)

        @pl.when(place < places - 1)
        def _():
            left(place, c, True).wait_recv()
            add(place, c, line, places)

        sum_ref[part(c)] = gr[2 * place + side, part(c)].astype(F32)
    for out in outs:
        out.wait()
    for slot in range(2):
        pltpu.make_async_copy(dn.at[slot], down_hbm.at[pl.ds(0, 2)], out_sems.at[3 + slot]).wait()

    def settle(t, _):
        for c in range(chunks):
            across(t, c).wait_send()
            move(2 * t + side, 0, c).wait_send()

            @pl.when((place < places - 1) & (t <= place))
            def _():
                move(2 * t + side, 1, c).wait_send()

            @pl.when((place > 0) & (t >= place))
            def _():
                move(2 * t + side, 2, c).wait_send()

            @pl.when(t > place)
            def _():
                right(t, c).wait_send()

            @pl.when(t < place)
            def _():
                left(t, c).wait_send()
        return 0

    lax.fori_loop(0, places, settle, 0)


def feed(own, cot, w_gate, w_up, w_down, call_id, chunks=2):
    count = lax.axis_size("wide")
    places = count // 2
    quarter, width = own.shape
    units = w_down.shape[0]
    hbm, vmem = pl.BlockSpec(memory_space=pl.ANY), pl.BlockSpec(memory_space=pltpu.VMEM)
    blocks = lambda columns: pltpu.VMEM((count, quarter, columns), BF)
    line = lambda amount: pltpu.VMEM((amount, quarter, width), BF)
    sems = pltpu.SemaphoreType.DMA((places, chunks))
    return pl.pallas_call(
        functools.partial(feed_kernel, places, chunks),
        in_specs=[vmem, hbm, hbm, hbm, hbm],
        out_specs=[vmem, hbm, hbm, hbm, hbm],
        out_shape=[jax.ShapeDtypeStruct((quarter, width), F32), jax.ShapeDtypeStruct((count, quarter, width), BF),
                   jax.ShapeDtypeStruct((units, width), BF), jax.ShapeDtypeStruct((units, width), BF),
                   jax.ShapeDtypeStruct((units, width), BF)],
        scratch_shapes=[blocks(width), blocks(width), pltpu.VMEM((units, width), BF), pltpu.VMEM((units, width), BF),
                        pltpu.VMEM((units, width), BF), blocks(units), blocks(units), blocks(units), blocks(width),
                        line(places), line(places + 1), pltpu.VMEM((2, 2, quarter, width), BF), pltpu.VMEM((units, width), BF),
                        pltpu.VMEM((units, width), BF), pltpu.VMEM((units, width), BF), pltpu.SemaphoreType.DMA((4,)),
                        pltpu.SemaphoreType.DMA((5,)), pltpu.SemaphoreType.DMA, pltpu.SemaphoreType.DMA((3, count, chunks)),
                        pltpu.SemaphoreType.DMA((count, chunks))] + [sems] * 6,
        compiler_params=pltpu.CompilerParams(collective_id=call_id, has_side_effects=True, vmem_limit_bytes=60 * 2**20),
    )(own, cot.reshape(count, quarter, width), w_gate, w_up, w_down)


CONV = 4


def rms_norm(value, gain):
    return value * lax.rsqrt(jnp.mean(value * value, axis=-1, keepdims=True) + EPS) * gain


def after(value, *others):
    return lax.optimization_barrier((value,) + others)[0]


def part(value, axis, index, count=2):
    size = value.shape[axis] // count
    return lax.dynamic_slice_in_dim(value, index * size, size, axis)


def ordered(mine, theirs, side, axis):
    return jnp.concatenate([jnp.where(side == 0, mine, theirs), jnp.where(side == 0, theirs, mine)], axis=axis)


def sequence_tables(doc_lengths, first_row, row_count, block_size):
    padded = (doc_lengths + block_size - 1) // block_size * block_size
    seq_ends = jnp.cumsum(padded)
    seq_starts = seq_ends - padded
    row_places = first_row + jnp.arange(row_count, dtype=jnp.int32)
    inside_mask = (row_places[:, None] >= seq_starts[None, :]) & (row_places[:, None] < seq_ends[None, :])
    live_mask = jnp.any(inside_mask & (row_places[:, None] < (seq_starts + doc_lengths)[None, :]), axis=1, keepdims=True)
    fresh_block = jnp.any(row_places[::block_size][:, None] == seq_starts[None, :], axis=1)
    return live_mask.astype(F32), jnp.where(fresh_block, 0.0, 1.0).astype(F32)


def contract_rows(left, right):
    return lax.dot_general(left, right, (((0,), (0,)), ((), ())), preferred_element_type=F32)


def contract_cols(left, right):
    return lax.dot_general(left, right, (((1,), (1,)), ((), ())), preferred_element_type=F32)


def feed_apart(own, cot, w_gate, w_up, w_down):
    quarter = own.shape[0]
    blocks = lambda a: a.astype(BF).reshape(-1, quarter, a.shape[1])
    gathered_rows = line_gather([own], 3)[0]
    gate_pre = contract_cols(gathered_rows, w_gate)
    up_pre = contract_cols(gathered_rows, w_up)
    gate_sig = jax.nn.sigmoid(gate_pre)
    gate_act = gate_pre * gate_sig
    hidden_low = (gate_act * up_pre).astype(BF)
    grad_hidden = contract_cols(cot, w_down)
    grad_gate_low = (grad_hidden * up_pre * gate_sig * (1.0 + gate_pre * (1.0 - gate_sig))).astype(BF)
    grad_up_low = (grad_hidden * gate_act).astype(BF)
    grad_rows = (jnp.dot(grad_gate_low, w_gate, preferred_element_type=F32)
                 + jnp.dot(grad_up_low, w_up, preferred_element_type=F32))
    grad_sum = line_scatter([], [blocks(grad_rows)], [], [], 4)[1][0]
    down_rows = blocks(jnp.dot(hidden_low, w_down, preferred_element_type=F32))
    grad_w_down = contract_rows(hidden_low, cot).astype(BF)
    grad_w_gate = contract_rows(grad_gate_low, gathered_rows).astype(BF)
    grad_w_up = contract_rows(grad_up_low, gathered_rows).astype(BF)
    return grad_sum, down_rows, grad_w_down, grad_w_gate, grad_w_up


def shards(block_input, gain_attn, w_query, w_key, w_value, w_gate_out, w_decay, w_beta, conv_query, conv_key,
           conv_value, a_log, dt_bias, out_gain, w_out, gain_mlp, w_gate, w_up, w_down, doc_lengths, cotangent):
    d_model = block_input.shape[1]
    row_count = 2 * block_input.shape[0]
    quarter = cotangent.shape[0]
    depth = w_query.shape[0]
    heads = a_log.shape[0] // 2
    narrow = lax.axis_size("narrow")
    wide = lax.axis_size("wide")
    wide_index = lax.axis_index("wide")
    place, side = wide_index // 2, wide_index % 2
    live, flags = sequence_tables(doc_lengths, place * row_count, row_count, BLOCK)
    gain_row, a_row, dt_row = out_gain[None, :], part(a_log, 0, side)[None, :], part(dt_bias, 0, side)[None, :]
    key_width, value_width = heads * DK, heads * DV
    columns = 2 * key_width + value_width
    row_blocks = lambda a: a.astype(BF).reshape(-1, quarter, a.shape[1])
    halves = lambda *arrays: tuple(
        jnp.concatenate([part(a, 1, s) for a in arrays], axis=1) for s in (side, 1 - side))
    padded = lambda a: jnp.pad(a, ((0, 16 - 4 * heads), (0, 0)))

    first, small_weight, their_input, rim_input = line_gather(
        [halves(w_query, w_key, w_value), padded(jnp.concatenate([w_decay.T, w_beta.T], axis=0))], 1, rows=block_input)
    rim_input = jnp.where(place > 0, rim_input, jnp.zeros_like(rim_input))
    small_weight = small_weight.reshape(wide, 16, depth).transpose(1, 0, 2).reshape(16, d_model)
    small_weight = jnp.concatenate([part(small_weight[:2 * heads], 0, side), part(small_weight[2 * heads:4 * heads], 0, side)],
                                   axis=0)
    taps = jnp.concatenate([part(conv_query, 1, side), part(conv_key, 1, side), part(conv_value, 1, side)], axis=1)
    side_word = side.astype(jnp.int32)[None]
    padded_small = jnp.pad(small_weight, ((0, 16 - 2 * heads), (0, 0)))
    normed_low, mixed, small = project(side_word, block_input, their_input, rim_input, gain_attn[None, :], first, padded_small)
    small = small[:, :2 * heads]

    (local_out, reach, inverses, states, end, entry), (gate_weight, gathered_cot, out_weight) = forward_gather(
        flags, mixed, taps, small, live, a_row, dt_row, heads, [halves(w_gate_out), cotangent, halves(w_out)], 7)
    gate_rows, mixer_low, head_part = mix(normed_low, gate_weight, out_weight, local_out, reach, entry, live,
                                          gain_row, heads)
    own_rows = cube_scatter(row_blocks(head_part), 9) + part(
        block_input, 0, lax.axis_index("narrow"), narrow).astype(F32)
    mlp_normed, mlp_norm_back = jax.vjp(rms_norm, own_rows, gain_mlp)
    feed_forward = feed_apart if wide > 8 else functools.partial(feed, call_id=3)
    grad_mlp_normed, down_rows, grad_w_down, grad_w_gate, grad_w_up = feed_forward(
        mlp_normed.astype(BF), gathered_cot, w_gate.T, w_up.T, w_down)
    grad_own_norm, grad_gain_mlp = mlp_norm_back(grad_mlp_normed)
    grad_own = cotangent.astype(F32) + grad_own_norm
    grad_attn = cube_gather(grad_own.astype(BF), 10)

    grad_mixer = jnp.dot(grad_attn, out_weight, preferred_element_type=F32)
    grad_outputs, grad_gate_rows, grad_out_gain, direct = unfinish(local_out, reach, entry, gate_rows, live, gain_row,
                                                                   grad_mixer, heads)
    grad_w_out = contract_rows(grad_attn, mixer_low).astype(BF)
    grad_w_gate_out = contract_rows(normed_low[:row_count], grad_gate_rows).astype(BF)
    (grad_mixed, grad_small, grad_taps, grad_scalars), (sum_w_out, sum_w_gate_out), (sum_down,), shares = backward_scatter(
        flags, mixed, taps, small, live, a_row, dt_row, inverses, states, grad_outputs, entry, direct, end, heads,
        [grad_w_out, grad_w_gate_out], [down_rows], [grad_w_gate, grad_w_up, grad_w_down], 8)
    output = (own_rows + sum_down).astype(BF)
    grad_small = grad_small.astype(BF)
    grad_first = contract_rows(normed_low, grad_mixed).astype(BF)
    grad_small_weight = contract_rows(grad_small, normed_low[:row_count]).astype(BF)
    both_sides = lambda a: ordered(a, jnp.zeros_like(a), side, 0)
    grad_small_weight = padded(jnp.concatenate([both_sides(grad_small_weight[:heads]), both_sides(grad_small_weight[heads:])],
                                               axis=0))
    small_blocks = grad_small_weight.reshape(16, wide, depth).transpose(1, 0, 2)
    grad_input_part, grad_rim, grad_gain_attn = unproject(
        side_word, block_input, their_input, rim_input, gain_attn[None, :], grad_mixed, grad_gate_rows, grad_small.astype(F32),
        first, gate_weight, small_weight.astype(F32))
    grad_rim = jnp.pad(grad_rim[None], ((7, 0), (0, 0), (0, 0)))

    lanes = lambda a: jnp.pad(a, (0, -a.shape[0] % 1024)).reshape(-1, 128)
    head_sums = lanes(jnp.concatenate([grad_taps.reshape(-1), grad_scalars[0], grad_scalars[1]]))
    whole_sums = lanes(jnp.concatenate([grad_gain_attn[0], grad_gain_mlp, grad_out_gain[0]]))
    (sum_first,), (sum_small,), (input_sum, _), (every,) = line_scatter(
        [grad_first], [small_blocks], [row_blocks(grad_input_part), grad_rim],
        [jnp.concatenate([head_sums, whole_sums], axis=0)], 6)
    grad_input = input_sum + grad_own
    whole_sums = jnp.sum(every[:, head_sums.shape[0]:], axis=0).reshape(-1)
    every = every[:, :head_sums.shape[0]].reshape(2, narrow, -1)
    conv_all = every[:, :, :4 * columns].reshape(2, narrow, 4, columns)
    conv_parts = [conv_all[:, :, :, lo:hi].transpose(2, 1, 0, 3).reshape(4, -1) for lo, hi in
                  ((0, key_width), (key_width, 2 * key_width), (2 * key_width, columns))]
    scalars = [every[:, :, lo:lo + heads].transpose(1, 0, 2).reshape(-1) for lo in (4 * columns, 4 * columns + heads)]
    joined = lambda found, lo, hi: ordered(found[0][:, lo:hi], found[1][:, lo:hi], side, 1)
    return (
        output, grad_input, whole_sums[:d_model],
        joined(sum_first, 0, key_width), joined(sum_first, key_width, 2 * key_width), joined(sum_first, 2 * key_width, columns),
        joined(sum_w_gate_out, 0, value_width),
        sum_small[:2 * heads].T, sum_small[2 * heads:4 * heads].T, conv_parts[0], conv_parts[1], conv_parts[2],
        scalars[0], scalars[1], whole_sums[2 * d_model:2 * d_model + DV], joined(sum_w_out, 0, value_width),
        whole_sums[d_model:2 * d_model], shares[0].T, shares[1].T, shares[2],
    )


def solution(mesh):
    both = P("wide", "narrow")
    rows = P(("wide", "narrow"), None)
    return jax.shard_map(
        shards,
        mesh=mesh,
        in_specs=(P("wide", None), P(), both, both, both, both, both, both, P(None, "narrow"), P(None, "narrow"),
                  P(None, "narrow"), P("narrow"), P("narrow"), P(), both, P(), P(None, "wide"), P(None, "wide"),
                  P("wide", None), P(), rows),
        out_specs=(rows, rows, P(), both, both, both, both, both, both, P(), P(), P(), P(), P(), P(), both, P(),
                   P("narrow", "wide"), P("narrow", "wide"), both),
        check_vma=False,
    )
```

```python
import functools
import jax
import jax.numpy as jnp
from jax import lax
from jax.experimental import pallas as pl
from jax.experimental.pallas import tpu as pltpu
from jax.sharding import PartitionSpec as P

DK, DV, BLOCK, EPS = 128, 256, 64, 1e-6
BF = jnp.bfloat16
F32 = jnp.float32


def mm(a, b):
    return jnp.dot(a.astype(BF), b.astype(BF), preferred_element_type=F32)


def mm_nt(a, b):
    return lax.dot_general(a.astype(BF), b.astype(BF), (((1,), (1,)), ((), ())), preferred_element_type=F32)


def mm_tn(a, b):
    return lax.dot_general(a.astype(BF), b.astype(BF), (((0,), (0,)), ((), ())), preferred_element_type=F32)


def split(a):
    high = a.astype(BF)
    return high, (a - high.astype(F32)).astype(BF)


def mm_fine(a, b):
    ah, al = split(a)
    bh, bl = split(b)
    return mm(ah, bh) + (mm(ah, bl) + mm(al, bh))


def unit_lower_inverses(systems, rows, cols):
    gap = rows ^ cols
    below = rows > cols
    unit = jnp.where(rows == cols, 1.0, 0.0)
    found = [unit - jnp.where(below & (gap < 2), a, 0.0) for a in systems]
    size = 2
    while size < systems[0].shape[0]:
        mask = below & (gap >= size) & (gap < 2 * size)
        inner = [mm_fine(jnp.where(mask, a, 0.0), t) for a, t in zip(systems, found)]
        found = [t - mm_fine(t, m) for t, m in zip(found, inner)]
        size *= 2
    return found


def block_tables(g_col, g_row, rows, cols):
    lower = rows >= cols
    return jnp.where(lower, jnp.exp(jnp.where(lower, g_col - g_row, 0.0)), 0.0)


def shifted(rows, before, back):
    if back == 0:
        return rows
    return jnp.concatenate([before[8 - back:], rows[:rows.shape[0] - back]], axis=0)


def conv_rows(rows, before, taps):
    count = taps.shape[0]
    total = taps[count - 1:count] * rows
    for back in range(1, count):
        total = total + taps[count - 1 - back:count - back] * shifted(rows, before, back)
    return total


def head_slices(heads, h):
    key = heads * DK
    return slice(h * DK, (h + 1) * DK), slice(key + h * DK, key + (h + 1) * DK), slice(2 * key + h * DV, 2 * key + (h + 1) * DV)


def unit_factor(rows):
    return lax.rsqrt(jnp.sum(rows * rows, axis=1, keepdims=True) + EPS)


def exact_tn(a, b):
    return lax.dot_general(a, b, (((0,), (0,)), ((), ())), precision=lax.Precision.HIGHEST, preferred_element_type=F32)


def softplus(x):
    return jnp.maximum(x, 0.0) + jnp.log(1.0 + jnp.exp(-jnp.abs(x)))


def decay_tables(heads, small, a_log, dt_bias, live, rows, cols):
    speed = -jnp.exp(a_log)
    biased = small[:, :heads] + dt_bias
    log_decay = speed * softplus(biased)
    sig = jax.nn.sigmoid(small[:, heads:2 * heads])
    upto = jnp.where(rows <= cols, 1.0, 0.0)
    run = exact_tn(upto, log_decay)
    run_row = exact_tn(log_decay, upto)
    return speed, biased, log_decay, sig, sig * live, run, run_row


def forward_kernel(heads, flag_ref, x_ref, rim_ref, taps_ref, small_ref, live_ref, alog_ref, dt_ref,
                   o_ref, e_ref, t_ref, z_ref, end_ref, carry, before_ref):
    step = pl.program_id(0)
    rows = lax.broadcasted_iota(jnp.int32, (BLOCK, BLOCK), 0)
    cols = lax.broadcasted_iota(jnp.int32, (BLOCK, BLOCK), 1)
    flag = flag_ref[step]

    @pl.when(step == 0)
    def _():
        before_ref[...] = rim_ref[8:16, :].astype(F32)
        unit = jnp.where(lax.broadcasted_iota(jnp.int32, (DK, DK), 0) == lax.broadcasted_iota(jnp.int32, (DK, DK), 1), 1.0, 0.0)
        for h in range(heads):
            carry[h, :, :DV] = jnp.zeros((DK, DV), F32)
            carry[h, :, DV:] = unit

    _, _, _, _, betas, run, run_row = decay_tables(heads, small_ref[...], alog_ref[...], dt_ref[...], live_ref[...], rows, cols)
    openings = flag * jnp.exp(run)
    closings = jnp.exp(run[BLOCK - 1:BLOCK] - run)

    def active(columns):
        c = conv_rows(x_ref[:, columns].astype(F32), before_ref[:, columns] * flag, taps_ref[:, columns])
        return c * jax.nn.sigmoid(c)

    tables, systems, parts = [], [], []
    for h in range(heads):
        qs, ks, vs = head_slices(heads, h)
        q, k, v = active(qs), active(ks), active(vs).astype(BF)
        q = (q * unit_factor(q) * DK ** (-0.5)).astype(BF)
        k = (k * unit_factor(k)).astype(BF)
        parts.append((q, k, v))
        table = block_tables(run[:, h:h + 1], run_row[h:h + 1, :], rows, cols)
        tables.append(table)
        systems.append(jnp.where(rows > cols, betas[:, h:h + 1] * table * mm_nt(k, k), 0.0))
    before_ref[...] = x_ref[BLOCK - 8:, :].astype(F32)
    inverses = unit_lower_inverses(systems, rows, cols)
    for h in range(heads):
        q, k, v = parts[h]
        beta, opening, closing = betas[:, h:h + 1], openings[:, h:h + 1], closings[:, h:h + 1]
        low_t = inverses[h].astype(BF)
        t_ref[0, h] = low_t
        u = mm(low_t, beta * v.astype(F32))
        w = mm(low_t, (beta * opening) * k.astype(F32))
        scores = mm_nt(q, k) * tables[h]
        state = carry[h]
        low_state = state.astype(BF)
        z_ref[0, h] = low_state
        reach = mm(jnp.concatenate([w.astype(BF), (opening * q.astype(F32)).astype(BF)], axis=0), low_state)
        c = jnp.concatenate([u, jnp.zeros((BLOCK, DK), F32)], axis=1) - reach[:BLOCK]
        low_c = c.astype(BF)
        out = reach[BLOCK:] + mm(scores, low_c)
        o_ref[:, h * DV:(h + 1) * DV] = out[:, :DV]
        e_ref[:, h * DK:(h + 1) * DK] = out[:, DV:].astype(BF)
        new = opening[BLOCK - 1:BLOCK] * state + mm_tn(closing * k.astype(F32), low_c)
        carry[h] = new
        end_ref[h] = new


def unfinish_kernel(heads, o_ref, e_ref, s_ref, gate_ref, live_ref, gain_ref, gm_ref, go_ref, gg_ref, ggain_ref, direct_ref):
    @pl.when(pl.program_id(0) == 0)
    def _():
        ggain_ref[...] = jnp.zeros_like(ggain_ref)
        direct_ref[...] = jnp.zeros_like(direct_ref)

    live = live_ref[...]
    gain = gain_ref[...]
    total = jnp.zeros((1, DV), F32)
    for h in range(heads):
        vs = slice(h * DV, (h + 1) * DV)
        e = e_ref[:, h * DK:(h + 1) * DK]
        y = (o_ref[:, vs] + mm(e, s_ref[h])) * live
        r = lax.rsqrt(jnp.mean(y * y, axis=1, keepdims=True) + EPS)
        gate = gate_ref[:, vs]
        sig = jax.nn.sigmoid(gate)
        act = gate * sig
        gm = gm_ref[:, vs]
        unit = y * r
        gn = gm * act
        total = total + jnp.sum(gn * unit, axis=0, keepdims=True)
        gn = gn * gain
        gg_ref[:, vs] = (gm * unit * gain * (sig * (1.0 + gate * (1.0 - sig)))).astype(BF)
        go = (r * (gn - unit * jnp.mean(gn * unit, axis=1, keepdims=True)) * live).astype(BF)
        go_ref[:, vs] = go
        direct_ref[h] += mm_tn(e, go)
    ggain_ref[...] += total


def unfinish(o, e, entry, gate, live, gain, gm, heads, tile=256):
    rows = o.shape[0]
    row = lambda width: pl.BlockSpec((tile, width), lambda i: (i, 0))
    return pl.pallas_call(
        functools.partial(unfinish_kernel, heads),
        grid=(rows // tile,),
        in_specs=[row(heads * DV), row(heads * DK), pl.BlockSpec((heads, DK, DV), lambda i: (0, 0, 0)), row(heads * DV),
                  row(1), pl.BlockSpec((1, DV), lambda i: (0, 0)), row(heads * DV)],
        out_specs=[row(heads * DV), row(heads * DV), pl.BlockSpec((1, DV), lambda i: (0, 0)),
                   pl.BlockSpec((heads, DK, DV), lambda i: (0, 0, 0))],
        out_shape=[jax.ShapeDtypeStruct((rows, heads * DV), BF), jax.ShapeDtypeStruct((rows, heads * DV), BF),
                   jax.ShapeDtypeStruct((1, DV), F32), jax.ShapeDtypeStruct((heads, DK, DV), F32)],
        compiler_params=pltpu.CompilerParams(vmem_limit_bytes=48 * 2**20),
    )(o, e, entry, gate, live, gain, gm)


def silu_back(c, grad):
    sig = jax.nn.sigmoid(c)
    return grad * (sig * (1.0 + c * (1.0 - sig)))


def backward_kernel(heads, flag_ref, x_ref, prev_ref, rim_ref, taps_ref, small_ref, live_ref, alog_ref, dt_ref, t_ref, z_ref,
                    go_ref, s_ref, exit_ref, gx_ref, gsmall_ref, gtaps_ref, gscalar_ref, carry, after_ref):
    step = pl.program_id(0)
    nb = pl.num_programs(0)
    at = nb - 1 - step
    rows = lax.broadcasted_iota(jnp.int32, (BLOCK, BLOCK), 0)
    cols = lax.broadcasted_iota(jnp.int32, (BLOCK, BLOCK), 1)
    last = lax.broadcasted_iota(jnp.int32, (BLOCK, 1), 0) == BLOCK - 1
    flag = flag_ref[at]
    taps_count = taps_ref.shape[0]

    @pl.when(step == 0)
    def _():
        carry[...] = exit_ref[...].astype(F32)
        after_ref[...] = jnp.zeros_like(after_ref)
        gtaps_ref[...] = jnp.zeros_like(gtaps_ref)
        gscalar_ref[...] = jnp.zeros_like(gscalar_ref)

    live = live_ref[...]
    speed, biased, log_decay, sig, betas, run, run_row = decay_tables(
        heads, small_ref[...], alog_ref[...], dt_ref[...], live, rows, cols)
    openings = flag * jnp.exp(run)
    closings = jnp.exp(run[BLOCK - 1:BLOCK] - run)
    row_block = pl.ds(pl.multiple_of(at * BLOCK, BLOCK), BLOCK)

    def inputs(columns):
        x = x_ref[:, columns].astype(F32)
        before = jnp.where(at == 0, rim_ref[8:16, columns].astype(F32), prev_ref[8:16, columns].astype(F32)) * flag
        return x, before, conv_rows(x, before, taps_ref[:, columns])

    def conv_back(columns, x, before, grad):
        taps = taps_ref[:, columns]
        later = after_ref[:, columns]
        longer = jnp.concatenate([grad, later], axis=0)
        gx = taps[taps_count - 1:taps_count] * grad
        sums = [jnp.sum(grad * x, axis=0, keepdims=True)]
        for back in range(1, taps_count):
            gx = gx + taps[taps_count - 1 - back:taps_count - back] * longer[back:back + BLOCK]
            sums.append(jnp.sum(grad * shifted(x, before, back), axis=0, keepdims=True))
        gx_ref[row_block, columns] = gx.astype(BF)
        gtaps_ref[:, columns] += jnp.concatenate(sums[::-1], axis=0)
        after_ref[:, columns] = grad[:8] * flag

    grad_runs, grad_betas = [], []
    for h in range(heads):
        qs, ks, vs = head_slices(heads, h)
        xq, bq, cq = inputs(qs)
        xk, bk, ck = inputs(ks)
        xv, bv, cv = inputs(vs)
        aq, ak = cq * jax.nn.sigmoid(cq), ck * jax.nn.sigmoid(ck)
        rq, rk_unit = unit_factor(aq), unit_factor(ak)
        uq, uk = aq * rq, ak * rk_unit
        q, k = (uq * DK ** (-0.5)).astype(BF), uk.astype(BF)
        v = (cv * jax.nn.sigmoid(cv)).astype(BF)
        qf, kf, vf = q.astype(F32), k.astype(F32), v.astype(F32)
        beta, opening, closing = betas[:, h:h + 1], openings[:, h:h + 1], closings[:, h:h + 1]
        gamma = opening[BLOCK - 1:BLOCK]
        table = block_tables(run[:, h:h + 1], run_row[h:h + 1, :], rows, cols)
        kk = mm_nt(k, k)
        scores = mm_nt(q, k) * table
        low_t = t_ref[0, h]
        u = mm(low_t, beta * vf)
        w = mm(low_t, (beta * opening) * kf)
        low_w = w.astype(BF)
        state = z_ref[0, h, :, :DV].astype(F32) + mm(z_ref[0, h, :, DV:], s_ref[h])
        low_s = state.astype(BF)
        c = u - mm(low_w, low_s)
        low_c = c.astype(BF)
        go = go_ref[:, h * DV:(h + 1) * DV]
        g = carry[h]
        low_g = g.astype(BF)
        low_ck = (closing * kf).astype(BF)
        low_oq = (opening * qf).astype(BF)
        dc = mm_tn(scores, go) + mm(low_ck, low_g)
        low_dc = dc.astype(BF)
        both = jnp.concatenate([go, low_dc], axis=0)
        carry[h] = gamma * g + mm_tn(jnp.concatenate([low_oq, -low_w], axis=0), both)
        dkeyed = mm_nt(low_c, low_g)
        dgamma = jnp.sum(jnp.sum(state * g, axis=1, keepdims=True), axis=0, keepdims=True)
        dscore = jnp.where(rows >= cols, mm_nt(go, low_c), 0.0)
        back = mm_nt(both, low_s)
        doq, dw = back[:BLOCK], -back[BLOCK:]
        drv = mm_tn(low_t, low_dc)
        drw = mm_tn(low_t, dw)
        low_drv, low_drw = drv.astype(BF), drw.astype(BF)
        da = jnp.where(rows > cols, -(mm_nt(low_drv, u) + mm_nt(low_drw, low_w)), 0.0)
        dat = da * table
        dkk = (beta * dat).astype(BF)
        dqk = (dscore * table).astype(BF)
        gq = (opening * doq + mm(dqk, k)) * DK ** (-0.5)
        gk = mm_tn(dqk, q) + mm(dkk, k) + mm_tn(dkk, k) + closing * dkeyed + (beta * opening) * drw
        gq = rq * (gq - uq * jnp.sum(gq * uq, axis=1, keepdims=True))
        gk = rk_unit * (gk - uk * jnp.sum(gk * uk, axis=1, keepdims=True))
        conv_back(qs, xq, bq, silu_back(cq, gq))
        conv_back(ks, xk, bk, silu_back(ck, gk))
        conv_back(vs, xv, bv, silu_back(cv, beta * drv))
        rk = jnp.sum(drw * kf, axis=1, keepdims=True)
        atk = dat * kk
        grad_betas.append(jnp.sum(drv * vf, axis=1, keepdims=True) + opening * rk + jnp.sum(atk, axis=1, keepdims=True))
        dopen = opening * (jnp.sum(doq * qf, axis=1, keepdims=True) + beta * rk)
        dclose = closing * jnp.sum(dkeyed * kf, axis=1, keepdims=True)
        e = dscore * scores + beta * atk
        by_col = exact_tn(e, jnp.ones((BLOCK, 8), F32))[:, :1]
        dg = jnp.sum(e, axis=1, keepdims=True) - by_col + dopen - dclose
        grad_runs.append(dg + jnp.where(last, jnp.sum(dclose, axis=0, keepdims=True) + dgamma * gamma, 0.0))

    lane = lax.broadcasted_iota(jnp.int32, (BLOCK, heads), 1)
    grad_run = sum(jnp.where(lane == h, grad_runs[h], 0.0) for h in range(heads))
    grad_beta = sum(jnp.where(lane == h, grad_betas[h], 0.0) for h in range(heads))
    grad_log = exact_tn(jnp.where(cols <= rows, 1.0, 0.0), grad_run)
    grad_biased = grad_log * speed * jax.nn.sigmoid(biased)
    gsmall_ref[:, :heads] = grad_biased
    gsmall_ref[:, heads:] = grad_beta * live * sig * (1.0 - sig)
    gscalar_ref[0:1, :] += jnp.sum(grad_log * log_decay, axis=0, keepdims=True)
    gscalar_ref[1:2, :] += jnp.sum(grad_biased, axis=0, keepdims=True)

    @pl.when(step == nb - 1)
    def _():
        longer = jnp.concatenate([jnp.zeros((16, taps_ref.shape[1]), F32), after_ref[...]], axis=0)
        gx = jnp.zeros((16, taps_ref.shape[1]), F32)
        for back in range(1, taps_count):
            gx = gx + taps_ref[taps_count - 1 - back:taps_count - back, :] * longer[back:back + 16]
        gx_ref[pl.ds(nb * BLOCK, 16), :] = gx.astype(BF)


MESH = pl.DeviceIdType.MESH


def position():
    w = lax.axis_index("wide")
    return w, w // 2, w % 2, lax.axis_index("narrow")


def greet(line=0, pair=False, cube=False, bits=(), places=0, rim=False):
    w, place, side, n = position()
    barrier = pltpu.get_barrier_semaphore()

    def signal(*device):
        pl.semaphore_signal(barrier, inc=1, device_id=device, device_id_type=MESH)

    count = 0
    if pair:
        signal(w + 1 - 2 * side, n)
        count += 1
    if cube:
        signal(w, n ^ 1)
        signal(w, n ^ 2)
        count += 2
    for bit in bits:
        signal(w ^ bit, n)
        count += 1
    if line:
        @pl.when(place > 0)
        def _():
            signal(w - 2, n)

        @pl.when(place < line - 1)
        def _():
            signal(w + 2, n)

        count = count + jnp.where(place > 0, 1, 0) + jnp.where(place < line - 1, 1, 0)
    if rim:
        @pl.when((side == 0) & (place > 0))
        def _():
            signal(w - 1, n)

        @pl.when((side == 1) & (place < line - 1))
        def _():
            signal(w + 1, n)

        count = count + jnp.where(side == 0, jnp.where(place > 0, 1, 0), jnp.where(place < line - 1, 1, 0))
    for k in range(1, places):
        for there in (place + k, place - k):
            @pl.when((there >= 0) & (there < places))
            def _():
                signal(2 * there + side, n)

    pl.semaphore_wait(barrier, count + max(places - 1, 0))


def row_cuts(rows, chunks):
    units = rows // 16
    chunks = min(chunks, units)
    edges = [16 * (units * c // chunks) for c in range(chunks + 1)]
    return [(edges[c], edges[c + 1] - edges[c]) for c in range(chunks)]


class LineGather:
    def __init__(self, places, cuts, sources, others, targets, local_sems, send_sems, recv_sems):
        self.places, self.sources, self.others, self.targets = places, sources, others, targets
        self.local_sems, self.send_sems, self.recv_sems = local_sems, send_sems, recv_sems
        self.w, self.place, self.side, self.n = position()
        self.items = [(i,) + cut for i, found in enumerate(cuts) for cut in found]

    def both(self, item):
        return self.others[self.items[item][0]] is not None

    def copy(self, item, slot, way, own=False):
        i, start, size = self.items[item]
        rows = pl.ds(start, size)
        source = self.targets[i].at[slot, rows]
        if own:
            source = (self.others if way == 0 and self.both(item) else self.sources)[i].at[rows]
        device = [self.w + 1 - 2 * self.side, self.w + 2, self.w - 2][way]
        return pltpu.make_async_remote_copy(
            src_ref=source, dst_ref=self.targets[i].at[slot, rows], send_sem=self.send_sems.at[way, slot, item],
            recv_sem=self.recv_sems.at[slot, item], device_id=(device, self.n), device_id_type=MESH)

    def start(self):
        for i, source in enumerate(self.sources):
            pltpu.make_async_copy(source, self.targets[i].at[self.w], self.local_sems.at[i]).start()
        for item in range(len(self.items)):
            self.copy(item, self.w, 0, True).start()
            self.along(item, self.w, 1, True)
            self.along(item, self.w, 2, True)

    def along(self, item, slot, way, own=False):
        @pl.when(self.place < self.places - 1 if way == 1 else self.place > 0)
        def _():
            self.copy(item, slot, way, own).start()

    def events(self):
        items = range(len(self.items))
        found = [(item, 0, 1) for item in items if self.both(item)]
        return found + [(item, t, s) for t in range(1, self.places) for item in items
                        for s in ((0, 1) if self.both(item) else (0,))]

    def run(self, event):
        item, t, s = event
        if t == 0:
            slot = self.w + 1 - 2 * self.side
            self.copy(item, slot, 0).wait_recv()
            self.along(item, slot, 1)
            self.along(item, slot, 2)
            return

        for way, there in ((1, self.place - t), (2, self.place + t)):
            slot = 2 * there + (self.side if s == 0 else 1 - self.side)

            @pl.when((there >= 0) & (there < self.places))
            def _():
                self.copy(item, slot, way).wait_recv()
                self.along(item, slot, way)
                if not self.both(item):
                    self.copy(item, slot, 0).start()

    def finish(self):
        for item in range(len(self.items)):
            if not self.both(item):
                for t in range(self.places):
                    self.copy(item, 2 * t + 1 - self.side, 0).wait_recv()
        for i, source in enumerate(self.sources):
            pltpu.make_async_copy(source, self.targets[i].at[self.w], self.local_sems.at[i]).wait()
        for item in range(len(self.items)):
            both = self.both(item)
            if both:
                self.copy(item, self.w, 0, True).wait_send()
            for t in range(self.places):
                if not both:
                    self.copy(item, 2 * t + self.side, 0).wait_send()
                for s in ((0, 1) if both else (0,)):
                    slot = 2 * t + (self.side if s == 0 else 1 - self.side)

                    @pl.when((self.place < self.places - 1) & (t <= self.place))
                    def _():
                        self.copy(item, slot, 1).wait_send()

                    @pl.when((self.place > 0) & (t >= self.place))
                    def _():
                        self.copy(item, slot, 2).wait_send()

    @staticmethod
    def scratch(count, cuts):
        items = sum(len(found) for found in cuts)
        return [pltpu.SemaphoreType.DMA((len(cuts),)), pltpu.SemaphoreType.DMA((3, count, items)),
                pltpu.SemaphoreType.DMA((count, items))]


class PairRows:
    def __init__(self, places, source, target, rim, send_sems, recv_sems, rim_send, rim_recv):
        self.places, self.source, self.target, self.rim = places, source, target, rim
        self.send_sems, self.recv_sems, self.rim_sems = send_sems, recv_sems, (rim_send, rim_recv)
        self.w, self.place, self.side, self.n = position()

    def copy(self, number, part):
        size = self.target.shape[1]
        device = [(self.w + 1 - 2 * self.side, self.n), (self.w, self.n ^ 2), (self.w, self.n ^ 1), (self.w, self.n ^ 1)][number]
        source = self.source.at[pl.ds(part * size, size)] if number == 0 else self.target.at[part]
        return pltpu.make_async_remote_copy(
            src_ref=source, dst_ref=self.target.at[part], send_sem=self.send_sems.at[number],
            recv_sem=self.recv_sems.at[part], device_id=device, device_id_type=MESH)

    def rim_copy(self, side):
        size = self.rim.shape[0]
        return pltpu.make_async_remote_copy(
            src_ref=self.source.at[pl.ds(self.source.shape[0] - size, size)], dst_ref=self.rim,
            send_sem=self.rim_sems[0].at[side], recv_sem=self.rim_sems[1],
            device_id=(2 * self.place + 2 + side, self.n), device_id_type=MESH)

    def sends_rim(self):
        return (self.side == 1) & (self.place < self.places - 1)

    def start(self):
        self.copy(0, self.n).start()

        @pl.when(self.sends_rim())
        def _():
            self.rim_copy(0).start()
            self.rim_copy(1).start()

    def events(self):
        return [0, 1]

    def run(self, event):
        if event == 0:
            self.copy(0, self.n).wait_recv()
            self.copy(1, self.n).start()
            self.copy(2, self.n).start()
        else:
            self.copy(1, self.n ^ 2).wait_recv()
            self.copy(3, self.n ^ 2).start()

    def finish(self):
        self.copy(2, self.n ^ 1).wait_recv()
        self.copy(3, self.n ^ 3).wait_recv()
        for number in range(4):
            self.copy(number, self.n ^ 2 if number == 3 else self.n).wait_send()

        @pl.when(self.place > 0)
        def _():
            self.rim_copy(0).wait_recv()

        @pl.when(self.sends_rim())
        def _():
            self.rim_copy(0).wait_send()
            self.rim_copy(1).wait_send()


def gather_kernel(places, cuts, halved, rows, *refs):
    m = len(cuts)
    sources, refs = refs[:m], refs[m:]
    others, refs = iter(refs[:sum(halved)]), refs[sum(halved):]
    others = [next(others) if h else None for h in halved]
    rows_in, refs = refs[:rows], refs[rows:]
    targets, rows_out, refs = refs[:m], refs[m:m + 2 * rows], refs[m + 2 * rows:]
    groups = [LineGather(places, cuts, sources, others, targets, *refs[:3])]
    if rows:
        groups.append(PairRows(places, rows_in[0], *rows_out, *refs[3:]))
    greet(line=places, pair=True, cube=bool(rows), rim=bool(rows))
    for group in groups[::-1]:
        group.start()
    for group, event in merged(groups):
        group.run(event)
    for group in groups[::-1]:
        group.finish()


def flat_blocks(gathered):
    return [g.reshape((g.shape[0] * g.shape[1],) + g.shape[2:]) for g in gathered]


def line_gather(values, call_id, chunks=4, rows=None):
    count = lax.axis_size("wide")
    halved = [isinstance(value, tuple) for value in values]
    sources = [value[0] if h else value for value, h in zip(values, halved)]
    others = [value[1] for value, h in zip(values, halved) if h]
    cuts = [row_cuts(value.shape[0], chunks if value.shape[0] > 64 else 1) for value in sources]
    hbm = pl.BlockSpec(memory_space=pl.ANY)
    shapes = [jax.ShapeDtypeStruct((count,) + value.shape, value.dtype) for value in sources]
    scratch = LineGather.scratch(count, cuts)
    if rows is not None:
        narrow = lax.axis_size("narrow")
        others.append(rows)
        shapes.append(jax.ShapeDtypeStruct((narrow, rows.shape[0] // narrow, rows.shape[1]), rows.dtype))
        shapes.append(jax.ShapeDtypeStruct((16, rows.shape[1]), rows.dtype))
        scratch += [pltpu.SemaphoreType.DMA((4,)), pltpu.SemaphoreType.DMA((narrow,)), pltpu.SemaphoreType.DMA((2,)),
                    pltpu.SemaphoreType.DMA]
    found = pl.pallas_call(
        functools.partial(gather_kernel, count // 2, cuts, halved, 0 if rows is None else 1),
        out_shape=shapes,
        in_specs=[hbm] * (len(sources) + len(others)),
        out_specs=[hbm] * len(shapes),
        scratch_shapes=scratch,
        compiler_params=pltpu.CompilerParams(collective_id=call_id, has_side_effects=True),
    )(*sources, *others)
    return flat_blocks(found[:-1]) + [found[-1]] if rows is not None else flat_blocks(found)


class LineScatter:
    def __init__(self, places, cuts, paired, sources, owns, pairs, lines, load_sems, pair_send, pair_recv, right_send,
                 right_recv, left_send, left_recv):
        self.places, self.paired = places, paired
        self.sources, self.owns, self.pairs, self.lines = sources, owns, pairs, lines
        self.load_sems, self.pair_sems = load_sems, (pair_send, pair_recv)
        self.right_sems, self.left_sems = (right_send, right_recv), (left_send, left_recv)
        self.w, self.place, self.side, self.n = position()
        self.items = [(i,) + cut for i, found in enumerate(cuts) for cut in found]
        self.fill = None
        self.order = [(t, item) for j in range(places // 2) for item in range(len(self.items)) for t in (places - 1 - j, j)]

    def remote(self, source, target, sems, t, item, device):
        return pltpu.make_async_remote_copy(src_ref=source, dst_ref=target, send_sem=sems[0].at[t, item],
                                            recv_sem=sems[1].at[t, item], device_id=(device, self.n), device_id_type=MESH)

    def at(self, t, item):
        i, start, size = self.items[item]
        return (t, pl.ds(start, size)) if self.paired else (t, slice(None), pl.ds(start, size))

    def across(self, t, item):
        i = self.items[item][0]
        source = self.sources[i].at[2 * t + 1 - self.side, self.at(t, item)[1]]
        return self.remote(source, self.pairs[i].at[self.at(t, item)], self.pair_sems, t, item, self.w + 1 - 2 * self.side)

    def load(self, t, item):
        i = self.items[item][0]
        slot = 2 * t + self.side if self.paired else t
        return pltpu.make_async_copy(self.sources[i].at[self.at(slot, item)], self.owns[i].at[self.at(t, item)],
                                     self.load_sems.at[t, item])

    def right(self, t, item):
        i, at = self.items[item][0], self.at(t, item)
        return self.remote(self.owns[i].at[at], self.lines[i].at[at], self.right_sems, t, item, self.w + 2)

    def left(self, t, item, arriving=False):
        i, at = self.items[item][0], self.at(t, item)
        slot = jnp.where(t == self.place - (0 if arriving else 1), self.places, t)
        return self.remote(self.owns[i].at[at], self.lines[i].at[(slot,) + at[1:]], self.left_sems, t, item, self.w - 2)

    ahead = 4

    def start(self):
        if self.sources is not None:
            for t, item in self.order:
                self.load(t, item).start()
        if self.paired:
            for t, item in self.order[:self.ahead]:
                self.across(t, item).start()

    def events(self):
        return self.order

    def run(self, event):
        t, item = event
        i, at = self.items[item][0], self.at(t, item)
        own, place, places = self.owns[i], self.place, self.places

        def add(other):
            own[at] = (own[at].astype(F32) + other[at].astype(F32)).astype(own.dtype)

        if self.fill is not None and item == 0:
            self.fill(t)
        if self.sources is not None:
            self.load(t, item).wait()
        if self.paired:
            following = self.order.index(event) + self.ahead
            if following < len(self.order):
                self.across(*self.order[following]).start()
            self.across(t, item).wait_recv()
            add(self.pairs[i])

        @pl.when(t > place)
        def _():
            @pl.when(place > 0)
            def _():
                self.right(t, item).wait_recv()
                add(self.lines[i])

            self.right(t, item).start()

        @pl.when(t < place)
        def _():
            @pl.when(place < places - 1)
            def _():
                self.left(t, item, True).wait_recv()
                add(self.lines[i])

            self.left(t, item).start()

    def finish(self, outs, theirs=None):
        place, copies = self.place, []
        for item in range(len(self.items)):
            i, start, size = self.items[item]
            own, line, at, rows = self.owns[i], self.lines[i], self.at(place, item), pl.ds(start, size)

            @pl.when(place > 0)
            def _():
                self.right(place, item).wait_recv()
                own[at] = (own[at].astype(F32) + line[at].astype(F32)).astype(own.dtype)

            @pl.when(place < self.places - 1)
            def _():
                self.left(place, item, True).wait_recv()
                own[at] = (own[at].astype(F32) + line[(self.places,) + at[1:]].astype(F32)).astype(own.dtype)

            if self.paired:
                outs[i][rows] = own[at].astype(F32)
            else:
                copy = self.remote(own.at[place, 1 - self.side, rows], self.pairs[i].at[rows], self.pair_sems, 0, item,
                                   self.w + 1 - 2 * self.side)
                copy.start()
                copies.append((i, rows, copy))
                outs[i][rows] = own[place, self.side, rows].astype(F32)
        for i, rows, copy in copies:
            copy.wait()
            theirs[i][rows] = self.pairs[i][rows].astype(F32)
        for t in range(self.places):
            for item in range(len(self.items)):
                if self.paired:
                    self.across(t, item).wait_send()

                @pl.when(t > place)
                def _():
                    self.right(t, item).wait_send()

                @pl.when(t < place)
                def _():
                    self.left(t, item).wait_send()

    @staticmethod
    def scratch(places, cuts, paired, values):
        owns = [pltpu.VMEM((places,) + value.shape[1:], value.dtype) for value in values]
        pairs = owns if paired else [pltpu.VMEM(value.shape[2:], value.dtype) for value in values]
        lines = [pltpu.VMEM((places + 1,) + value.shape[1:], value.dtype) for value in values]
        items = sum(len(found) for found in cuts)
        return owns + pairs + lines + [pltpu.SemaphoreType.DMA((places, items))] * 7

    @staticmethod
    def take(places, cuts, paired, sources, refs):
        m = len(cuts)
        amount = 3 * m + 7
        groups = [refs[m * g:m * (g + 1)] for g in range(3)]
        return LineScatter(places, cuts, paired, sources, *groups, *refs[3 * m:amount]), refs[amount:]


class CubeScatter:
    def __init__(self, source, own, near, second, third, load_sems, send_sems, recv_sems):
        self.source, self.own, self.near, self.second, self.third = source, own, near, second, third
        self.load_sems, self.send_sems, self.recv_sems = load_sems, send_sems, recv_sems
        self.w, self.place, self.side, self.n = position()
        self.half = own.shape[2] // 2
        self.order = (3, 1, 2, 0)

    def block(self, s, m):
        return (self.side ^ s) * 4 + (self.n ^ m)

    def remote(self, number, source, target, device):
        return pltpu.make_async_remote_copy(src_ref=source, dst_ref=target, send_sem=self.send_sems.at[number],
                                            recv_sem=self.recv_sems.at[number], device_id=device, device_id_type=MESH)

    def cut(self, part):
        return pl.ds(part * self.half, self.half)

    def first(self, j):
        return self.remote(j, self.source.at[self.block(j // 2, 1 + 2 * (j % 2))], self.near.at[j], (self.w, self.n ^ 1))

    def load(self, j):
        return pltpu.make_async_copy(self.source.at[self.block(j // 2, 2 * (j % 2))], self.own.at[j], self.load_sems.at[j])

    def device(self, part, stage):
        return (self.w, self.n ^ 2) if part == stage else (self.w + 1 - 2 * self.side, self.n)

    def middle(self, part, k):
        j = 2 * k + 1 if part == 0 else 2 + k
        return self.remote(4 + 2 * part + k, self.own.at[j, :, self.cut(part)], self.second.at[part, k], self.device(part, 0))

    def end(self, part):
        j = 2 if part == 0 else 1
        return self.remote(8 + part, self.own.at[j, :, self.cut(part)], self.third.at[part], self.device(part, 1))

    def start(self):
        for j in self.order:
            self.load(j).start()
        for j in self.order:
            self.first(j).start()

    def events(self):
        return [("near", j) for j in self.order] + [("middle", k) for k in (1, 0)]

    def run(self, event):
        kind, j = event
        if kind == "near":
            self.load(j).wait()
            self.first(j).wait_recv()
            self.own[j] = (self.own[j].astype(F32) + self.near[j].astype(F32)).astype(self.own.dtype)
            if j % 2 == 1:
                self.middle(0, j // 2).start()
            if j // 2 == 1:
                self.middle(1, j % 2).start()
            return
        for part in (0, 1):
            self.middle(part, j).wait_recv()
            target = (2 * j if part == 0 else j, slice(None), self.cut(part))
            self.own[target] = (self.own[target].astype(F32) + self.second[part, j].astype(F32)).astype(self.own.dtype)
            if j == 1:
                self.end(part).start()

    def finish(self, out):
        for part in (0, 1):
            self.end(part).wait_recv()
            out[:, self.cut(part)] = self.own[0, :, self.cut(part)].astype(F32) + self.third[part].astype(F32)
        for j in range(4):
            self.first(j).wait_send()
        for part in (0, 1):
            for k in (0, 1):
                self.middle(part, k).wait_send()
            self.end(part).wait_send()

    @staticmethod
    def scratch(value):
        rows, columns = value.shape[1:]
        block = pltpu.VMEM((4, rows, columns), value.dtype)
        return [block, block, pltpu.VMEM((2, 2, rows, columns // 2), value.dtype),
                pltpu.VMEM((2, rows, columns // 2), value.dtype), pltpu.SemaphoreType.DMA((4,)),
                pltpu.SemaphoreType.DMA((10,)), pltpu.SemaphoreType.DMA((10,))]


class NarrowScatter:
    def __init__(self, sources, owns, nears, fars, load_sems, send_sems, recv_sems):
        self.sources, self.owns, self.nears, self.fars = sources, owns, nears, fars
        self.load_sems, self.send_sems, self.recv_sems = load_sems, send_sems, recv_sems
        self.w, self.place, self.side, self.n = position()

    def cut(self, i, m):
        size = self.owns[i].shape[2]
        return self.sources[i].at[:, pl.ds(pl.multiple_of((self.n ^ m) * size, size), size)]

    def remote(self, i, number, source, target, bit):
        return pltpu.make_async_remote_copy(
            src_ref=source, dst_ref=target, send_sem=self.send_sems.at[i, number], recv_sem=self.recv_sems.at[i, number],
            device_id=(self.w, self.n ^ bit), device_id_type=MESH)

    def near(self, i, m):
        return self.remote(i, m, self.cut(i, 1 + 2 * m), self.nears[i].at[m], 1)

    def far(self, i):
        return self.remote(i, 2, self.owns[i].at[1], self.fars[i], 2)

    def load(self, i, m):
        return pltpu.make_async_copy(self.cut(i, 2 * m), self.owns[i].at[m], self.load_sems.at[i, m])

    def start(self):
        for i in range(len(self.owns)):
            for m in (1, 0):
                self.load(i, m).start()
        for i in range(len(self.owns)):
            for m in (1, 0):
                self.near(i, m).start()

    def events(self):
        return [(kind, i) for i in range(len(self.owns)) for kind in ("high", "low")]

    def run(self, event):
        kind, i = event
        m = 1 if kind == "high" else 0
        self.load(i, m).wait()
        self.near(i, m).wait_recv()
        self.owns[i][m] = (self.owns[i][m].astype(F32) + self.nears[i][m].astype(F32)).astype(self.owns[i].dtype)
        if m == 1:
            self.far(i).start()

    def finish(self, outs):
        for i, out in enumerate(outs):
            self.far(i).wait_recv()
            out[...] = self.owns[i][0].astype(F32) + self.fars[i][...].astype(F32)
            for m in (0, 1):
                self.near(i, m).wait_send()
            self.far(i).wait_send()

    @staticmethod
    def scratch(values, narrow):
        shapes = [(value.shape[0], value.shape[1] // narrow) for value in values]
        pairs = [pltpu.VMEM((2,) + shape, value.dtype) for shape, value in zip(shapes, values)]
        m = len(values)
        return (pairs * 2 + [pltpu.VMEM(shape, value.dtype) for shape, value in zip(shapes, values)]
                + [pltpu.SemaphoreType.DMA((m, 2)), pltpu.SemaphoreType.DMA((m, 3)), pltpu.SemaphoreType.DMA((m, 3))])

    @staticmethod
    def take(sources, refs):
        m = len(sources)
        amount = 3 * m + 3
        return NarrowScatter(sources, refs[:m], refs[m:2 * m], refs[2 * m:3 * m], *refs[3 * m:amount]), refs[amount:]


def cube_scatter_kernel(x_ref, o_ref, *refs):
    cube = CubeScatter(x_ref, *refs)
    greet(pair=True, cube=True)
    cube.start()
    for event in cube.events():
        cube.run(event)
    cube.finish(o_ref)


def cube_scatter(value, call_id):
    return pl.pallas_call(
        cube_scatter_kernel,
        out_shape=jax.ShapeDtypeStruct(value.shape[1:], F32),
        in_specs=[pl.BlockSpec(memory_space=pl.ANY)],
        out_specs=pl.BlockSpec(memory_space=pltpu.VMEM),
        scratch_shapes=CubeScatter.scratch(value),
        compiler_params=pltpu.CompilerParams(collective_id=call_id, has_side_effects=True, vmem_limit_bytes=32 * 2**20),
    )(value)


def cube_gather_kernel(x_ref, o_ref, local_sem, send_sems, recv_sems):
    w, place, side, n = position()
    half = x_ref.shape[1] // 2
    devices = [(w + 1 - 2 * side, n), (w, n ^ 2), (w, n ^ 1)]

    def copy(s, m, part, way, own=False):
        slot = (side ^ s) * 4 + (n ^ m)
        columns = pl.ds(part * half, half)
        source = x_ref.at[:, columns] if own else o_ref.at[slot, :, columns]
        return pltpu.make_async_remote_copy(
            src_ref=source, dst_ref=o_ref.at[slot, :, columns], send_sem=send_sems.at[way, slot, part],
            recv_sem=recv_sems.at[slot, part], device_id=devices[way], device_id_type=MESH)

    greet(pair=True, cube=True)
    local = pltpu.make_async_copy(x_ref, o_ref.at[side * 4 + n], local_sem)
    local.start()
    sent = []

    def send(s, m, part, way, own=False):
        found = copy(s, m, part, way, own)
        found.start()
        sent.append(found)

    for way in (0, 1, 2):
        for part in (0, 1):
            send(0, 0, part, way, True)
    copy(1, 0, 0, 0).wait_recv()
    send(1, 0, 0, 1)
    copy(0, 2, 1, 1).wait_recv()
    send(0, 2, 1, 0)
    send(1, 0, 0, 2)
    send(0, 2, 1, 2)
    copy(0, 2, 0, 1).wait_recv()
    send(0, 2, 0, 2)
    copy(1, 0, 1, 0).wait_recv()
    send(1, 0, 1, 2)
    copy(1, 2, 0, 1).wait_recv()
    send(1, 2, 0, 2)
    copy(1, 2, 1, 0).wait_recv()
    send(1, 2, 1, 2)
    for s in (0, 1):
        for m in (1, 3):
            for part in (0, 1):
                copy(s, m, part, 2).wait_recv()
    local.wait()
    for found in sent:
        found.wait_send()


def cube_gather(value, call_id):
    return pl.pallas_call(
        cube_gather_kernel,
        out_shape=jax.ShapeDtypeStruct((8,) + value.shape, value.dtype),
        in_specs=[pl.BlockSpec(memory_space=pltpu.VMEM)],
        out_specs=pl.BlockSpec(memory_space=pl.ANY),
        scratch_shapes=[pltpu.SemaphoreType.DMA, pltpu.SemaphoreType.DMA((3, 8, 2)), pltpu.SemaphoreType.DMA((8, 2))],
        compiler_params=pltpu.CompilerParams(collective_id=call_id, has_side_effects=True, vmem_limit_bytes=16 * 2**20),
    )(value).reshape(8 * value.shape[0], value.shape[1])


class SmallSums:
    def __init__(self, steps, value, stages, inbox, cube, place_send, place_recv, cube_send, cube_recv):
        self.steps, self.value, self.stages, self.inbox, self.cube = steps, value, stages, inbox, cube
        self.place_sems, self.cube_sems = (place_send, place_recv), (cube_send, cube_recv)
        self.w, self.place, self.side, self.n = position()

    def step(self, i):
        return pltpu.make_async_remote_copy(
            src_ref=self.stages.at[i], dst_ref=self.inbox.at[i], send_sem=self.place_sems[0].at[i],
            recv_sem=self.place_sems[1].at[i], device_id=(self.w ^ (2 << i), self.n), device_id_type=MESH)

    def spread(self, way, s, m):
        slot = (self.side ^ s) * 4 + (self.n ^ m)
        device = [(self.w + 1 - 2 * self.side, self.n), (self.w, self.n ^ 2), (self.w, self.n ^ 1)][way]
        return pltpu.make_async_remote_copy(
            src_ref=self.cube.at[slot], dst_ref=self.cube.at[slot], send_sem=self.cube_sems[0].at[way, slot],
            recv_sem=self.cube_sems[1].at[slot], device_id=device, device_id_type=MESH)

    sent = {0: [(0, 0)], 1: [(0, 0), (1, 0)], 2: [(0, 0), (1, 0), (0, 2), (1, 2)]}
    arriving = {0: [(1, 0)], 1: [(0, 2), (1, 2)], 2: [(0, 1), (1, 1), (0, 3), (1, 3)]}

    def send(self, way):
        for s, m in self.sent[way]:
            self.spread(way, s, m).start()

    def start(self):
        self.stages[0] = self.value[...]
        self.step(0).start()

    def events(self):
        return [("place", i) for i in range(self.steps)] + [("cube", way) for way in range(3)]

    def run(self, event):
        kind, i = event
        if kind == "place":
            self.step(i).wait_recv()
            self.stages[i + 1] = self.stages[i] + self.inbox[i]
            if i + 1 < self.steps:
                self.step(i + 1).start()
            else:
                self.cube[self.side * 4 + self.n] = self.stages[i + 1]
                self.send(0)
            return
        for s, m in self.arriving[i]:
            self.spread(i, s, m).wait_recv()
        if i < 2:
            self.send(i + 1)

    def finish(self, out):
        out[...] = self.cube[...]
        for i in range(self.steps):
            self.step(i).wait_send()
        for way in range(3):
            for s, m in self.sent[way]:
                self.spread(way, s, m).wait_send()

    @staticmethod
    def scratch(steps, value):
        rows = pltpu.VMEM((steps + 1,) + value.shape, value.dtype)
        return [rows, rows, pltpu.VMEM((8,) + value.shape, value.dtype), pltpu.SemaphoreType.DMA((steps,)),
                pltpu.SemaphoreType.DMA((steps,)), pltpu.SemaphoreType.DMA((3, 8)), pltpu.SemaphoreType.DMA((8,))]


class Products:
    def __init__(self, scatter, operands, buffers, sems):
        self.scatter, self.buffers = scatter, buffers
        self.loads = [pltpu.make_async_copy(source, target, sems.at[i])
                      for i, (source, target) in enumerate(zip(operands, buffers))]
        scatter.fill = self.fill

    def start(self):
        for load in self.loads:
            load.start()

    def wait(self):
        for load in self.loads:
            load.wait()

    def fill(self, t):
        for i, own in enumerate(self.scatter.owns):
            left, right = self.buffers[2 * i], self.buffers[2 * i + 1]
            depth = 2 * own.shape[2]
            term = mm_tn(left[:right.shape[0], t * depth:(t + 1) * depth], right[...]).astype(own.dtype)
            own[t] = term.reshape(own.shape[1:])

    @staticmethod
    def scratch(operands):
        return [pltpu.VMEM(a.shape, a.dtype) for a in operands] + [pltpu.SemaphoreType.DMA((len(operands),))]


def product_terms(products, places):
    terms = [jax.ShapeDtypeStruct((places, 2, left.shape[1] // (2 * places), right.shape[1]), BF) for left, right in products]
    return terms, [a for product in products for a in product]


def place_bits(places):
    return [2 << i for i in range(places.bit_length() - 1)]


def scatter_kernel(places, half_cuts, pair_cuts, cubes, small, narrow, *refs):
    hm, pm = len(half_cuts), len(pair_cuts)

    def take(count):
        nonlocal refs
        found, refs = refs[:count], refs[count:]
        return found

    operands, pairs, cube_in, small_in = take(2 * hm), take(pm), take(cubes), take(small)
    half_outs, half_theirs, pair_outs, cube_outs, small_outs = take(hm), take(hm), take(pm), take(cubes), take(small)
    groups, ends = [], []
    if hm:
        buffers, product_sems = take(2 * hm), take(1)[0]
        half, refs = LineScatter.take(places, half_cuts, False, None, refs)
        products = Products(half, operands, buffers, product_sems)
        products.start()
        groups.append(half)
        ends.append(lambda: half.finish(half_outs, half_theirs))
    if pm:
        pair, refs = LineScatter.take(places, pair_cuts, True, pairs, refs)
        groups.append(pair)
        ends.append(lambda: pair.finish(pair_outs))
    for source, out in zip(cube_in, cube_outs):
        cube = CubeScatter(source, *take(7))
        groups.append(cube)
        ends.append(lambda cube=cube, out=out: cube.finish(out))
    if small:
        sums = SmallSums(len(place_bits(places)), small_in[0], *take(7))
        groups.append(sums)
        ends.append(lambda: sums.finish(small_outs[0]))
    greet(line=places, pair=True, cube=bool(cubes), bits=place_bits(places) if small else ())
    for group in groups[::-1]:
        group.start()
    if hm:
        products.wait()
    for group, event in merged(groups):
        group.run(event)
    for end in ends[:0:-1]:
        end()
    if cubes == 2:
        w, place, side, n = position()
        rim_in, rim_send, rim_recv = take(3)
        rim = pltpu.make_async_remote_copy(src_ref=cube_outs[1], dst_ref=rim_in, send_sem=rim_send, recv_sem=rim_recv,
                                           device_id=(w - 2, n), device_id_type=MESH)
        last = (side == 1) & (n == narrow - 1)

        @pl.when(last & (place > 0))
        def _():
            rim.start()

        @pl.when(last & (place < places - 1))
        def _():
            rim.wait_recv()
            rows = pl.ds(cube_outs[0].shape[0] - rim_in.shape[0], rim_in.shape[0])
            cube_outs[0][rows] = cube_outs[0][rows] + rim_in[...]

        @pl.when(last & (place > 0))
        def _():
            rim.wait_send()
    ends[0]()


def merged(groups):
    found = []
    for order, group in enumerate(groups):
        events = group.events()
        found += [((i + 0.5) / len(events), order, i, group, event) for i, event in enumerate(events)]
    return [(group, event) for _, _, _, group, event in sorted(found, key=lambda e: e[:3])]


def line_scatter(halves, pairs, cubes, small, call_id, chunks=4):
    places = lax.axis_size("wide") // 2
    halves, operands = product_terms(halves, places)
    half_cuts = [row_cuts(term.shape[2], chunks) for term in halves]
    pair_cuts = [row_cuts(term.shape[1], chunks if term.shape[1] > 64 else 1) for term in pairs]
    shapes = [term.shape[2:] for term in halves] * 2 + [term.shape[1:] for term in list(pairs) + list(cubes)]
    shapes += [(8,) + term.shape for term in small]
    scratch = []
    if halves:
        scratch += Products.scratch(operands) + LineScatter.scratch(places, half_cuts, False, halves)
    if pairs:
        scratch += LineScatter.scratch(places, pair_cuts, True, pairs)
    for term in cubes:
        scratch += CubeScatter.scratch(term)
    for term in small:
        scratch += SmallSums.scratch(len(place_bits(places)), term)
    if cubes:
        scratch += [pltpu.VMEM(cubes[1].shape[1:], F32), pltpu.SemaphoreType.DMA, pltpu.SemaphoreType.DMA]
    vmem = pl.BlockSpec(memory_space=pltpu.VMEM)
    found = pl.pallas_call(
        functools.partial(scatter_kernel, places, half_cuts, pair_cuts, len(cubes), len(small), lax.axis_size("narrow")),
        out_shape=[jax.ShapeDtypeStruct(shape, F32) for shape in shapes],
        in_specs=[pl.BlockSpec(memory_space=pl.ANY)] * (len(operands) + len(pairs) + len(cubes)) + [vmem] * len(small),
        out_specs=[vmem] * len(shapes),
        scratch_shapes=scratch,
        compiler_params=pltpu.CompilerParams(collective_id=call_id, has_side_effects=True, vmem_limit_bytes=60 * 2**20),
    )(*operands, *pairs, *cubes, *small)
    h, p, c = len(halves), len(pairs), len(cubes)
    return list(zip(found[:h], found[h:2 * h])), found[2 * h:2 * h + p], found[2 * h + p:2 * h + p + c], found[2 * h + p + c:]


class PassStates:
    def __init__(self, places, forward, mine, turned, total, send_sems, recv_sems):
        self.places, self.forward, self.ahead = places, forward, 1 if forward else -1
        self.mine, self.turned, self.total = mine, turned, total
        self.send_sems, self.recv_sems = send_sems, recv_sems
        self.w, self.place, self.side, self.n = position()

    def copy(self, k):
        return pltpu.make_async_remote_copy(
            src_ref=self.mine, dst_ref=self.turned.at[k], send_sem=self.send_sems.at[k], recv_sem=self.recv_sems.at[k],
            device_id=(self.w + 2 * self.ahead * k, self.n), device_id_type=MESH)

    def inside(self, there):
        return (there >= 0) & (there < self.places)

    def start(self, state, maps):
        self.mine[:, :, :DV] = state.astype(BF)
        self.mine[:, :, DV:] = maps.astype(BF)
        for k in range(1, self.places):
            @pl.when(self.inside(self.place + self.ahead * k))
            def _():
                self.copy(k).start()

    def finish(self, out):
        total, turned = self.total, self.turned
        total[...] = jnp.zeros_like(total)
        for k in range(self.places - 1, 0, -1):
            @pl.when(self.inside(self.place - self.ahead * k))
            def _():
                self.copy(k).wait_recv()
                for h in range(total.shape[0]):
                    apply = mm if self.forward else mm_tn
                    total[h] = apply(turned[k, h, :, DV:], total[h]) + turned[k, h, :, :DV].astype(F32)

        out[...] = total[...].astype(out.dtype)
        for k in range(1, self.places):
            @pl.when(self.inside(self.place + self.ahead * k))
            def _():
                self.copy(k).wait_send()

    @staticmethod
    def scratch(places, heads):
        return [pltpu.VMEM((heads, DK, DV + DK), BF), pltpu.VMEM((places, heads, DK, DV + DK), BF),
                pltpu.VMEM((heads, DK, DV), F32), pltpu.SemaphoreType.DMA((places,)), pltpu.SemaphoreType.DMA((places,))]


def forward_gather_kernel(heads, nb, places, cuts, halved, *refs):
    m = len(cuts)
    inputs, sources, refs = refs[:8], refs[8:8 + m], refs[8 + m:]
    others, refs = iter(refs[:sum(halved)]), refs[sum(halved):]
    others = [next(others) if h else None for h in halved]
    outs, entry_ref, targets, refs = refs[:5], refs[5], refs[6:6 + m], refs[6 + m:]
    gather = LineGather(places, cuts, sources, others, targets, *refs[2:5])
    states = PassStates(places, True, *refs[5:])
    step = pl.program_id(0)

    @pl.when(step == 0)
    def _():
        greet(line=places, pair=True, places=places)
        gather.start()

    forward_kernel(heads, *inputs, *outs, *refs[:2])
    events = gather.events()
    early = min(len(events) // 2, nb)
    for i in range(nb):
        @pl.when(step == i)
        def _():
            for event in events[early * i // nb:early * (i + 1) // nb]:
                gather.run(event)

    @pl.when(step == nb - 1)
    def _():
        states.start(outs[4][:, :, :DV], outs[4][:, :, DV:])
        for event in events[early:(early + len(events)) // 2]:
            gather.run(event)
        states.finish(entry_ref)
        for event in events[(early + len(events)) // 2:]:
            gather.run(event)
        gather.finish()


def forward_gather(flags, mixed, taps, small, live, a_log, dt_bias, heads, blocks, call_id, chunks=2):
    rows, width = live.shape[0], mixed.shape[1]
    nb = rows // BLOCK
    count = lax.axis_size("wide")
    halved = [isinstance(block, tuple) for block in blocks]
    others = [b[1] for b, h in zip(blocks, halved) if h]
    blocks = [b[0] if h else b for b, h in zip(blocks, halved)]
    cuts = [row_cuts(block.shape[0], chunks) for block in blocks]
    row = lambda width: pl.BlockSpec((BLOCK, width), lambda i: (i, 0))
    same = lambda *shape: pl.BlockSpec(shape, lambda i: (0,) * len(shape))
    hbm = pl.BlockSpec(memory_space=pl.ANY)
    found = pl.pallas_call(
        functools.partial(forward_gather_kernel, heads, nb, count // 2, cuts, halved),
        grid=(nb,),
        in_specs=[pl.BlockSpec(memory_space=pltpu.SMEM), row(width), pl.BlockSpec((16, width), lambda i: (rows // 16, 0)),
                  same(*taps.shape), row(small.shape[1]), row(1), same(1, heads), same(1, heads)]
                 + [hbm] * (len(blocks) + len(others)),
        out_specs=[row(heads * DV), row(heads * DK),
                   pl.BlockSpec((1, heads, BLOCK, BLOCK), lambda i: (i, 0, 0, 0)),
                   pl.BlockSpec((1, heads, DK, DV + DK), lambda i: (i, 0, 0, 0)),
                   same(heads, DK, DV + DK), same(heads, DK, DV)] + [hbm] * len(blocks),
        out_shape=[jax.ShapeDtypeStruct((rows, heads * DV), F32), jax.ShapeDtypeStruct((rows, heads * DK), BF),
                   jax.ShapeDtypeStruct((nb, heads, BLOCK, BLOCK), BF),
                   jax.ShapeDtypeStruct((nb, heads, DK, DV + DK), BF),
                   jax.ShapeDtypeStruct((heads, DK, DV + DK), F32), jax.ShapeDtypeStruct((heads, DK, DV), BF)]
                  + [jax.ShapeDtypeStruct((count,) + block.shape, block.dtype) for block in blocks],
        scratch_shapes=[pltpu.VMEM((heads, DK, DV + DK), F32), pltpu.VMEM((8, width), F32)]
                       + LineGather.scratch(count, cuts) + PassStates.scratch(count // 2, heads),
        compiler_params=pltpu.CompilerParams(collective_id=call_id, has_side_effects=True, vmem_limit_bytes=48 * 2**20),
    )(flags, mixed, mixed, taps, small, live, a_log, dt_bias, *blocks, *others)
    return found[:6], flat_blocks(found[6:])


def backward_scatter_kernel(heads, nb, places, half_cuts, pair_cuts, shares, *refs):
    hm, pm = len(half_cuts), len(pair_cuts)

    def take(count):
        nonlocal refs
        found, refs = refs[:count], refs[count:]
        return found

    inputs, operands, pairs, share_in = tuple(take(15)), take(2 * hm), take(pm), take(shares)
    outs, half_outs, half_theirs, pair_outs, share_outs = take(4), take(hm), take(hm), take(pm), take(shares)
    scratch = take(2)
    states, exit_ref = PassStates(places, False, *take(5)), take(1)[0]
    direct_ref, end_ref = inputs[-2:]
    inputs = inputs[:-2] + (exit_ref,)
    buffers, product_sems = take(2 * hm), take(1)[0]
    half, refs = LineScatter.take(places, half_cuts, False, None, refs)
    products = Products(half, operands, buffers, product_sems)
    groups = [half]
    if pm:
        pair, refs = LineScatter.take(places, pair_cuts, True, pairs, refs)
        groups.append(pair)
    share, refs = NarrowScatter.take(share_in, refs)
    groups.append(share)
    step = pl.program_id(0)

    @pl.when(step == 0)
    def _():
        products.start()
        greet(line=places, pair=True, cube=True, places=places)
        states.start(direct_ref[...], end_ref[:, :, DV:])
        for group in groups:
            group.start()
        states.finish(exit_ref)
        products.wait()

    backward_kernel(heads, *inputs, *outs, *scratch)
    events = merged(groups)
    for i in range(nb):
        @pl.when(step == i)
        def _():
            for group, event in events[len(events) * i // nb:len(events) * (i + 1) // nb]:
                group.run(event)

    @pl.when(step == nb - 1)
    def _():
        share.finish(share_outs)
        if pm:
            pair.finish(pair_outs)
        half.finish(half_outs, half_theirs)


def backward_scatter(flags, mixed, taps, small, live, a_log, dt_bias, t, z, go, entry, direct, end, heads, halves, pairs, shares, call_id,
                     chunks=2):
    rows, width = live.shape[0], mixed.shape[1]
    nb = rows // BLOCK
    places = lax.axis_size("wide") // 2
    halves, operands = product_terms(halves, places)
    half_cuts = [row_cuts(term.shape[2], chunks) for term in halves]
    pair_cuts = [row_cuts(term.shape[1], chunks) for term in pairs]
    h = len(halves)
    narrow = lax.axis_size("narrow")
    sums = [term.shape[2:] for term in halves] * 2 + [term.shape[1:] for term in pairs]
    sums += [(term.shape[0], term.shape[1] // narrow) for term in shares]
    row = lambda width: pl.BlockSpec((BLOCK, width), lambda i: (nb - 1 - i, 0))
    same = lambda *shape: pl.BlockSpec(shape, lambda i: (0,) * len(shape))
    prev = pl.BlockSpec((16, width), lambda i: (jnp.maximum((nb - 1 - i) * (BLOCK // 16) - 1, 0), 0))
    found = pl.pallas_call(
        functools.partial(backward_scatter_kernel, heads, nb, places, half_cuts, pair_cuts, len(shares)),
        grid=(nb,),
        in_specs=[pl.BlockSpec(memory_space=pltpu.SMEM), row(width), prev,
                  pl.BlockSpec((16, width), lambda i: (rows // 16, 0)), same(*taps.shape), row(small.shape[1]), row(1),
                  same(1, heads), same(1, heads),
                  pl.BlockSpec((1, heads, BLOCK, BLOCK), lambda i: (nb - 1 - i, 0, 0, 0)),
                  pl.BlockSpec((1, heads, DK, DV + DK), lambda i: (nb - 1 - i, 0, 0, 0)),
                  row(heads * DV), same(heads, DK, DV), same(heads, DK, DV), same(heads, DK, DV + DK)]
                 + [pl.BlockSpec(memory_space=pl.ANY)] * (len(operands) + len(pairs) + len(shares)),
        out_specs=[same(rows + 16, width), row(2 * heads), same(*taps.shape), same(8, heads)]
                  + [pl.BlockSpec(shape, lambda i: (0, 0), pipeline_mode=pl.Buffered(1)) for shape in sums],
        out_shape=[jax.ShapeDtypeStruct((rows + 16, width), BF), jax.ShapeDtypeStruct((rows, 2 * heads), F32),
                   jax.ShapeDtypeStruct(taps.shape, F32), jax.ShapeDtypeStruct((8, heads), F32)]
                  + [jax.ShapeDtypeStruct(shape, F32) for shape in sums],
        scratch_shapes=[pltpu.VMEM((heads, DK, DV), F32), pltpu.VMEM((8, width), F32)]
                       + PassStates.scratch(places, heads) + [pltpu.VMEM((heads, DK, DV), F32)]
                       + Products.scratch(operands) + LineScatter.scratch(places, half_cuts, False, halves)
                       + (LineScatter.scratch(places, pair_cuts, True, pairs) if pairs else [])
                       + NarrowScatter.scratch(shares, narrow),
        compiler_params=pltpu.CompilerParams(collective_id=call_id, has_side_effects=True, vmem_limit_bytes=60 * 2**20),
    )(flags, mixed, mixed, mixed, taps, small, live, a_log, dt_bias, t, z, go, entry, direct, end, *operands, *pairs, *shares)
    p = len(pairs)
    return (found[:4], list(zip(found[4:4 + h], found[4 + h:4 + 2 * h])), found[4 + 2 * h:4 + 2 * h + p],
            found[4 + 2 * h + p:])


TILE = 256


def place_rows(side_ref, own_ref, their_ref):
    return jnp.where(pl.program_id(0) // (pl.num_programs(0) // 2) == side_ref[0], own_ref[...], their_ref[...]).astype(F32)


def project_kernel(side_ref, own_ref, their_ref, rim_ref, gain_ref, w_ref, sw_ref, normed_ref, mixed_ref, small_ref):
    step = pl.program_id(0)

    def normal(x):
        return (x * lax.rsqrt(jnp.mean(x * x, axis=1, keepdims=True) + EPS) * gain_ref[...]).astype(BF)

    @pl.when(step < pl.num_programs(0) - 1)
    def _():
        normed = normal(place_rows(side_ref, own_ref, their_ref))
        normed_ref[...] = normed
        mixed_ref[...] = mm(normed, w_ref[...]).astype(BF)
        small_ref[...] = mm_nt(normed, sw_ref[...])

    @pl.when(step == pl.num_programs(0) - 1)
    def _():
        normed = normal(rim_ref[...].astype(F32))
        normed_ref[:16] = normed
        mixed_ref[:16] = mm(normed, w_ref[...]).astype(BF)


def row_specs(rows):
    tiles = 2 * rows // TILE
    held = lambda width: pl.BlockSpec((TILE, width), lambda i: (jnp.minimum(i, tiles - 1) % (tiles // 2), 0))
    tile = lambda width: pl.BlockSpec((TILE, width), lambda i: (jnp.minimum(i, tiles - 1), 0))
    every = lambda width: pl.BlockSpec((TILE, width), lambda i: (i, 0))
    same = lambda *shape: pl.BlockSpec(shape, lambda i: (0,) * len(shape))
    return tiles + 1, held, tile, every, same


def project(side, own, their, rim, gain, weight, small_weight):
    rows, width = own.shape
    steps, held, tile, every, same = row_specs(rows)
    columns = weight.shape[1]
    return pl.pallas_call(
        project_kernel,
        grid=(steps,),
        in_specs=[pl.BlockSpec(memory_space=pltpu.SMEM), held(width), held(width), same(16, width), same(1, width),
                  same(*weight.shape), same(*small_weight.shape)],
        out_specs=[every(width), every(columns), tile(small_weight.shape[0])],
        out_shape=[jax.ShapeDtypeStruct((2 * rows + 16, width), BF), jax.ShapeDtypeStruct((2 * rows + 16, columns), BF),
                   jax.ShapeDtypeStruct((2 * rows, small_weight.shape[0]), F32)],
        compiler_params=pltpu.CompilerParams(vmem_limit_bytes=48 * 2**20),
    )(side, own, their, rim, gain, weight, small_weight)


def unproject_kernel(side_ref, own_ref, their_ref, rim_ref, gain_ref, gm_ref, gg_ref, gs_ref, w_ref, gw_ref, sw_ref, back_ref,
                     rim_back_ref, grad_gain_ref):
    step = pl.program_id(0)

    @pl.when(step == 0)
    def _():
        grad_gain_ref[...] = jnp.zeros_like(grad_gain_ref)

    def norm_back(x, grad):
        factor = lax.rsqrt(jnp.mean(x * x, axis=1, keepdims=True) + EPS)
        unit = x * factor
        grad_gain_ref[...] += jnp.sum(grad * unit, axis=0, keepdims=True)
        scaled = grad * gain_ref[...]
        return (factor * (scaled - unit * jnp.mean(scaled * unit, axis=1, keepdims=True))).astype(BF)

    @pl.when(step < pl.num_programs(0) - 1)
    def _():
        grad = mm_nt(gm_ref[...], w_ref[...]) + mm_nt(gg_ref[...], gw_ref[...])
        for i in range(sw_ref.shape[0]):
            grad = grad + gs_ref[:, i:i + 1] * sw_ref[i:i + 1]
        back_ref[...] = norm_back(place_rows(side_ref, own_ref, their_ref), grad)

    @pl.when(step == pl.num_programs(0) - 1)
    def _():
        rim_back_ref[...] = norm_back(rim_ref[...].astype(F32), mm_nt(gm_ref[:16], w_ref[...]))


def unproject(side, own, their, rim, gain, grad_mixed, grad_gate, grad_small, weight, gate_weight, small_weight):
    rows, width = own.shape
    steps, held, tile, every, same = row_specs(rows)
    return pl.pallas_call(
        unproject_kernel,
        grid=(steps,),
        in_specs=[pl.BlockSpec(memory_space=pltpu.SMEM), held(width), held(width), same(16, width), same(1, width),
                  every(weight.shape[1]), tile(gate_weight.shape[1]), tile(grad_small.shape[1]), same(*weight.shape),
                  same(*gate_weight.shape), same(*small_weight.shape)],
        out_specs=[tile(width), same(16, width), same(1, width)],
        out_shape=[jax.ShapeDtypeStruct((2 * rows, width), BF), jax.ShapeDtypeStruct((16, width), BF),
                   jax.ShapeDtypeStruct((1, width), F32)],
        compiler_params=pltpu.CompilerParams(vmem_limit_bytes=56 * 2**20),
    )(side, own, their, rim, gain, grad_mixed, grad_gate, grad_small, weight, gate_weight, small_weight)


def mix_kernel(heads, x_ref, gw_ref, ow_ref, o_ref, e_ref, s_ref, live_ref, gain_ref, gate_ref, m_ref, out_ref):
    live = live_ref[...]
    gain = gain_ref[...]
    gates = mm(x_ref[...], gw_ref[...])
    gate_ref[...] = gates
    for h in range(heads):
        vs = slice(h * DV, (h + 1) * DV)
        y = (o_ref[:, vs] + mm(e_ref[:, h * DK:(h + 1) * DK], s_ref[h])) * live
        r = lax.rsqrt(jnp.mean(y * y, axis=1, keepdims=True) + EPS)
        gate = gates[:, vs]
        m_ref[:, vs] = (y * r * gain * (gate * jax.nn.sigmoid(gate))).astype(BF)
    out_ref[...] = mm_nt(m_ref[...], ow_ref[...]).astype(BF)


def mix(normed, gate_weight, out_weight, o, e, entry, live, gain, heads):
    rows, width = o.shape[0], normed.shape[1]
    row = lambda width: pl.BlockSpec((TILE, width), lambda i: (i, 0))
    same = lambda *shape: pl.BlockSpec(shape, lambda i: (0,) * len(shape))
    return pl.pallas_call(
        functools.partial(mix_kernel, heads),
        grid=(rows // TILE,),
        in_specs=[row(width), same(*gate_weight.shape), same(*out_weight.shape), row(heads * DV), row(heads * DK),
                  same(heads, DK, DV), row(1), same(1, DV)],
        out_specs=[row(heads * DV), row(heads * DV), row(width)],
        out_shape=[jax.ShapeDtypeStruct((rows, heads * DV), F32), jax.ShapeDtypeStruct((rows, heads * DV), BF),
                   jax.ShapeDtypeStruct((rows, width), BF)],
        compiler_params=pltpu.CompilerParams(vmem_limit_bytes=48 * 2**20),
    )(normed, gate_weight, out_weight, o, e, entry, live, gain)


def feed_kernel(places, chunks, own_ref, cot_hbm, wg_hbm, wu_hbm, wd_hbm, sum_ref, down_hbm, dwd_hbm, dwg_hbm, dwu_hbm,
                rows, cot, wg, wu, wd, hid, gg, gu, gr, pair, line, dn, dwd, dwg, dwu, load_sems, out_sems, own_sem,
                ag_send, ag_recv, pair_send, pair_recv, right_send, right_recv, left_send, left_recv):
    w, place, side, n = position()
    partner = w + 1 - 2 * side
    quarter, width = own_ref.shape
    size = quarter // chunks
    part = lambda c: pl.ds(c * size, size)
    devices = [(partner, n), (w + 2, n), (w - 2, n)]
    loads = [pltpu.make_async_copy(source, target, load_sems.at[i]) for i, (source, target) in enumerate(
        ((wg_hbm, wg), (wu_hbm, wu), (cot_hbm, cot), (wd_hbm, wd)))]

    def remote(source, target, send, recv, device):
        return pltpu.make_async_remote_copy(src_ref=source, dst_ref=target, send_sem=send, recv_sem=recv, device_id=device,
                                            device_id_type=MESH)

    def move(slot, way, c, own=False):
        source = own_ref.at[part(c)] if own else rows.at[slot, part(c)]
        return remote(source, rows.at[slot, part(c)], ag_send.at[way, slot, c], ag_recv.at[slot, c], devices[way])

    def along(slot, way, c, own=False):
        @pl.when(place < places - 1 if way == 1 else place > 0)
        def _():
            move(slot, way, c, own).start()

    def across(t, c):
        return remote(gr.at[2 * t + 1 - side, part(c)], pair.at[t, part(c)], pair_send.at[t, c], pair_recv.at[t, c], devices[0])

    def right(t, c):
        return remote(gr.at[2 * t + side, part(c)], line.at[t, part(c)], right_send.at[t, c], right_recv.at[t, c], devices[1])

    def left(t, c, arriving=False):
        slot = jnp.where(t == place - (0 if arriving else 1), places, t)
        return remote(gr.at[2 * t + side, part(c)], line.at[slot, part(c)], left_send.at[t, c], left_recv.at[t, c], devices[2])

    def inside(there):
        return (there >= 0) & (there < places)

    def arrive(s):
        for way, there in ((1, place - s), (2, place + s)):
            @pl.when(inside(there))
            def _():
                for c in range(chunks):
                    move(2 * there + side, way, c).wait_recv()
                    along(2 * there + side, way, c)
                    move(2 * there + side, 0, c).start()

    def work(there):
        for c in range(chunks):
            move(2 * there + 1 - side, 0, c).wait_recv()
        both = pl.ds(2 * there, 2)
        flat = lambda ref: ref[both].reshape(2 * quarter, ref.shape[2])
        x = flat(rows)
        gate = mm_nt(x, wg[...])
        up = mm_nt(x, wu[...])
        grad = mm_nt(flat(cot), wd[...])
        sig = jax.nn.sigmoid(gate)
        act = gate * sig
        hid[both] = (act * up).astype(BF).reshape(2, quarter, -1)
        low_gate = (grad * up * (sig + act * (1.0 - sig))).astype(BF)
        low_up = (grad * act).astype(BF)
        gg[both] = low_gate.reshape(2, quarter, -1)
        gu[both] = low_up.reshape(2, quarter, -1)
        gr[both] = (mm(low_gate, wg[...]) + mm(low_up, wu[...])).astype(BF).reshape(2, quarter, width)
        for c in range(chunks):
            across(there, c).start()

    def add(t, c, other, slot):
        at = (2 * t + side, part(c))
        gr[at] = (gr[at].astype(F32) + other[slot, part(c)].astype(F32)).astype(BF)

    def pass_on(s):
        t = s

        @pl.when(place < t)
        def _():
            for c in range(chunks):
                across(t, c).wait_recv()
                add(t, c, pair, t)

                @pl.when(place > 0)
                def _():
                    right(t, c).wait_recv()
                    add(t, c, line, t)

                right(t, c).start()

        t_left = places - 1 - s

        @pl.when(place > t_left)
        def _():
            for c in range(chunks):
                across(t_left, c).wait_recv()
                add(t_left, c, pair, t_left)

                @pl.when(place < places - 1)
                def _():
                    left(t_left, c, True).wait_recv()
                    add(t_left, c, line, t_left)

                left(t_left, c).start()

    greet(line=places, pair=True)
    for load in loads:
        load.start()
    for c in range(chunks):
        move(w, 0, c, True).start()
        along(w, 1, c, True)
        along(w, 2, c, True)
    own = pltpu.make_async_copy(own_ref, rows.at[w], own_sem)
    own.start()
    own.wait()
    for load in loads:
        load.wait()

    def rows_work(s, _):
        @pl.when(inside(place - s))
        def _():
            work(place - s)

        @pl.when(inside(place + s) & (s > 0))
        def _():
            work(place + s)
        return 0

    def advance(s, _):
        arrive(s)
        rows_work(s - 1, 0)

        @pl.when(s > 1)
        def _():
            pass_on(s - 1)
        return 0

    lax.fori_loop(1, places, advance, 0)
    rows_work(places - 1, 0)

    columns = width // 4

    def weights(i, _):
        cut = pl.ds(pl.multiple_of(i * columns, columns), columns)
        everything = lambda ref: ref[...].reshape(2 * places * quarter, ref.shape[2])
        slot = lax.rem(i, 2)

        @pl.when(i >= 2)
        def _():
            pltpu.make_async_copy(dn.at[slot], down_hbm.at[pl.ds(0, 2)], out_sems.at[3 + slot]).wait()

        dwd[:, cut] = mm_tn(everything(hid), cot[:, :, cut].reshape(2 * places * quarter, columns)).astype(BF)
        x = rows[:, :, cut].reshape(2 * places * quarter, columns)
        dwg[:, cut] = mm_tn(everything(gg), x).astype(BF)
        dwu[:, cut] = mm_tn(everything(gu), x).astype(BF)
        both = pl.ds(2 * i, 2)
        dn[slot] = jnp.dot(hid[both].reshape(2 * quarter, hid.shape[2]), wd[...],
                           preferred_element_type=F32).astype(BF).reshape(2, quarter, width)
        pltpu.make_async_copy(dn.at[slot], down_hbm.at[both], out_sems.at[3 + slot]).start()
        return 0

    before = jnp.where((place > 0) & (place < places - 1), 2, 0)
    lax.fori_loop(0, before, weights, 0)
    pass_on(places - 1)
    lax.fori_loop(before, 4, weights, 0)
    outs = [pltpu.make_async_copy(source, target, out_sems.at[i]) for i, (source, target) in enumerate(
        ((dwd, dwd_hbm), (dwg, dwg_hbm), (dwu, dwu_hbm)))]
    for out in outs:
        out.start()
    for c in range(chunks):
        across(place, c).wait_recv()
        add(place, c, pair, place)

        @pl.when(place > 0)
        def _():
            right(place, c).wait_recv()
            add(place, c, line, place)

        @pl.when(place < places - 1)
        def _():
            left(place, c, True).wait_recv()
            add(place, c, line, places)

        sum_ref[part(c)] = gr[2 * place + side, part(c)].astype(F32)
    for out in outs:
        out.wait()
    for slot in range(2):
        pltpu.make_async_copy(dn.at[slot], down_hbm.at[pl.ds(0, 2)], out_sems.at[3 + slot]).wait()

    def settle(t, _):
        for c in range(chunks):
            across(t, c).wait_send()
            move(2 * t + side, 0, c).wait_send()

            @pl.when((place < places - 1) & (t <= place))
            def _():
                move(2 * t + side, 1, c).wait_send()

            @pl.when((place > 0) & (t >= place))
            def _():
                move(2 * t + side, 2, c).wait_send()

            @pl.when(t > place)
            def _():
                right(t, c).wait_send()

            @pl.when(t < place)
            def _():
                left(t, c).wait_send()
        return 0

    lax.fori_loop(0, places, settle, 0)


def feed(own, cot, w_gate, w_up, w_down, call_id, chunks=4):
    count = lax.axis_size("wide")
    places = count // 2
    quarter, width = own.shape
    units = w_down.shape[0]
    hbm, vmem = pl.BlockSpec(memory_space=pl.ANY), pl.BlockSpec(memory_space=pltpu.VMEM)
    blocks = lambda columns: pltpu.VMEM((count, quarter, columns), BF)
    line = lambda amount: pltpu.VMEM((amount, quarter, width), BF)
    sems = pltpu.SemaphoreType.DMA((places, chunks))
    return pl.pallas_call(
        functools.partial(feed_kernel, places, chunks),
        in_specs=[vmem, hbm, hbm, hbm, hbm],
        out_specs=[vmem, hbm, hbm, hbm, hbm],
        out_shape=[jax.ShapeDtypeStruct((quarter, width), F32), jax.ShapeDtypeStruct((count, quarter, width), BF),
                   jax.ShapeDtypeStruct((units, width), BF), jax.ShapeDtypeStruct((units, width), BF),
                   jax.ShapeDtypeStruct((units, width), BF)],
        scratch_shapes=[blocks(width), blocks(width), pltpu.VMEM((units, width), BF), pltpu.VMEM((units, width), BF),
                        pltpu.VMEM((units, width), BF), blocks(units), blocks(units), blocks(units), blocks(width),
                        line(places), line(places + 1), pltpu.VMEM((2, 2, quarter, width), BF), pltpu.VMEM((units, width), BF),
                        pltpu.VMEM((units, width), BF), pltpu.VMEM((units, width), BF), pltpu.SemaphoreType.DMA((4,)),
                        pltpu.SemaphoreType.DMA((5,)), pltpu.SemaphoreType.DMA, pltpu.SemaphoreType.DMA((3, count, chunks)),
                        pltpu.SemaphoreType.DMA((count, chunks))] + [sems] * 6,
        compiler_params=pltpu.CompilerParams(collective_id=call_id, has_side_effects=True, vmem_limit_bytes=60 * 2**20),
    )(own, cot.reshape(count, quarter, width), w_gate, w_up, w_down)


CONV = 4


def rms_norm(value, gain):
    return value * lax.rsqrt(jnp.mean(value * value, axis=-1, keepdims=True) + EPS) * gain


def after(value, *others):
    return lax.optimization_barrier((value,) + others)[0]


def part(value, axis, index, count=2):
    size = value.shape[axis] // count
    return lax.dynamic_slice_in_dim(value, index * size, size, axis)


def ordered(mine, theirs, side, axis):
    return jnp.concatenate([jnp.where(side == 0, mine, theirs), jnp.where(side == 0, theirs, mine)], axis=axis)


def sequence_tables(doc_lengths, first_row, row_count, block_size):
    padded = (doc_lengths + block_size - 1) // block_size * block_size
    seq_ends = jnp.cumsum(padded)
    seq_starts = seq_ends - padded
    row_places = first_row + jnp.arange(row_count, dtype=jnp.int32)
    inside_mask = (row_places[:, None] >= seq_starts[None, :]) & (row_places[:, None] < seq_ends[None, :])
    live_mask = jnp.any(inside_mask & (row_places[:, None] < (seq_starts + doc_lengths)[None, :]), axis=1, keepdims=True)
    fresh_block = jnp.any(row_places[::block_size][:, None] == seq_starts[None, :], axis=1)
    return live_mask.astype(F32), jnp.where(fresh_block, 0.0, 1.0).astype(F32)


def contract_rows(left, right):
    return lax.dot_general(left, right, (((0,), (0,)), ((), ())), preferred_element_type=F32)


def contract_cols(left, right):
    return lax.dot_general(left, right, (((1,), (1,)), ((), ())), preferred_element_type=F32)


def feed_apart(own, cot, w_gate, w_up, w_down):
    quarter = own.shape[0]
    blocks = lambda a: a.astype(BF).reshape(-1, quarter, a.shape[1])
    gathered_rows = line_gather([own], 3)[0]
    gate_pre = contract_cols(gathered_rows, w_gate)
    up_pre = contract_cols(gathered_rows, w_up)
    gate_sig = jax.nn.sigmoid(gate_pre)
    gate_act = gate_pre * gate_sig
    hidden_low = (gate_act * up_pre).astype(BF)
    grad_hidden = contract_cols(cot, w_down)
    grad_gate_low = (grad_hidden * up_pre * gate_sig * (1.0 + gate_pre * (1.0 - gate_sig))).astype(BF)
    grad_up_low = (grad_hidden * gate_act).astype(BF)
    grad_rows = (jnp.dot(grad_gate_low, w_gate, preferred_element_type=F32)
                 + jnp.dot(grad_up_low, w_up, preferred_element_type=F32))
    grad_sum = line_scatter([], [blocks(grad_rows)], [], [], 4)[1][0]
    down_rows = blocks(jnp.dot(hidden_low, w_down, preferred_element_type=F32))
    grad_w_down = contract_rows(hidden_low, cot).astype(BF)
    grad_w_gate = contract_rows(grad_gate_low, gathered_rows).astype(BF)
    grad_w_up = contract_rows(grad_up_low, gathered_rows).astype(BF)
    return grad_sum, down_rows, grad_w_down, grad_w_gate, grad_w_up


def shards(block_input, gain_attn, w_query, w_key, w_value, w_gate_out, w_decay, w_beta, conv_query, conv_key,
           conv_value, a_log, dt_bias, out_gain, w_out, gain_mlp, w_gate, w_up, w_down, doc_lengths, cotangent):
    d_model = block_input.shape[1]
    row_count = 2 * block_input.shape[0]
    quarter = cotangent.shape[0]
    depth = w_query.shape[0]
    heads = a_log.shape[0] // 2
    narrow = lax.axis_size("narrow")
    wide = lax.axis_size("wide")
    wide_index = lax.axis_index("wide")
    place, side = wide_index // 2, wide_index % 2
    live, flags = sequence_tables(doc_lengths, place * row_count, row_count, BLOCK)
    gain_row, a_row, dt_row = out_gain[None, :], part(a_log, 0, side)[None, :], part(dt_bias, 0, side)[None, :]
    key_width, value_width = heads * DK, heads * DV
    columns = 2 * key_width + value_width
    row_blocks = lambda a: a.astype(BF).reshape(-1, quarter, a.shape[1])
    halves = lambda *arrays: tuple(
        jnp.concatenate([part(a, 1, s) for a in arrays], axis=1) for s in (side, 1 - side))
    padded = lambda a: jnp.pad(a, ((0, 16 - 4 * heads), (0, 0)))

    first, small_weight, their_input, rim_input = line_gather(
        [halves(w_query, w_key, w_value), padded(jnp.concatenate([w_decay.T, w_beta.T], axis=0))], 1, rows=block_input)
    rim_input = jnp.where(place > 0, rim_input, jnp.zeros_like(rim_input))
    small_weight = small_weight.reshape(wide, 16, depth).transpose(1, 0, 2).reshape(16, d_model)
    small_weight = jnp.concatenate([part(small_weight[:2 * heads], 0, side), part(small_weight[2 * heads:4 * heads], 0, side)],
                                   axis=0)
    taps = jnp.concatenate([part(conv_query, 1, side), part(conv_key, 1, side), part(conv_value, 1, side)], axis=1)
    side_word = side.astype(jnp.int32)[None]
    padded_small = jnp.pad(small_weight, ((0, 16 - 2 * heads), (0, 0)))
    normed_low, mixed, small = project(side_word, block_input, their_input, rim_input, gain_attn[None, :], first, padded_small)
    small = small[:, :2 * heads]

    (local_out, reach, inverses, states, end, entry), (gate_weight, gathered_cot, out_weight) = forward_gather(
        flags, mixed, taps, small, live, a_row, dt_row, heads, [halves(w_gate_out), cotangent, halves(w_out)], 7)
    gate_rows, mixer_low, head_part = mix(normed_low, gate_weight, out_weight, local_out, reach, entry, live,
                                          gain_row, heads)
    own_rows = cube_scatter(row_blocks(head_part), 9) + part(
        block_input, 0, lax.axis_index("narrow"), narrow).astype(F32)
    mlp_normed, mlp_norm_back = jax.vjp(rms_norm, own_rows, gain_mlp)
    feed_forward = feed_apart if wide > 8 else functools.partial(feed, call_id=3)
    grad_mlp_normed, down_rows, grad_w_down, grad_w_gate, grad_w_up = feed_forward(
        mlp_normed.astype(BF), gathered_cot, w_gate.T, w_up.T, w_down)
    grad_own_norm, grad_gain_mlp = mlp_norm_back(grad_mlp_normed)
    grad_own = cotangent.astype(F32) + grad_own_norm
    grad_attn = cube_gather(grad_own.astype(BF), 10)

    grad_mixer = jnp.dot(grad_attn, out_weight, preferred_element_type=F32)
    grad_outputs, grad_gate_rows, grad_out_gain, direct = unfinish(local_out, reach, entry, gate_rows, live, gain_row,
                                                                   grad_mixer, heads)
    (grad_mixed, grad_small, grad_taps, grad_scalars), (sum_w_out, sum_w_gate_out), (sum_down,), shares = backward_scatter(
        flags, mixed, taps, small, live, a_row, dt_row, inverses, states, grad_outputs, entry, direct, end, heads,
        [(grad_attn, mixer_low), (normed_low, grad_gate_rows)], [down_rows], [grad_w_gate, grad_w_up, grad_w_down], 8)
    output = (own_rows + sum_down).astype(BF)
    grad_small = grad_small.astype(BF)
    grad_small_weight = contract_rows(grad_small, normed_low[:row_count]).astype(BF)
    both_sides = lambda a: ordered(a, jnp.zeros_like(a), side, 0)
    grad_small_weight = padded(jnp.concatenate([both_sides(grad_small_weight[:heads]), both_sides(grad_small_weight[heads:])],
                                               axis=0))
    small_blocks = grad_small_weight.reshape(16, wide, depth).transpose(1, 0, 2)
    grad_input_part, grad_rim, grad_gain_attn = unproject(
        side_word, block_input, their_input, rim_input, gain_attn[None, :], grad_mixed, grad_gate_rows, grad_small.astype(F32),
        first, gate_weight, small_weight.astype(F32))
    grad_rim = jnp.pad(grad_rim[None], ((7, 0), (0, 0), (0, 0)))

    lanes = lambda a: jnp.pad(a, (0, -a.shape[0] % 1024)).reshape(-1, 128)
    head_sums = lanes(jnp.concatenate([grad_taps.reshape(-1), grad_scalars[0], grad_scalars[1]]))
    whole_sums = lanes(jnp.concatenate([grad_gain_attn[0], grad_gain_mlp, grad_out_gain[0]]))
    (sum_first,), (sum_small,), (input_sum, _), (every,) = line_scatter(
        [(normed_low, grad_mixed)], [small_blocks], [row_blocks(grad_input_part), grad_rim],
        [jnp.concatenate([head_sums, whole_sums], axis=0)], 6)
    grad_input = input_sum + grad_own
    whole_sums = jnp.sum(every[:, head_sums.shape[0]:], axis=0).reshape(-1)
    every = every[:, :head_sums.shape[0]].reshape(2, narrow, -1)
    conv_all = every[:, :, :4 * columns].reshape(2, narrow, 4, columns)
    conv_parts = [conv_all[:, :, :, lo:hi].transpose(2, 1, 0, 3).reshape(4, -1) for lo, hi in
                  ((0, key_width), (key_width, 2 * key_width), (2 * key_width, columns))]
    scalars = [every[:, :, lo:lo + heads].transpose(1, 0, 2).reshape(-1) for lo in (4 * columns, 4 * columns + heads)]
    joined = lambda found, lo, hi: ordered(found[0][:, lo:hi], found[1][:, lo:hi], side, 1)
    return (
        output, grad_input, whole_sums[:d_model],
        joined(sum_first, 0, key_width), joined(sum_first, key_width, 2 * key_width), joined(sum_first, 2 * key_width, columns),
        joined(sum_w_gate_out, 0, value_width),
        sum_small[:2 * heads].T, sum_small[2 * heads:4 * heads].T, conv_parts[0], conv_parts[1], conv_parts[2],
        scalars[0], scalars[1], whole_sums[2 * d_model:2 * d_model + DV], joined(sum_w_out, 0, value_width),
        whole_sums[d_model:2 * d_model], shares[0].T, shares[1].T, shares[2],
    )


def solution(mesh):
    both = P("wide", "narrow")
    rows = P(("wide", "narrow"), None)
    return jax.shard_map(
        shards,
        mesh=mesh,
        in_specs=(P("wide", None), P(), both, both, both, both, both, both, P(None, "narrow"), P(None, "narrow"),
                  P(None, "narrow"), P("narrow"), P("narrow"), P(), both, P(), P(None, "wide"), P(None, "wide"),
                  P("wide", None), P(), rows),
        out_specs=(rows, rows, P(), both, both, both, both, both, both, P(), P(), P(), P(), P(), P(), both, P(),
                   P("narrow", "wide"), P("narrow", "wide"), both),
        check_vma=False,
    )
```

```python
import functools
import jax
import jax.numpy as jnp
from jax import lax
from jax.experimental import pallas as pl
from jax.experimental.pallas import tpu as pltpu
from jax.sharding import PartitionSpec as P

DK, DV, BLOCK, EPS = 128, 256, 64, 1e-6
BF = jnp.bfloat16
F32 = jnp.float32


def mm(a, b):
    return jnp.dot(a.astype(BF), b.astype(BF), preferred_element_type=F32)


def mm_nt(a, b):
    return lax.dot_general(a.astype(BF), b.astype(BF), (((1,), (1,)), ((), ())), preferred_element_type=F32)


def mm_tn(a, b):
    return lax.dot_general(a.astype(BF), b.astype(BF), (((0,), (0,)), ((), ())), preferred_element_type=F32)


def split(a):
    high = a.astype(BF)
    return high, (a - high.astype(F32)).astype(BF)


def mm_fine(a, b):
    ah, al = split(a)
    bh, bl = split(b)
    return mm(ah, bh) + (mm(ah, bl) + mm(al, bh))


def unit_lower_inverses(systems, rows, cols):
    gap = rows ^ cols
    below = rows > cols
    unit = jnp.where(rows == cols, 1.0, 0.0)
    found = [unit - jnp.where(below & (gap < 2), a, 0.0) for a in systems]
    size = 2
    while size < systems[0].shape[0]:
        mask = below & (gap >= size) & (gap < 2 * size)
        inner = [mm_fine(jnp.where(mask, a, 0.0), t) for a, t in zip(systems, found)]
        found = [t - mm_fine(t, m) for t, m in zip(found, inner)]
        size *= 2
    return found


def block_tables(g_col, g_row, rows, cols):
    lower = rows >= cols
    return jnp.where(lower, jnp.exp(jnp.where(lower, g_col - g_row, 0.0)), 0.0)


def shifted(rows, before, back):
    if back == 0:
        return rows
    return jnp.concatenate([before[8 - back:], rows[:rows.shape[0] - back]], axis=0)


def conv_rows(rows, before, taps):
    count = taps.shape[0]
    total = taps[count - 1:count] * rows
    for back in range(1, count):
        total = total + taps[count - 1 - back:count - back] * shifted(rows, before, back)
    return total


def head_slices(heads, h):
    key = heads * DK
    return slice(h * DK, (h + 1) * DK), slice(key + h * DK, key + (h + 1) * DK), slice(2 * key + h * DV, 2 * key + (h + 1) * DV)


def unit_factor(rows):
    return lax.rsqrt(jnp.sum(rows * rows, axis=1, keepdims=True) + EPS)


def exact_tn(a, b):
    return lax.dot_general(a, b, (((0,), (0,)), ((), ())), precision=lax.Precision.HIGHEST, preferred_element_type=F32)


def softplus(x):
    return jnp.maximum(x, 0.0) + jnp.log(1.0 + jnp.exp(-jnp.abs(x)))


def decay_tables(heads, small, a_log, dt_bias, live, rows, cols):
    speed = -jnp.exp(a_log)
    biased = small[:, :heads] + dt_bias
    log_decay = speed * softplus(biased)
    sig = jax.nn.sigmoid(small[:, heads:2 * heads])
    upto = jnp.where(rows <= cols, 1.0, 0.0)
    run = exact_tn(upto, log_decay)
    run_row = exact_tn(log_decay, upto)
    return speed, biased, log_decay, sig, sig * live, run, run_row


def forward_kernel(heads, flag_ref, x_ref, rim_ref, taps_ref, small_ref, live_ref, alog_ref, dt_ref,
                   o_ref, e_ref, t_ref, z_ref, end_ref, carry, before_ref):
    step = pl.program_id(0)
    rows = lax.broadcasted_iota(jnp.int32, (BLOCK, BLOCK), 0)
    cols = lax.broadcasted_iota(jnp.int32, (BLOCK, BLOCK), 1)
    flag = flag_ref[step]

    @pl.when(step == 0)
    def _():
        before_ref[...] = rim_ref[8:16, :].astype(F32)
        unit = jnp.where(lax.broadcasted_iota(jnp.int32, (DK, DK), 0) == lax.broadcasted_iota(jnp.int32, (DK, DK), 1), 1.0, 0.0)
        for h in range(heads):
            carry[h, :, :DV] = jnp.zeros((DK, DV), F32)
            carry[h, :, DV:] = unit

    _, _, _, _, betas, run, run_row = decay_tables(heads, small_ref[...], alog_ref[...], dt_ref[...], live_ref[...], rows, cols)
    openings = flag * jnp.exp(run)
    closings = jnp.exp(run[BLOCK - 1:BLOCK] - run)

    def active(columns):
        c = conv_rows(x_ref[:, columns].astype(F32), before_ref[:, columns] * flag, taps_ref[:, columns])
        return c * jax.nn.sigmoid(c)

    tables, systems, parts = [], [], []
    for h in range(heads):
        qs, ks, vs = head_slices(heads, h)
        q, k, v = active(qs), active(ks), active(vs).astype(BF)
        q = (q * unit_factor(q) * DK ** (-0.5)).astype(BF)
        k = (k * unit_factor(k)).astype(BF)
        parts.append((q, k, v))
        table = block_tables(run[:, h:h + 1], run_row[h:h + 1, :], rows, cols)
        tables.append(table)
        systems.append(jnp.where(rows > cols, betas[:, h:h + 1] * table * mm_nt(k, k), 0.0))
    before_ref[...] = x_ref[BLOCK - 8:, :].astype(F32)
    inverses = unit_lower_inverses(systems, rows, cols)
    for h in range(heads):
        q, k, v = parts[h]
        beta, opening, closing = betas[:, h:h + 1], openings[:, h:h + 1], closings[:, h:h + 1]
        low_t = inverses[h].astype(BF)
        t_ref[0, h] = low_t
        u = mm(low_t, beta * v.astype(F32))
        w = mm(low_t, (beta * opening) * k.astype(F32))
        scores = mm_nt(q, k) * tables[h]
        state = carry[h]
        low_state = state.astype(BF)
        z_ref[0, h] = low_state
        reach = mm(jnp.concatenate([w.astype(BF), (opening * q.astype(F32)).astype(BF)], axis=0), low_state)
        c = jnp.concatenate([u, jnp.zeros((BLOCK, DK), F32)], axis=1) - reach[:BLOCK]
        low_c = c.astype(BF)
        out = reach[BLOCK:] + mm(scores, low_c)
        o_ref[:, h * DV:(h + 1) * DV] = out[:, :DV]
        e_ref[:, h * DK:(h + 1) * DK] = out[:, DV:].astype(BF)
        new = opening[BLOCK - 1:BLOCK] * state + mm_tn(closing * k.astype(F32), low_c)
        carry[h] = new
        end_ref[h] = new


def unfinish_kernel(heads, o_ref, e_ref, s_ref, gate_ref, live_ref, gain_ref, gm_ref, go_ref, gg_ref, ggain_ref, direct_ref):
    @pl.when(pl.program_id(0) == 0)
    def _():
        ggain_ref[...] = jnp.zeros_like(ggain_ref)
        direct_ref[...] = jnp.zeros_like(direct_ref)

    live = live_ref[...]
    gain = gain_ref[...]
    total = jnp.zeros((1, DV), F32)
    for h in range(heads):
        vs = slice(h * DV, (h + 1) * DV)
        e = e_ref[:, h * DK:(h + 1) * DK]
        y = (o_ref[:, vs] + mm(e, s_ref[h])) * live
        r = lax.rsqrt(jnp.mean(y * y, axis=1, keepdims=True) + EPS)
        gate = gate_ref[:, vs]
        sig = jax.nn.sigmoid(gate)
        act = gate * sig
        gm = gm_ref[:, vs]
        unit = y * r
        gn = gm * act
        total = total + jnp.sum(gn * unit, axis=0, keepdims=True)
        gn = gn * gain
        gg_ref[:, vs] = (gm * unit * gain * (sig * (1.0 + gate * (1.0 - sig)))).astype(BF)
        go = (r * (gn - unit * jnp.mean(gn * unit, axis=1, keepdims=True)) * live).astype(BF)
        go_ref[:, vs] = go
        direct_ref[h] += mm_tn(e, go)
    ggain_ref[...] += total


def unfinish(o, e, entry, gate, live, gain, gm, heads, tile=256):
    rows = o.shape[0]
    row = lambda width: pl.BlockSpec((tile, width), lambda i: (i, 0))
    return pl.pallas_call(
        functools.partial(unfinish_kernel, heads),
        grid=(rows // tile,),
        in_specs=[row(heads * DV), row(heads * DK), pl.BlockSpec((heads, DK, DV), lambda i: (0, 0, 0)), row(heads * DV),
                  row(1), pl.BlockSpec((1, DV), lambda i: (0, 0)), row(heads * DV)],
        out_specs=[row(heads * DV), row(heads * DV), pl.BlockSpec((1, DV), lambda i: (0, 0)),
                   pl.BlockSpec((heads, DK, DV), lambda i: (0, 0, 0))],
        out_shape=[jax.ShapeDtypeStruct((rows, heads * DV), BF), jax.ShapeDtypeStruct((rows, heads * DV), BF),
                   jax.ShapeDtypeStruct((1, DV), F32), jax.ShapeDtypeStruct((heads, DK, DV), F32)],
        compiler_params=pltpu.CompilerParams(vmem_limit_bytes=48 * 2**20),
    )(o, e, entry, gate, live, gain, gm)


def silu_back(c, grad):
    sig = jax.nn.sigmoid(c)
    return grad * (sig * (1.0 + c * (1.0 - sig)))


def backward_kernel(heads, flag_ref, x_ref, prev_ref, rim_ref, taps_ref, small_ref, live_ref, alog_ref, dt_ref, t_ref, z_ref,
                    go_ref, s_ref, exit_ref, gx_ref, gsmall_ref, gtaps_ref, gscalar_ref, carry, after_ref):
    step = pl.program_id(0)
    nb = pl.num_programs(0)
    at = nb - 1 - step
    rows = lax.broadcasted_iota(jnp.int32, (BLOCK, BLOCK), 0)
    cols = lax.broadcasted_iota(jnp.int32, (BLOCK, BLOCK), 1)
    last = lax.broadcasted_iota(jnp.int32, (BLOCK, 1), 0) == BLOCK - 1
    flag = flag_ref[at]
    taps_count = taps_ref.shape[0]

    @pl.when(step == 0)
    def _():
        carry[...] = exit_ref[...].astype(F32)
        after_ref[...] = jnp.zeros_like(after_ref)
        gtaps_ref[...] = jnp.zeros_like(gtaps_ref)
        gscalar_ref[...] = jnp.zeros_like(gscalar_ref)

    live = live_ref[...]
    speed, biased, log_decay, sig, betas, run, run_row = decay_tables(
        heads, small_ref[...], alog_ref[...], dt_ref[...], live, rows, cols)
    openings = flag * jnp.exp(run)
    closings = jnp.exp(run[BLOCK - 1:BLOCK] - run)
    row_block = pl.ds(pl.multiple_of(at * BLOCK, BLOCK), BLOCK)

    def inputs(columns):
        x = x_ref[:, columns].astype(F32)
        before = jnp.where(at == 0, rim_ref[8:16, columns].astype(F32), prev_ref[8:16, columns].astype(F32)) * flag
        return x, before, conv_rows(x, before, taps_ref[:, columns])

    def conv_back(columns, x, before, grad):
        taps = taps_ref[:, columns]
        later = after_ref[:, columns]
        longer = jnp.concatenate([grad, later], axis=0)
        gx = taps[taps_count - 1:taps_count] * grad
        sums = [jnp.sum(grad * x, axis=0, keepdims=True)]
        for back in range(1, taps_count):
            gx = gx + taps[taps_count - 1 - back:taps_count - back] * longer[back:back + BLOCK]
            sums.append(jnp.sum(grad * shifted(x, before, back), axis=0, keepdims=True))
        gx_ref[row_block, columns] = gx.astype(BF)
        gtaps_ref[:, columns] += jnp.concatenate(sums[::-1], axis=0)
        after_ref[:, columns] = grad[:8] * flag

    grad_runs, grad_betas = [], []
    for h in range(heads):
        qs, ks, vs = head_slices(heads, h)
        xq, bq, cq = inputs(qs)
        xk, bk, ck = inputs(ks)
        xv, bv, cv = inputs(vs)
        aq, ak = cq * jax.nn.sigmoid(cq), ck * jax.nn.sigmoid(ck)
        rq, rk_unit = unit_factor(aq), unit_factor(ak)
        uq, uk = aq * rq, ak * rk_unit
        q, k = (uq * DK ** (-0.5)).astype(BF), uk.astype(BF)
        v = (cv * jax.nn.sigmoid(cv)).astype(BF)
        qf, kf, vf = q.astype(F32), k.astype(F32), v.astype(F32)
        beta, opening, closing = betas[:, h:h + 1], openings[:, h:h + 1], closings[:, h:h + 1]
        gamma = opening[BLOCK - 1:BLOCK]
        table = block_tables(run[:, h:h + 1], run_row[h:h + 1, :], rows, cols)
        kk = mm_nt(k, k)
        scores = mm_nt(q, k) * table
        low_t = t_ref[0, h]
        u = mm(low_t, beta * vf)
        w = mm(low_t, (beta * opening) * kf)
        low_w = w.astype(BF)
        state = z_ref[0, h, :, :DV].astype(F32) + mm(z_ref[0, h, :, DV:], s_ref[h])
        low_s = state.astype(BF)
        c = u - mm(low_w, low_s)
        low_c = c.astype(BF)
        go = go_ref[:, h * DV:(h + 1) * DV]
        g = carry[h]
        low_g = g.astype(BF)
        low_ck = (closing * kf).astype(BF)
        low_oq = (opening * qf).astype(BF)
        dc = mm_tn(scores, go) + mm(low_ck, low_g)
        low_dc = dc.astype(BF)
        both = jnp.concatenate([go, low_dc], axis=0)
        carry[h] = gamma * g + mm_tn(jnp.concatenate([low_oq, -low_w], axis=0), both)
        dkeyed = mm_nt(low_c, low_g)
        dgamma = jnp.sum(jnp.sum(state * g, axis=1, keepdims=True), axis=0, keepdims=True)
        dscore = jnp.where(rows >= cols, mm_nt(go, low_c), 0.0)
        back = mm_nt(both, low_s)
        doq, dw = back[:BLOCK], -back[BLOCK:]
        drv = mm_tn(low_t, low_dc)
        drw = mm_tn(low_t, dw)
        low_drv, low_drw = drv.astype(BF), drw.astype(BF)
        da = jnp.where(rows > cols, -(mm_nt(low_drv, u) + mm_nt(low_drw, low_w)), 0.0)
        dat = da * table
        dkk = (beta * dat).astype(BF)
        dqk = (dscore * table).astype(BF)
        gq = (opening * doq + mm(dqk, k)) * DK ** (-0.5)
        gk = mm_tn(dqk, q) + mm(dkk, k) + mm_tn(dkk, k) + closing * dkeyed + (beta * opening) * drw
        gq = rq * (gq - uq * jnp.sum(gq * uq, axis=1, keepdims=True))
        gk = rk_unit * (gk - uk * jnp.sum(gk * uk, axis=1, keepdims=True))
        conv_back(qs, xq, bq, silu_back(cq, gq))
        conv_back(ks, xk, bk, silu_back(ck, gk))
        conv_back(vs, xv, bv, silu_back(cv, beta * drv))
        rk = jnp.sum(drw * kf, axis=1, keepdims=True)
        atk = dat * kk
        grad_betas.append(jnp.sum(drv * vf, axis=1, keepdims=True) + opening * rk + jnp.sum(atk, axis=1, keepdims=True))
        dopen = opening * (jnp.sum(doq * qf, axis=1, keepdims=True) + beta * rk)
        dclose = closing * jnp.sum(dkeyed * kf, axis=1, keepdims=True)
        e = dscore * scores + beta * atk
        by_col = exact_tn(e, jnp.ones((BLOCK, 8), F32))[:, :1]
        dg = jnp.sum(e, axis=1, keepdims=True) - by_col + dopen - dclose
        grad_runs.append(dg + jnp.where(last, jnp.sum(dclose, axis=0, keepdims=True) + dgamma * gamma, 0.0))

    lane = lax.broadcasted_iota(jnp.int32, (BLOCK, heads), 1)
    grad_run = sum(jnp.where(lane == h, grad_runs[h], 0.0) for h in range(heads))
    grad_beta = sum(jnp.where(lane == h, grad_betas[h], 0.0) for h in range(heads))
    grad_log = exact_tn(jnp.where(cols <= rows, 1.0, 0.0), grad_run)
    grad_biased = grad_log * speed * jax.nn.sigmoid(biased)
    gsmall_ref[:, :heads] = grad_biased
    gsmall_ref[:, heads:] = grad_beta * live * sig * (1.0 - sig)
    gscalar_ref[0:1, :] += jnp.sum(grad_log * log_decay, axis=0, keepdims=True)
    gscalar_ref[1:2, :] += jnp.sum(grad_biased, axis=0, keepdims=True)

    @pl.when(step == nb - 1)
    def _():
        longer = jnp.concatenate([jnp.zeros((16, taps_ref.shape[1]), F32), after_ref[...]], axis=0)
        gx = jnp.zeros((16, taps_ref.shape[1]), F32)
        for back in range(1, taps_count):
            gx = gx + taps_ref[taps_count - 1 - back:taps_count - back, :] * longer[back:back + 16]
        gx_ref[pl.ds(nb * BLOCK, 16), :] = gx.astype(BF)


MESH = pl.DeviceIdType.MESH


def position():
    w = lax.axis_index("wide")
    return w, w // 2, w % 2, lax.axis_index("narrow")


def greet(line=0, pair=False, cube=False, bits=(), places=0, rim=False):
    w, place, side, n = position()
    barrier = pltpu.get_barrier_semaphore()

    def signal(*device):
        pl.semaphore_signal(barrier, inc=1, device_id=device, device_id_type=MESH)

    count = 0
    if pair:
        signal(w + 1 - 2 * side, n)
        count += 1
    if cube:
        signal(w, n ^ 1)
        signal(w, n ^ 2)
        count += 2
    for bit in bits:
        signal(w ^ bit, n)
        count += 1
    if line:
        @pl.when(place > 0)
        def _():
            signal(w - 2, n)

        @pl.when(place < line - 1)
        def _():
            signal(w + 2, n)

        count = count + jnp.where(place > 0, 1, 0) + jnp.where(place < line - 1, 1, 0)
    if rim:
        @pl.when((side == 0) & (place > 0))
        def _():
            signal(w - 1, n)

        @pl.when((side == 1) & (place < line - 1))
        def _():
            signal(w + 1, n)

        count = count + jnp.where(side == 0, jnp.where(place > 0, 1, 0), jnp.where(place < line - 1, 1, 0))
    for k in range(1, places):
        for there in (place + k, place - k):
            @pl.when((there >= 0) & (there < places))
            def _():
                signal(2 * there + side, n)

    pl.semaphore_wait(barrier, count + max(places - 1, 0))


def row_cuts(rows, chunks):
    units = rows // 16
    chunks = min(chunks, units)
    edges = [16 * (units * c // chunks) for c in range(chunks + 1)]
    return [(edges[c], edges[c + 1] - edges[c]) for c in range(chunks)]


class LineGather:
    def __init__(self, places, cuts, sources, others, targets, local_sems, send_sems, recv_sems):
        self.places, self.sources, self.others, self.targets = places, sources, others, targets
        self.local_sems, self.send_sems, self.recv_sems = local_sems, send_sems, recv_sems
        self.w, self.place, self.side, self.n = position()
        self.items = [(i,) + cut for i, found in enumerate(cuts) for cut in found]

    def both(self, item):
        return self.others[self.items[item][0]] is not None

    def copy(self, item, slot, way, own=False):
        i, start, size = self.items[item]
        rows = pl.ds(start, size)
        source = self.targets[i].at[slot, rows]
        if own:
            source = (self.others if way == 0 and self.both(item) else self.sources)[i].at[rows]
        device = [self.w + 1 - 2 * self.side, self.w + 2, self.w - 2][way]
        return pltpu.make_async_remote_copy(
            src_ref=source, dst_ref=self.targets[i].at[slot, rows], send_sem=self.send_sems.at[way, slot, item],
            recv_sem=self.recv_sems.at[slot, item], device_id=(device, self.n), device_id_type=MESH)

    def start(self):
        for i, source in enumerate(self.sources):
            pltpu.make_async_copy(source, self.targets[i].at[self.w], self.local_sems.at[i]).start()
        for item in range(len(self.items)):
            self.copy(item, self.w, 0, True).start()
            self.along(item, self.w, 1, True)
            self.along(item, self.w, 2, True)

    def along(self, item, slot, way, own=False):
        @pl.when(self.place < self.places - 1 if way == 1 else self.place > 0)
        def _():
            self.copy(item, slot, way, own).start()

    def events(self):
        items = range(len(self.items))
        found = [(item, 0, 1) for item in items if self.both(item)]
        return found + [(item, t, s) for t in range(1, self.places) for item in items
                        for s in ((0, 1) if self.both(item) else (0,))]

    def run(self, event):
        item, t, s = event
        if t == 0:
            slot = self.w + 1 - 2 * self.side
            self.copy(item, slot, 0).wait_recv()
            self.along(item, slot, 1)
            self.along(item, slot, 2)
            return

        for way, there in ((1, self.place - t), (2, self.place + t)):
            slot = 2 * there + (self.side if s == 0 else 1 - self.side)

            @pl.when((there >= 0) & (there < self.places))
            def _():
                self.copy(item, slot, way).wait_recv()
                self.along(item, slot, way)
                if not self.both(item):
                    self.copy(item, slot, 0).start()

    def finish(self):
        for item in range(len(self.items)):
            if not self.both(item):
                for t in range(self.places):
                    self.copy(item, 2 * t + 1 - self.side, 0).wait_recv()
        for i, source in enumerate(self.sources):
            pltpu.make_async_copy(source, self.targets[i].at[self.w], self.local_sems.at[i]).wait()
        for item in range(len(self.items)):
            both = self.both(item)
            if both:
                self.copy(item, self.w, 0, True).wait_send()
            for t in range(self.places):
                if not both:
                    self.copy(item, 2 * t + self.side, 0).wait_send()
                for s in ((0, 1) if both else (0,)):
                    slot = 2 * t + (self.side if s == 0 else 1 - self.side)

                    @pl.when((self.place < self.places - 1) & (t <= self.place))
                    def _():
                        self.copy(item, slot, 1).wait_send()

                    @pl.when((self.place > 0) & (t >= self.place))
                    def _():
                        self.copy(item, slot, 2).wait_send()

    @staticmethod
    def scratch(count, cuts):
        items = sum(len(found) for found in cuts)
        return [pltpu.SemaphoreType.DMA((len(cuts),)), pltpu.SemaphoreType.DMA((3, count, items)),
                pltpu.SemaphoreType.DMA((count, items))]


class PairRows:
    def __init__(self, places, source, target, rim, send_sems, recv_sems, rim_send, rim_recv):
        self.places, self.source, self.target, self.rim = places, source, target, rim
        self.send_sems, self.recv_sems, self.rim_sems = send_sems, recv_sems, (rim_send, rim_recv)
        self.w, self.place, self.side, self.n = position()

    def copy(self, number, part):
        size = self.target.shape[1]
        device = [(self.w + 1 - 2 * self.side, self.n), (self.w, self.n ^ 2), (self.w, self.n ^ 1), (self.w, self.n ^ 1)][number]
        source = self.source.at[pl.ds(part * size, size)] if number == 0 else self.target.at[part]
        return pltpu.make_async_remote_copy(
            src_ref=source, dst_ref=self.target.at[part], send_sem=self.send_sems.at[number],
            recv_sem=self.recv_sems.at[part], device_id=device, device_id_type=MESH)

    def rim_copy(self, side):
        size = self.rim.shape[0]
        return pltpu.make_async_remote_copy(
            src_ref=self.source.at[pl.ds(self.source.shape[0] - size, size)], dst_ref=self.rim,
            send_sem=self.rim_sems[0].at[side], recv_sem=self.rim_sems[1],
            device_id=(2 * self.place + 2 + side, self.n), device_id_type=MESH)

    def sends_rim(self):
        return (self.side == 1) & (self.place < self.places - 1)

    def start(self):
        self.copy(0, self.n).start()

        @pl.when(self.sends_rim())
        def _():
            self.rim_copy(0).start()
            self.rim_copy(1).start()

    def events(self):
        return [0, 1]

    def run(self, event):
        if event == 0:
            self.copy(0, self.n).wait_recv()
            self.copy(1, self.n).start()
            self.copy(2, self.n).start()
        else:
            self.copy(1, self.n ^ 2).wait_recv()
            self.copy(3, self.n ^ 2).start()

    def finish(self):
        self.copy(2, self.n ^ 1).wait_recv()
        self.copy(3, self.n ^ 3).wait_recv()
        for number in range(4):
            self.copy(number, self.n ^ 2 if number == 3 else self.n).wait_send()

        @pl.when(self.place > 0)
        def _():
            self.rim_copy(0).wait_recv()

        @pl.when(self.sends_rim())
        def _():
            self.rim_copy(0).wait_send()
            self.rim_copy(1).wait_send()


def gather_kernel(places, cuts, halved, rows, *refs):
    m = len(cuts)
    sources, refs = refs[:m], refs[m:]
    others, refs = iter(refs[:sum(halved)]), refs[sum(halved):]
    others = [next(others) if h else None for h in halved]
    rows_in, refs = refs[:rows], refs[rows:]
    targets, rows_out, refs = refs[:m], refs[m:m + 2 * rows], refs[m + 2 * rows:]
    groups = [LineGather(places, cuts, sources, others, targets, *refs[:3])]
    if rows:
        groups.append(PairRows(places, rows_in[0], *rows_out, *refs[3:]))
    greet(line=places, pair=True, cube=bool(rows), rim=bool(rows))
    for group in groups[::-1]:
        group.start()
    for group, event in merged(groups):
        group.run(event)
    for group in groups[::-1]:
        group.finish()


def flat_blocks(gathered):
    return [g.reshape((g.shape[0] * g.shape[1],) + g.shape[2:]) for g in gathered]


def line_gather(values, call_id, chunks=4, rows=None):
    count = lax.axis_size("wide")
    halved = [isinstance(value, tuple) for value in values]
    sources = [value[0] if h else value for value, h in zip(values, halved)]
    others = [value[1] for value, h in zip(values, halved) if h]
    cuts = [row_cuts(value.shape[0], chunks if value.shape[0] > 64 else 1) for value in sources]
    hbm = pl.BlockSpec(memory_space=pl.ANY)
    shapes = [jax.ShapeDtypeStruct((count,) + value.shape, value.dtype) for value in sources]
    scratch = LineGather.scratch(count, cuts)
    if rows is not None:
        narrow = lax.axis_size("narrow")
        others.append(rows)
        shapes.append(jax.ShapeDtypeStruct((narrow, rows.shape[0] // narrow, rows.shape[1]), rows.dtype))
        shapes.append(jax.ShapeDtypeStruct((16, rows.shape[1]), rows.dtype))
        scratch += [pltpu.SemaphoreType.DMA((4,)), pltpu.SemaphoreType.DMA((narrow,)), pltpu.SemaphoreType.DMA((2,)),
                    pltpu.SemaphoreType.DMA]
    found = pl.pallas_call(
        functools.partial(gather_kernel, count // 2, cuts, halved, 0 if rows is None else 1),
        out_shape=shapes,
        in_specs=[hbm] * (len(sources) + len(others)),
        out_specs=[hbm] * len(shapes),
        scratch_shapes=scratch,
        compiler_params=pltpu.CompilerParams(collective_id=call_id, has_side_effects=True),
    )(*sources, *others)
    return flat_blocks(found[:-1]) + [found[-1]] if rows is not None else flat_blocks(found)


class LineScatter:
    def __init__(self, places, cuts, paired, sources, owns, pairs, lines, load_sems, pair_send, pair_recv, right_send,
                 right_recv, left_send, left_recv):
        self.places, self.paired = places, paired
        self.sources, self.owns, self.pairs, self.lines = sources, owns, pairs, lines
        self.load_sems, self.pair_sems = load_sems, (pair_send, pair_recv)
        self.right_sems, self.left_sems = (right_send, right_recv), (left_send, left_recv)
        self.w, self.place, self.side, self.n = position()
        self.items = [(i,) + cut for i, found in enumerate(cuts) for cut in found]
        self.fill = None
        self.order = [(t, item) for j in range(places // 2) for item in range(len(self.items)) for t in (places - 1 - j, j)]

    def remote(self, source, target, sems, t, item, device):
        return pltpu.make_async_remote_copy(src_ref=source, dst_ref=target, send_sem=sems[0].at[t, item],
                                            recv_sem=sems[1].at[t, item], device_id=(device, self.n), device_id_type=MESH)

    def at(self, t, item):
        i, start, size = self.items[item]
        return (t, pl.ds(start, size)) if self.paired else (t, slice(None), pl.ds(start, size))

    def across(self, t, item):
        i = self.items[item][0]
        source = self.sources[i].at[2 * t + 1 - self.side, self.at(t, item)[1]]
        return self.remote(source, self.pairs[i].at[self.at(t, item)], self.pair_sems, t, item, self.w + 1 - 2 * self.side)

    def load(self, t, item):
        i = self.items[item][0]
        slot = 2 * t + self.side if self.paired else t
        return pltpu.make_async_copy(self.sources[i].at[self.at(slot, item)], self.owns[i].at[self.at(t, item)],
                                     self.load_sems.at[t, item])

    def right(self, t, item):
        i, at = self.items[item][0], self.at(t, item)
        return self.remote(self.owns[i].at[at], self.lines[i].at[at], self.right_sems, t, item, self.w + 2)

    def left(self, t, item, arriving=False):
        i, at = self.items[item][0], self.at(t, item)
        slot = jnp.where(t == self.place - (0 if arriving else 1), self.places, t)
        return self.remote(self.owns[i].at[at], self.lines[i].at[(slot,) + at[1:]], self.left_sems, t, item, self.w - 2)

    ahead = 4

    def start(self):
        if self.sources is not None:
            for t, item in self.order:
                self.load(t, item).start()
        if self.paired:
            for t, item in self.order[:self.ahead]:
                self.across(t, item).start()

    def events(self):
        return self.order

    def run(self, event):
        t, item = event
        i, at = self.items[item][0], self.at(t, item)
        own, place, places = self.owns[i], self.place, self.places

        def add(other):
            own[at] = (own[at].astype(F32) + other[at].astype(F32)).astype(own.dtype)

        if self.fill is not None and item == 0:
            self.fill(t)
        if self.sources is not None:
            self.load(t, item).wait()
        if self.paired:
            following = self.order.index(event) + self.ahead
            if following < len(self.order):
                self.across(*self.order[following]).start()
            self.across(t, item).wait_recv()
            add(self.pairs[i])

        @pl.when(t > place)
        def _():
            @pl.when(place > 0)
            def _():
                self.right(t, item).wait_recv()
                add(self.lines[i])

            self.right(t, item).start()

        @pl.when(t < place)
        def _():
            @pl.when(place < places - 1)
            def _():
                self.left(t, item, True).wait_recv()
                add(self.lines[i])

            self.left(t, item).start()

    def finish(self, outs, theirs=None):
        place, copies = self.place, []
        for item in range(len(self.items)):
            i, start, size = self.items[item]
            own, line, at, rows = self.owns[i], self.lines[i], self.at(place, item), pl.ds(start, size)

            @pl.when(place > 0)
            def _():
                self.right(place, item).wait_recv()
                own[at] = (own[at].astype(F32) + line[at].astype(F32)).astype(own.dtype)

            @pl.when(place < self.places - 1)
            def _():
                self.left(place, item, True).wait_recv()
                own[at] = (own[at].astype(F32) + line[(self.places,) + at[1:]].astype(F32)).astype(own.dtype)

            if self.paired:
                outs[i][rows] = own[at].astype(F32)
            else:
                copy = self.remote(own.at[place, 1 - self.side, rows], self.pairs[i].at[rows], self.pair_sems, 0, item,
                                   self.w + 1 - 2 * self.side)
                copy.start()
                copies.append((i, rows, copy))
                outs[i][rows] = own[place, self.side, rows].astype(F32)
        for i, rows, copy in copies:
            copy.wait()
            theirs[i][rows] = self.pairs[i][rows].astype(F32)
        for t in range(self.places):
            for item in range(len(self.items)):
                if self.paired:
                    self.across(t, item).wait_send()

                @pl.when(t > place)
                def _():
                    self.right(t, item).wait_send()

                @pl.when(t < place)
                def _():
                    self.left(t, item).wait_send()

    @staticmethod
    def scratch(places, cuts, paired, values):
        owns = [pltpu.VMEM((places,) + value.shape[1:], value.dtype) for value in values]
        pairs = owns if paired else [pltpu.VMEM(value.shape[2:], value.dtype) for value in values]
        lines = [pltpu.VMEM((places + 1,) + value.shape[1:], value.dtype) for value in values]
        items = sum(len(found) for found in cuts)
        return owns + pairs + lines + [pltpu.SemaphoreType.DMA((places, items))] * 7

    @staticmethod
    def take(places, cuts, paired, sources, refs):
        m = len(cuts)
        amount = 3 * m + 7
        groups = [refs[m * g:m * (g + 1)] for g in range(3)]
        return LineScatter(places, cuts, paired, sources, *groups, *refs[3 * m:amount]), refs[amount:]


class CubeScatter:
    def __init__(self, source, own, near, second, third, load_sems, send_sems, recv_sems):
        self.source, self.own, self.near, self.second, self.third = source, own, near, second, third
        self.load_sems, self.send_sems, self.recv_sems = load_sems, send_sems, recv_sems
        self.w, self.place, self.side, self.n = position()
        self.half = own.shape[2] // 2
        self.order = (3, 1, 2, 0)

    def block(self, s, m):
        return (self.side ^ s) * 4 + (self.n ^ m)

    def remote(self, number, source, target, device):
        return pltpu.make_async_remote_copy(src_ref=source, dst_ref=target, send_sem=self.send_sems.at[number],
                                            recv_sem=self.recv_sems.at[number], device_id=device, device_id_type=MESH)

    def cut(self, part):
        return pl.ds(part * self.half, self.half)

    def first(self, j):
        return self.remote(j, self.source.at[self.block(j // 2, 1 + 2 * (j % 2))], self.near.at[j], (self.w, self.n ^ 1))

    def load(self, j):
        return pltpu.make_async_copy(self.source.at[self.block(j // 2, 2 * (j % 2))], self.own.at[j], self.load_sems.at[j])

    def device(self, part, stage):
        return (self.w, self.n ^ 2) if part == stage else (self.w + 1 - 2 * self.side, self.n)

    def middle(self, part, k):
        j = 2 * k + 1 if part == 0 else 2 + k
        return self.remote(4 + 2 * part + k, self.own.at[j, :, self.cut(part)], self.second.at[part, k], self.device(part, 0))

    def end(self, part):
        j = 2 if part == 0 else 1
        return self.remote(8 + part, self.own.at[j, :, self.cut(part)], self.third.at[part], self.device(part, 1))

    def start(self):
        for j in self.order:
            self.load(j).start()
        for j in self.order:
            self.first(j).start()

    def events(self):
        return [("near", j) for j in self.order] + [("middle", k) for k in (1, 0)]

    def run(self, event):
        kind, j = event
        if kind == "near":
            self.load(j).wait()
            self.first(j).wait_recv()
            self.own[j] = (self.own[j].astype(F32) + self.near[j].astype(F32)).astype(self.own.dtype)
            if j % 2 == 1:
                self.middle(0, j // 2).start()
            if j // 2 == 1:
                self.middle(1, j % 2).start()
            return
        for part in (0, 1):
            self.middle(part, j).wait_recv()
            target = (2 * j if part == 0 else j, slice(None), self.cut(part))
            self.own[target] = (self.own[target].astype(F32) + self.second[part, j].astype(F32)).astype(self.own.dtype)
            if j == 1:
                self.end(part).start()

    def finish(self, out):
        for part in (0, 1):
            self.end(part).wait_recv()
            out[:, self.cut(part)] = self.own[0, :, self.cut(part)].astype(F32) + self.third[part].astype(F32)
        for j in range(4):
            self.first(j).wait_send()
        for part in (0, 1):
            for k in (0, 1):
                self.middle(part, k).wait_send()
            self.end(part).wait_send()

    @staticmethod
    def scratch(value):
        rows, columns = value.shape[1:]
        block = pltpu.VMEM((4, rows, columns), value.dtype)
        return [block, block, pltpu.VMEM((2, 2, rows, columns // 2), value.dtype),
                pltpu.VMEM((2, rows, columns // 2), value.dtype), pltpu.SemaphoreType.DMA((4,)),
                pltpu.SemaphoreType.DMA((10,)), pltpu.SemaphoreType.DMA((10,))]


class NarrowScatter:
    def __init__(self, sources, owns, nears, fars, load_sems, send_sems, recv_sems):
        self.sources, self.owns, self.nears, self.fars = sources, owns, nears, fars
        self.load_sems, self.send_sems, self.recv_sems = load_sems, send_sems, recv_sems
        self.w, self.place, self.side, self.n = position()

    def cut(self, i, m):
        size = self.owns[i].shape[2]
        return self.sources[i].at[:, pl.ds(pl.multiple_of((self.n ^ m) * size, size), size)]

    def remote(self, i, number, source, target, bit):
        return pltpu.make_async_remote_copy(
            src_ref=source, dst_ref=target, send_sem=self.send_sems.at[i, number], recv_sem=self.recv_sems.at[i, number],
            device_id=(self.w, self.n ^ bit), device_id_type=MESH)

    def near(self, i, m):
        return self.remote(i, m, self.cut(i, 1 + 2 * m), self.nears[i].at[m], 1)

    def far(self, i):
        return self.remote(i, 2, self.owns[i].at[1], self.fars[i], 2)

    def load(self, i, m):
        return pltpu.make_async_copy(self.cut(i, 2 * m), self.owns[i].at[m], self.load_sems.at[i, m])

    def start(self):
        for i in range(len(self.owns)):
            for m in (1, 0):
                self.load(i, m).start()
        for i in range(len(self.owns)):
            for m in (1, 0):
                self.near(i, m).start()

    def events(self):
        return [(kind, i) for i in range(len(self.owns)) for kind in ("high", "low")]

    def run(self, event):
        kind, i = event
        m = 1 if kind == "high" else 0
        self.load(i, m).wait()
        self.near(i, m).wait_recv()
        self.owns[i][m] = (self.owns[i][m].astype(F32) + self.nears[i][m].astype(F32)).astype(self.owns[i].dtype)
        if m == 1:
            self.far(i).start()

    def finish(self, outs):
        for i, out in enumerate(outs):
            self.far(i).wait_recv()
            out[...] = self.owns[i][0].astype(F32) + self.fars[i][...].astype(F32)
            for m in (0, 1):
                self.near(i, m).wait_send()
            self.far(i).wait_send()

    @staticmethod
    def scratch(values, narrow):
        shapes = [(value.shape[0], value.shape[1] // narrow) for value in values]
        pairs = [pltpu.VMEM((2,) + shape, value.dtype) for shape, value in zip(shapes, values)]
        m = len(values)
        return (pairs * 2 + [pltpu.VMEM(shape, value.dtype) for shape, value in zip(shapes, values)]
                + [pltpu.SemaphoreType.DMA((m, 2)), pltpu.SemaphoreType.DMA((m, 3)), pltpu.SemaphoreType.DMA((m, 3))])

    @staticmethod
    def take(sources, refs):
        m = len(sources)
        amount = 3 * m + 3
        return NarrowScatter(sources, refs[:m], refs[m:2 * m], refs[2 * m:3 * m], *refs[3 * m:amount]), refs[amount:]


def cube_scatter_kernel(x_ref, o_ref, *refs):
    cube = CubeScatter(x_ref, *refs)
    greet(pair=True, cube=True)
    cube.start()
    for event in cube.events():
        cube.run(event)
    cube.finish(o_ref)


def cube_scatter(value, call_id):
    return pl.pallas_call(
        cube_scatter_kernel,
        out_shape=jax.ShapeDtypeStruct(value.shape[1:], F32),
        in_specs=[pl.BlockSpec(memory_space=pl.ANY)],
        out_specs=pl.BlockSpec(memory_space=pltpu.VMEM),
        scratch_shapes=CubeScatter.scratch(value),
        compiler_params=pltpu.CompilerParams(collective_id=call_id, has_side_effects=True, vmem_limit_bytes=32 * 2**20),
    )(value)


def cube_gather_kernel(x_ref, o_ref, local_sem, send_sems, recv_sems):
    w, place, side, n = position()
    half = x_ref.shape[1] // 2
    devices = [(w + 1 - 2 * side, n), (w, n ^ 2), (w, n ^ 1)]

    def copy(s, m, part, way, own=False):
        slot = (side ^ s) * 4 + (n ^ m)
        columns = pl.ds(part * half, half)
        source = x_ref.at[:, columns] if own else o_ref.at[slot, :, columns]
        return pltpu.make_async_remote_copy(
            src_ref=source, dst_ref=o_ref.at[slot, :, columns], send_sem=send_sems.at[way, slot, part],
            recv_sem=recv_sems.at[slot, part], device_id=devices[way], device_id_type=MESH)

    greet(pair=True, cube=True)
    local = pltpu.make_async_copy(x_ref, o_ref.at[side * 4 + n], local_sem)
    local.start()
    sent = []

    def send(s, m, part, way, own=False):
        found = copy(s, m, part, way, own)
        found.start()
        sent.append(found)

    for way in (0, 1, 2):
        for part in (0, 1):
            send(0, 0, part, way, True)
    copy(1, 0, 0, 0).wait_recv()
    send(1, 0, 0, 1)
    copy(0, 2, 1, 1).wait_recv()
    send(0, 2, 1, 0)
    send(1, 0, 0, 2)
    send(0, 2, 1, 2)
    copy(0, 2, 0, 1).wait_recv()
    send(0, 2, 0, 2)
    copy(1, 0, 1, 0).wait_recv()
    send(1, 0, 1, 2)
    copy(1, 2, 0, 1).wait_recv()
    send(1, 2, 0, 2)
    copy(1, 2, 1, 0).wait_recv()
    send(1, 2, 1, 2)
    for s in (0, 1):
        for m in (1, 3):
            for part in (0, 1):
                copy(s, m, part, 2).wait_recv()
    local.wait()
    for found in sent:
        found.wait_send()


def cube_gather(value, call_id):
    return pl.pallas_call(
        cube_gather_kernel,
        out_shape=jax.ShapeDtypeStruct((8,) + value.shape, value.dtype),
        in_specs=[pl.BlockSpec(memory_space=pltpu.VMEM)],
        out_specs=pl.BlockSpec(memory_space=pl.ANY),
        scratch_shapes=[pltpu.SemaphoreType.DMA, pltpu.SemaphoreType.DMA((3, 8, 2)), pltpu.SemaphoreType.DMA((8, 2))],
        compiler_params=pltpu.CompilerParams(collective_id=call_id, has_side_effects=True, vmem_limit_bytes=16 * 2**20),
    )(value).reshape(8 * value.shape[0], value.shape[1])


class SmallSums:
    def __init__(self, steps, value, stages, inbox, cube, place_send, place_recv, cube_send, cube_recv):
        self.steps, self.value, self.stages, self.inbox, self.cube = steps, value, stages, inbox, cube
        self.place_sems, self.cube_sems = (place_send, place_recv), (cube_send, cube_recv)
        self.w, self.place, self.side, self.n = position()

    def step(self, i):
        return pltpu.make_async_remote_copy(
            src_ref=self.stages.at[i], dst_ref=self.inbox.at[i], send_sem=self.place_sems[0].at[i],
            recv_sem=self.place_sems[1].at[i], device_id=(self.w ^ (2 << i), self.n), device_id_type=MESH)

    def spread(self, way, s, m):
        slot = (self.side ^ s) * 4 + (self.n ^ m)
        device = [(self.w + 1 - 2 * self.side, self.n), (self.w, self.n ^ 2), (self.w, self.n ^ 1)][way]
        return pltpu.make_async_remote_copy(
            src_ref=self.cube.at[slot], dst_ref=self.cube.at[slot], send_sem=self.cube_sems[0].at[way, slot],
            recv_sem=self.cube_sems[1].at[slot], device_id=device, device_id_type=MESH)

    sent = {0: [(0, 0)], 1: [(0, 0), (1, 0)], 2: [(0, 0), (1, 0), (0, 2), (1, 2)]}
    arriving = {0: [(1, 0)], 1: [(0, 2), (1, 2)], 2: [(0, 1), (1, 1), (0, 3), (1, 3)]}

    def send(self, way):
        for s, m in self.sent[way]:
            self.spread(way, s, m).start()

    def start(self):
        self.stages[0] = self.value[...]
        self.step(0).start()

    def events(self):
        return [("place", i) for i in range(self.steps)] + [("cube", way) for way in range(3)]

    def run(self, event):
        kind, i = event
        if kind == "place":
            self.step(i).wait_recv()
            self.stages[i + 1] = self.stages[i] + self.inbox[i]
            if i + 1 < self.steps:
                self.step(i + 1).start()
            else:
                self.cube[self.side * 4 + self.n] = self.stages[i + 1]
                self.send(0)
            return
        for s, m in self.arriving[i]:
            self.spread(i, s, m).wait_recv()
        if i < 2:
            self.send(i + 1)

    def finish(self, out):
        out[...] = self.cube[...]
        for i in range(self.steps):
            self.step(i).wait_send()
        for way in range(3):
            for s, m in self.sent[way]:
                self.spread(way, s, m).wait_send()

    @staticmethod
    def scratch(steps, value):
        rows = pltpu.VMEM((steps + 1,) + value.shape, value.dtype)
        return [rows, rows, pltpu.VMEM((8,) + value.shape, value.dtype), pltpu.SemaphoreType.DMA((steps,)),
                pltpu.SemaphoreType.DMA((steps,)), pltpu.SemaphoreType.DMA((3, 8)), pltpu.SemaphoreType.DMA((8,))]


class Products:
    def __init__(self, scatter, operands, buffers, sems):
        self.scatter, self.buffers = scatter, buffers
        self.loads = [pltpu.make_async_copy(source, target, sems.at[i])
                      for i, (source, target) in enumerate(zip(operands, buffers))]
        scatter.fill = self.fill

    def start(self):
        for load in self.loads:
            load.start()

    def wait(self):
        for load in self.loads:
            load.wait()

    def fill(self, t):
        for i, own in enumerate(self.scatter.owns):
            left, right = self.buffers[2 * i], self.buffers[2 * i + 1]
            depth = 2 * own.shape[2]
            term = mm_tn(left[:right.shape[0], t * depth:(t + 1) * depth], right[...]).astype(own.dtype)
            own[t] = term.reshape(own.shape[1:])

    @staticmethod
    def scratch(operands):
        return [pltpu.VMEM(a.shape, a.dtype) for a in operands] + [pltpu.SemaphoreType.DMA((len(operands),))]


def product_terms(products, places):
    terms = [jax.ShapeDtypeStruct((places, 2, left.shape[1] // (2 * places), right.shape[1]), BF) for left, right in products]
    return terms, [a for product in products for a in product]


def place_bits(places):
    return [2 << i for i in range(places.bit_length() - 1)]


def scatter_kernel(places, half_cuts, pair_cuts, cubes, small, narrow, *refs):
    hm, pm = len(half_cuts), len(pair_cuts)

    def take(count):
        nonlocal refs
        found, refs = refs[:count], refs[count:]
        return found

    operands, pairs, cube_in, small_in = take(2 * hm), take(pm), take(cubes), take(small)
    half_outs, half_theirs, pair_outs, cube_outs, small_outs = take(hm), take(hm), take(pm), take(cubes), take(small)
    groups, ends = [], []
    if hm:
        buffers, product_sems = take(2 * hm), take(1)[0]
        half, refs = LineScatter.take(places, half_cuts, False, None, refs)
        products = Products(half, operands, buffers, product_sems)
        products.start()
        groups.append(half)
        ends.append(lambda: half.finish(half_outs, half_theirs))
    if pm:
        pair, refs = LineScatter.take(places, pair_cuts, True, pairs, refs)
        groups.append(pair)
        ends.append(lambda: pair.finish(pair_outs))
    for source, out in zip(cube_in, cube_outs):
        cube = CubeScatter(source, *take(7))
        groups.append(cube)
        ends.append(lambda cube=cube, out=out: cube.finish(out))
    if small:
        sums = SmallSums(len(place_bits(places)), small_in[0], *take(7))
        groups.append(sums)
        ends.append(lambda: sums.finish(small_outs[0]))
    greet(line=places, pair=True, cube=bool(cubes), bits=place_bits(places) if small else ())
    for group in groups[::-1]:
        group.start()
    if hm:
        products.wait()
    for group, event in merged(groups):
        group.run(event)
    for end in ends[:0:-1]:
        end()
    if cubes == 2:
        w, place, side, n = position()
        rim_in, rim_send, rim_recv = take(3)
        rim = pltpu.make_async_remote_copy(src_ref=cube_outs[1], dst_ref=rim_in, send_sem=rim_send, recv_sem=rim_recv,
                                           device_id=(w - 2, n), device_id_type=MESH)
        last = (side == 1) & (n == narrow - 1)

        @pl.when(last & (place > 0))
        def _():
            rim.start()

        @pl.when(last & (place < places - 1))
        def _():
            rim.wait_recv()
            rows = pl.ds(cube_outs[0].shape[0] - rim_in.shape[0], rim_in.shape[0])
            cube_outs[0][rows] = cube_outs[0][rows] + rim_in[...]

        @pl.when(last & (place > 0))
        def _():
            rim.wait_send()
    ends[0]()


def merged(groups):
    found = []
    for order, group in enumerate(groups):
        events = group.events()
        found += [((i + 0.5) / len(events), order, i, group, event) for i, event in enumerate(events)]
    return [(group, event) for _, _, _, group, event in sorted(found, key=lambda e: e[:3])]


def line_scatter(halves, pairs, cubes, small, call_id, chunks=2):
    places = lax.axis_size("wide") // 2
    halves, operands = product_terms(halves, places)
    half_cuts = [row_cuts(term.shape[2], chunks) for term in halves]
    pair_cuts = [row_cuts(term.shape[1], chunks if term.shape[1] > 64 else 1) for term in pairs]
    shapes = [term.shape[2:] for term in halves] * 2 + [term.shape[1:] for term in list(pairs) + list(cubes)]
    shapes += [(8,) + term.shape for term in small]
    scratch = []
    if halves:
        scratch += Products.scratch(operands) + LineScatter.scratch(places, half_cuts, False, halves)
    if pairs:
        scratch += LineScatter.scratch(places, pair_cuts, True, pairs)
    for term in cubes:
        scratch += CubeScatter.scratch(term)
    for term in small:
        scratch += SmallSums.scratch(len(place_bits(places)), term)
    if cubes:
        scratch += [pltpu.VMEM(cubes[1].shape[1:], F32), pltpu.SemaphoreType.DMA, pltpu.SemaphoreType.DMA]
    vmem = pl.BlockSpec(memory_space=pltpu.VMEM)
    found = pl.pallas_call(
        functools.partial(scatter_kernel, places, half_cuts, pair_cuts, len(cubes), len(small), lax.axis_size("narrow")),
        out_shape=[jax.ShapeDtypeStruct(shape, F32) for shape in shapes],
        in_specs=[pl.BlockSpec(memory_space=pl.ANY)] * (len(operands) + len(pairs) + len(cubes)) + [vmem] * len(small),
        out_specs=[vmem] * len(shapes),
        scratch_shapes=scratch,
        compiler_params=pltpu.CompilerParams(collective_id=call_id, has_side_effects=True, vmem_limit_bytes=60 * 2**20),
    )(*operands, *pairs, *cubes, *small)
    h, p, c = len(halves), len(pairs), len(cubes)
    return list(zip(found[:h], found[h:2 * h])), found[2 * h:2 * h + p], found[2 * h + p:2 * h + p + c], found[2 * h + p + c:]


class PassStates:
    def __init__(self, places, forward, mine, turned, total, send_sems, recv_sems):
        self.places, self.forward, self.ahead = places, forward, 1 if forward else -1
        self.mine, self.turned, self.total = mine, turned, total
        self.send_sems, self.recv_sems = send_sems, recv_sems
        self.w, self.place, self.side, self.n = position()

    def copy(self, k):
        return pltpu.make_async_remote_copy(
            src_ref=self.mine, dst_ref=self.turned.at[k], send_sem=self.send_sems.at[k], recv_sem=self.recv_sems.at[k],
            device_id=(self.w + 2 * self.ahead * k, self.n), device_id_type=MESH)

    def inside(self, there):
        return (there >= 0) & (there < self.places)

    def start(self, state, maps):
        self.mine[:, :, :DV] = state.astype(BF)
        self.mine[:, :, DV:] = maps.astype(BF)
        for k in range(1, self.places):
            @pl.when(self.inside(self.place + self.ahead * k))
            def _():
                self.copy(k).start()

    def finish(self, out):
        total, turned = self.total, self.turned
        total[...] = jnp.zeros_like(total)
        for k in range(self.places - 1, 0, -1):
            @pl.when(self.inside(self.place - self.ahead * k))
            def _():
                self.copy(k).wait_recv()
                for h in range(total.shape[0]):
                    apply = mm if self.forward else mm_tn
                    total[h] = apply(turned[k, h, :, DV:], total[h]) + turned[k, h, :, :DV].astype(F32)

        out[...] = total[...].astype(out.dtype)
        for k in range(1, self.places):
            @pl.when(self.inside(self.place + self.ahead * k))
            def _():
                self.copy(k).wait_send()

    @staticmethod
    def scratch(places, heads):
        return [pltpu.VMEM((heads, DK, DV + DK), BF), pltpu.VMEM((places, heads, DK, DV + DK), BF),
                pltpu.VMEM((heads, DK, DV), F32), pltpu.SemaphoreType.DMA((places,)), pltpu.SemaphoreType.DMA((places,))]


def forward_gather_kernel(heads, nb, places, cuts, halved, *refs):
    m = len(cuts)
    inputs, sources, refs = refs[:8], refs[8:8 + m], refs[8 + m:]
    others, refs = iter(refs[:sum(halved)]), refs[sum(halved):]
    others = [next(others) if h else None for h in halved]
    outs, entry_ref, targets, refs = refs[:5], refs[5], refs[6:6 + m], refs[6 + m:]
    gather = LineGather(places, cuts, sources, others, targets, *refs[2:5])
    states = PassStates(places, True, *refs[5:])
    step = pl.program_id(0)

    @pl.when(step == 0)
    def _():
        greet(line=places, pair=True, places=places)
        gather.start()

    forward_kernel(heads, *inputs, *outs, *refs[:2])
    events = gather.events()
    early = min(len(events) // 2, nb)
    for i in range(nb):
        @pl.when(step == i)
        def _():
            for event in events[early * i // nb:early * (i + 1) // nb]:
                gather.run(event)

    @pl.when(step == nb - 1)
    def _():
        states.start(outs[4][:, :, :DV], outs[4][:, :, DV:])
        for event in events[early:(early + len(events)) // 2]:
            gather.run(event)
        states.finish(entry_ref)
        for event in events[(early + len(events)) // 2:]:
            gather.run(event)
        gather.finish()


def forward_gather(flags, mixed, taps, small, live, a_log, dt_bias, heads, blocks, call_id, chunks=2):
    rows, width = live.shape[0], mixed.shape[1]
    nb = rows // BLOCK
    count = lax.axis_size("wide")
    halved = [isinstance(block, tuple) for block in blocks]
    others = [b[1] for b, h in zip(blocks, halved) if h]
    blocks = [b[0] if h else b for b, h in zip(blocks, halved)]
    cuts = [row_cuts(block.shape[0], chunks) for block in blocks]
    row = lambda width: pl.BlockSpec((BLOCK, width), lambda i: (i, 0))
    same = lambda *shape: pl.BlockSpec(shape, lambda i: (0,) * len(shape))
    hbm = pl.BlockSpec(memory_space=pl.ANY)
    found = pl.pallas_call(
        functools.partial(forward_gather_kernel, heads, nb, count // 2, cuts, halved),
        grid=(nb,),
        in_specs=[pl.BlockSpec(memory_space=pltpu.SMEM), row(width), pl.BlockSpec((16, width), lambda i: (rows // 16, 0)),
                  same(*taps.shape), row(small.shape[1]), row(1), same(1, heads), same(1, heads)]
                 + [hbm] * (len(blocks) + len(others)),
        out_specs=[row(heads * DV), row(heads * DK),
                   pl.BlockSpec((1, heads, BLOCK, BLOCK), lambda i: (i, 0, 0, 0)),
                   pl.BlockSpec((1, heads, DK, DV + DK), lambda i: (i, 0, 0, 0)),
                   same(heads, DK, DV + DK), same(heads, DK, DV)] + [hbm] * len(blocks),
        out_shape=[jax.ShapeDtypeStruct((rows, heads * DV), F32), jax.ShapeDtypeStruct((rows, heads * DK), BF),
                   jax.ShapeDtypeStruct((nb, heads, BLOCK, BLOCK), BF),
                   jax.ShapeDtypeStruct((nb, heads, DK, DV + DK), BF),
                   jax.ShapeDtypeStruct((heads, DK, DV + DK), F32), jax.ShapeDtypeStruct((heads, DK, DV), BF)]
                  + [jax.ShapeDtypeStruct((count,) + block.shape, block.dtype) for block in blocks],
        scratch_shapes=[pltpu.VMEM((heads, DK, DV + DK), F32), pltpu.VMEM((8, width), F32)]
                       + LineGather.scratch(count, cuts) + PassStates.scratch(count // 2, heads),
        compiler_params=pltpu.CompilerParams(collective_id=call_id, has_side_effects=True, vmem_limit_bytes=48 * 2**20),
    )(flags, mixed, mixed, taps, small, live, a_log, dt_bias, *blocks, *others)
    return found[:6], flat_blocks(found[6:])


def backward_scatter_kernel(heads, nb, places, half_cuts, pair_cuts, shares, *refs):
    hm, pm = len(half_cuts), len(pair_cuts)

    def take(count):
        nonlocal refs
        found, refs = refs[:count], refs[count:]
        return found

    inputs, operands, pairs, share_in = tuple(take(15)), take(2 * hm), take(pm), take(shares)
    outs, half_outs, half_theirs, pair_outs, share_outs = take(4), take(hm), take(hm), take(pm), take(shares)
    scratch = take(2)
    states, exit_ref = PassStates(places, False, *take(5)), take(1)[0]
    direct_ref, end_ref = inputs[-2:]
    inputs = inputs[:-2] + (exit_ref,)
    buffers, product_sems = take(2 * hm), take(1)[0]
    half, refs = LineScatter.take(places, half_cuts, False, None, refs)
    products = Products(half, operands, buffers, product_sems)
    groups = [half]
    if pm:
        pair, refs = LineScatter.take(places, pair_cuts, True, pairs, refs)
        groups.append(pair)
    share, refs = NarrowScatter.take(share_in, refs)
    groups.append(share)
    step = pl.program_id(0)

    @pl.when(step == 0)
    def _():
        products.start()
        greet(line=places, pair=True, cube=True, places=places)
        states.start(direct_ref[...], end_ref[:, :, DV:])
        for group in groups:
            group.start()
        states.finish(exit_ref)
        products.wait()

    backward_kernel(heads, *inputs, *outs, *scratch)
    events = merged(groups)
    for i in range(nb):
        @pl.when(step == i)
        def _():
            for group, event in events[len(events) * i // nb:len(events) * (i + 1) // nb]:
                group.run(event)

    @pl.when(step == nb - 1)
    def _():
        share.finish(share_outs)
        if pm:
            pair.finish(pair_outs)
        half.finish(half_outs, half_theirs)


def backward_scatter(flags, mixed, taps, small, live, a_log, dt_bias, t, z, go, entry, direct, end, heads, halves, pairs, shares, call_id,
                     chunks=2):
    rows, width = live.shape[0], mixed.shape[1]
    nb = rows // BLOCK
    places = lax.axis_size("wide") // 2
    halves, operands = product_terms(halves, places)
    half_cuts = [row_cuts(term.shape[2], chunks) for term in halves]
    pair_cuts = [row_cuts(term.shape[1], chunks) for term in pairs]
    h = len(halves)
    narrow = lax.axis_size("narrow")
    sums = [term.shape[2:] for term in halves] * 2 + [term.shape[1:] for term in pairs]
    sums += [(term.shape[0], term.shape[1] // narrow) for term in shares]
    row = lambda width: pl.BlockSpec((BLOCK, width), lambda i: (nb - 1 - i, 0))
    same = lambda *shape: pl.BlockSpec(shape, lambda i: (0,) * len(shape))
    prev = pl.BlockSpec((16, width), lambda i: (jnp.maximum((nb - 1 - i) * (BLOCK // 16) - 1, 0), 0))
    found = pl.pallas_call(
        functools.partial(backward_scatter_kernel, heads, nb, places, half_cuts, pair_cuts, len(shares)),
        grid=(nb,),
        in_specs=[pl.BlockSpec(memory_space=pltpu.SMEM), row(width), prev,
                  pl.BlockSpec((16, width), lambda i: (rows // 16, 0)), same(*taps.shape), row(small.shape[1]), row(1),
                  same(1, heads), same(1, heads),
                  pl.BlockSpec((1, heads, BLOCK, BLOCK), lambda i: (nb - 1 - i, 0, 0, 0)),
                  pl.BlockSpec((1, heads, DK, DV + DK), lambda i: (nb - 1 - i, 0, 0, 0)),
                  row(heads * DV), same(heads, DK, DV), same(heads, DK, DV), same(heads, DK, DV + DK)]
                 + [pl.BlockSpec(memory_space=pl.ANY)] * (len(operands) + len(pairs) + len(shares)),
        out_specs=[same(rows + 16, width), row(2 * heads), same(*taps.shape), same(8, heads)]
                  + [pl.BlockSpec(shape, lambda i: (0, 0), pipeline_mode=pl.Buffered(1)) for shape in sums],
        out_shape=[jax.ShapeDtypeStruct((rows + 16, width), BF), jax.ShapeDtypeStruct((rows, 2 * heads), F32),
                   jax.ShapeDtypeStruct(taps.shape, F32), jax.ShapeDtypeStruct((8, heads), F32)]
                  + [jax.ShapeDtypeStruct(shape, F32) for shape in sums],
        scratch_shapes=[pltpu.VMEM((heads, DK, DV), F32), pltpu.VMEM((8, width), F32)]
                       + PassStates.scratch(places, heads) + [pltpu.VMEM((heads, DK, DV), F32)]
                       + Products.scratch(operands) + LineScatter.scratch(places, half_cuts, False, halves)
                       + (LineScatter.scratch(places, pair_cuts, True, pairs) if pairs else [])
                       + NarrowScatter.scratch(shares, narrow),
        compiler_params=pltpu.CompilerParams(collective_id=call_id, has_side_effects=True, vmem_limit_bytes=60 * 2**20),
    )(flags, mixed, mixed, mixed, taps, small, live, a_log, dt_bias, t, z, go, entry, direct, end, *operands, *pairs, *shares)
    p = len(pairs)
    return (found[:4], list(zip(found[4:4 + h], found[4 + h:4 + 2 * h])), found[4 + 2 * h:4 + 2 * h + p],
            found[4 + 2 * h + p:])


TILE = 256


def place_rows(side_ref, own_ref, their_ref):
    return jnp.where(pl.program_id(0) // (pl.num_programs(0) // 2) == side_ref[0], own_ref[...], their_ref[...]).astype(F32)


def project_kernel(side_ref, own_ref, their_ref, rim_ref, gain_ref, w_ref, sw_ref, normed_ref, mixed_ref, small_ref):
    step = pl.program_id(0)

    def normal(x):
        return (x * lax.rsqrt(jnp.mean(x * x, axis=1, keepdims=True) + EPS) * gain_ref[...]).astype(BF)

    @pl.when(step < pl.num_programs(0) - 1)
    def _():
        normed = normal(place_rows(side_ref, own_ref, their_ref))
        normed_ref[...] = normed
        mixed_ref[...] = mm(normed, w_ref[...]).astype(BF)
        small_ref[...] = mm_nt(normed, sw_ref[...])

    @pl.when(step == pl.num_programs(0) - 1)
    def _():
        normed = normal(rim_ref[...].astype(F32))
        normed_ref[:16] = normed
        mixed_ref[:16] = mm(normed, w_ref[...]).astype(BF)


def row_specs(rows):
    tiles = 2 * rows // TILE
    held = lambda width: pl.BlockSpec((TILE, width), lambda i: (jnp.minimum(i, tiles - 1) % (tiles // 2), 0))
    tile = lambda width: pl.BlockSpec((TILE, width), lambda i: (jnp.minimum(i, tiles - 1), 0))
    every = lambda width: pl.BlockSpec((TILE, width), lambda i: (i, 0))
    same = lambda *shape: pl.BlockSpec(shape, lambda i: (0,) * len(shape))
    return tiles + 1, held, tile, every, same


def project(side, own, their, rim, gain, weight, small_weight):
    rows, width = own.shape
    steps, held, tile, every, same = row_specs(rows)
    columns = weight.shape[1]
    return pl.pallas_call(
        project_kernel,
        grid=(steps,),
        in_specs=[pl.BlockSpec(memory_space=pltpu.SMEM), held(width), held(width), same(16, width), same(1, width),
                  same(*weight.shape), same(*small_weight.shape)],
        out_specs=[every(width), every(columns), tile(small_weight.shape[0])],
        out_shape=[jax.ShapeDtypeStruct((2 * rows + 16, width), BF), jax.ShapeDtypeStruct((2 * rows + 16, columns), BF),
                   jax.ShapeDtypeStruct((2 * rows, small_weight.shape[0]), F32)],
        compiler_params=pltpu.CompilerParams(vmem_limit_bytes=48 * 2**20),
    )(side, own, their, rim, gain, weight, small_weight)


def unproject_kernel(side_ref, own_ref, their_ref, rim_ref, gain_ref, gm_ref, gg_ref, gs_ref, w_ref, gw_ref, sw_ref, back_ref,
                     rim_back_ref, grad_gain_ref):
    step = pl.program_id(0)

    @pl.when(step == 0)
    def _():
        grad_gain_ref[...] = jnp.zeros_like(grad_gain_ref)

    def norm_back(x, grad):
        factor = lax.rsqrt(jnp.mean(x * x, axis=1, keepdims=True) + EPS)
        unit = x * factor
        grad_gain_ref[...] += jnp.sum(grad * unit, axis=0, keepdims=True)
        scaled = grad * gain_ref[...]
        return (factor * (scaled - unit * jnp.mean(scaled * unit, axis=1, keepdims=True))).astype(BF)

    @pl.when(step < pl.num_programs(0) - 1)
    def _():
        grad = mm_nt(gm_ref[...], w_ref[...]) + mm_nt(gg_ref[...], gw_ref[...])
        for i in range(sw_ref.shape[0]):
            grad = grad + gs_ref[:, i:i + 1] * sw_ref[i:i + 1]
        back_ref[...] = norm_back(place_rows(side_ref, own_ref, their_ref), grad)

    @pl.when(step == pl.num_programs(0) - 1)
    def _():
        rim_back_ref[...] = norm_back(rim_ref[...].astype(F32), mm_nt(gm_ref[:16], w_ref[...]))


def unproject(side, own, their, rim, gain, grad_mixed, grad_gate, grad_small, weight, gate_weight, small_weight):
    rows, width = own.shape
    steps, held, tile, every, same = row_specs(rows)
    return pl.pallas_call(
        unproject_kernel,
        grid=(steps,),
        in_specs=[pl.BlockSpec(memory_space=pltpu.SMEM), held(width), held(width), same(16, width), same(1, width),
                  every(weight.shape[1]), tile(gate_weight.shape[1]), tile(grad_small.shape[1]), same(*weight.shape),
                  same(*gate_weight.shape), same(*small_weight.shape)],
        out_specs=[tile(width), same(16, width), same(1, width)],
        out_shape=[jax.ShapeDtypeStruct((2 * rows, width), BF), jax.ShapeDtypeStruct((16, width), BF),
                   jax.ShapeDtypeStruct((1, width), F32)],
        compiler_params=pltpu.CompilerParams(vmem_limit_bytes=56 * 2**20),
    )(side, own, their, rim, gain, grad_mixed, grad_gate, grad_small, weight, gate_weight, small_weight)


def mix_kernel(heads, x_ref, gw_ref, ow_ref, o_ref, e_ref, s_ref, live_ref, gain_ref, gate_ref, m_ref, out_ref):
    live = live_ref[...]
    gain = gain_ref[...]
    gates = mm(x_ref[...], gw_ref[...])
    gate_ref[...] = gates
    for h in range(heads):
        vs = slice(h * DV, (h + 1) * DV)
        y = (o_ref[:, vs] + mm(e_ref[:, h * DK:(h + 1) * DK], s_ref[h])) * live
        r = lax.rsqrt(jnp.mean(y * y, axis=1, keepdims=True) + EPS)
        gate = gates[:, vs]
        m_ref[:, vs] = (y * r * gain * (gate * jax.nn.sigmoid(gate))).astype(BF)
    out_ref[...] = mm_nt(m_ref[...], ow_ref[...]).astype(BF)


def mix(normed, gate_weight, out_weight, o, e, entry, live, gain, heads):
    rows, width = o.shape[0], normed.shape[1]
    row = lambda width: pl.BlockSpec((TILE, width), lambda i: (i, 0))
    same = lambda *shape: pl.BlockSpec(shape, lambda i: (0,) * len(shape))
    return pl.pallas_call(
        functools.partial(mix_kernel, heads),
        grid=(rows // TILE,),
        in_specs=[row(width), same(*gate_weight.shape), same(*out_weight.shape), row(heads * DV), row(heads * DK),
                  same(heads, DK, DV), row(1), same(1, DV)],
        out_specs=[row(heads * DV), row(heads * DV), row(width)],
        out_shape=[jax.ShapeDtypeStruct((rows, heads * DV), F32), jax.ShapeDtypeStruct((rows, heads * DV), BF),
                   jax.ShapeDtypeStruct((rows, width), BF)],
        compiler_params=pltpu.CompilerParams(vmem_limit_bytes=48 * 2**20),
    )(normed, gate_weight, out_weight, o, e, entry, live, gain)


def feed_kernel(places, chunks, own_ref, cot_hbm, wg_hbm, wu_hbm, wd_hbm, sum_ref, down_hbm, dwd_hbm, dwg_hbm, dwu_hbm,
                rows, cot, wg, wu, wd, hid, gg, gu, gr, pair, line, dn, dwd, dwg, dwu, load_sems, out_sems, own_sem,
                ag_send, ag_recv, pair_send, pair_recv, right_send, right_recv, left_send, left_recv):
    w, place, side, n = position()
    partner = w + 1 - 2 * side
    quarter, width = own_ref.shape
    size = quarter // chunks
    part = lambda c: pl.ds(c * size, size)
    devices = [(partner, n), (w + 2, n), (w - 2, n)]
    loads = [pltpu.make_async_copy(source, target, load_sems.at[i]) for i, (source, target) in enumerate(
        ((wg_hbm, wg), (wu_hbm, wu), (cot_hbm, cot), (wd_hbm, wd)))]

    def remote(source, target, send, recv, device):
        return pltpu.make_async_remote_copy(src_ref=source, dst_ref=target, send_sem=send, recv_sem=recv, device_id=device,
                                            device_id_type=MESH)

    def move(slot, way, c, own=False):
        source = own_ref.at[part(c)] if own else rows.at[slot, part(c)]
        return remote(source, rows.at[slot, part(c)], ag_send.at[way, slot, c], ag_recv.at[slot, c], devices[way])

    def along(slot, way, c, own=False):
        @pl.when(place < places - 1 if way == 1 else place > 0)
        def _():
            move(slot, way, c, own).start()

    def across(t, c):
        return remote(gr.at[2 * t + 1 - side, part(c)], pair.at[t, part(c)], pair_send.at[t, c], pair_recv.at[t, c], devices[0])

    def right(t, c):
        return remote(gr.at[2 * t + side, part(c)], line.at[t, part(c)], right_send.at[t, c], right_recv.at[t, c], devices[1])

    def left(t, c, arriving=False):
        slot = jnp.where(t == place - (0 if arriving else 1), places, t)
        return remote(gr.at[2 * t + side, part(c)], line.at[slot, part(c)], left_send.at[t, c], left_recv.at[t, c], devices[2])

    def inside(there):
        return (there >= 0) & (there < places)

    def arrive(s):
        for way, there in ((1, place - s), (2, place + s)):
            @pl.when(inside(there))
            def _():
                for c in range(chunks):
                    move(2 * there + side, way, c).wait_recv()
                    along(2 * there + side, way, c)
                    move(2 * there + side, 0, c).start()

    def work(there):
        for c in range(chunks):
            move(2 * there + 1 - side, 0, c).wait_recv()
        both = pl.ds(2 * there, 2)
        flat = lambda ref: ref[both].reshape(2 * quarter, ref.shape[2])
        x = flat(rows)
        gate = mm_nt(x, wg[...])
        up = mm_nt(x, wu[...])
        grad = mm_nt(flat(cot), wd[...])
        sig = jax.nn.sigmoid(gate)
        act = gate * sig
        hid[both] = (act * up).astype(BF).reshape(2, quarter, -1)
        low_gate = (grad * up * (sig + act * (1.0 - sig))).astype(BF)
        low_up = (grad * act).astype(BF)
        gg[both] = low_gate.reshape(2, quarter, -1)
        gu[both] = low_up.reshape(2, quarter, -1)
        gr[both] = (mm(low_gate, wg[...]) + mm(low_up, wu[...])).astype(BF).reshape(2, quarter, width)
        for c in range(chunks):
            across(there, c).start()

    def add(t, c, other, slot):
        at = (2 * t + side, part(c))
        gr[at] = (gr[at].astype(F32) + other[slot, part(c)].astype(F32)).astype(BF)

    def pass_on(s):
        t = s

        @pl.when(place < t)
        def _():
            for c in range(chunks):
                across(t, c).wait_recv()
                add(t, c, pair, t)

                @pl.when(place > 0)
                def _():
                    right(t, c).wait_recv()
                    add(t, c, line, t)

                right(t, c).start()

        t_left = places - 1 - s

        @pl.when(place > t_left)
        def _():
            for c in range(chunks):
                across(t_left, c).wait_recv()
                add(t_left, c, pair, t_left)

                @pl.when(place < places - 1)
                def _():
                    left(t_left, c, True).wait_recv()
                    add(t_left, c, line, t_left)

                left(t_left, c).start()

    greet(line=places, pair=True)
    for load in loads:
        load.start()
    for c in range(chunks):
        move(w, 0, c, True).start()
        along(w, 1, c, True)
        along(w, 2, c, True)
    own = pltpu.make_async_copy(own_ref, rows.at[w], own_sem)
    own.start()
    own.wait()
    for load in loads:
        load.wait()

    def rows_work(s, _):
        @pl.when(inside(place - s))
        def _():
            work(place - s)

        @pl.when(inside(place + s) & (s > 0))
        def _():
            work(place + s)
        return 0

    def advance(s, _):
        arrive(s)
        rows_work(s - 1, 0)

        @pl.when(s > 1)
        def _():
            pass_on(s - 1)
        return 0

    lax.fori_loop(1, places, advance, 0)
    rows_work(places - 1, 0)

    columns = width // 4

    def weights(i, _):
        cut = pl.ds(pl.multiple_of(i * columns, columns), columns)
        everything = lambda ref: ref[...].reshape(2 * places * quarter, ref.shape[2])
        slot = lax.rem(i, 2)

        @pl.when(i >= 2)
        def _():
            pltpu.make_async_copy(dn.at[slot], down_hbm.at[pl.ds(0, 2)], out_sems.at[3 + slot]).wait()

        dwd[:, cut] = mm_tn(everything(hid), cot[:, :, cut].reshape(2 * places * quarter, columns)).astype(BF)
        x = rows[:, :, cut].reshape(2 * places * quarter, columns)
        dwg[:, cut] = mm_tn(everything(gg), x).astype(BF)
        dwu[:, cut] = mm_tn(everything(gu), x).astype(BF)
        both = pl.ds(2 * i, 2)
        dn[slot] = jnp.dot(hid[both].reshape(2 * quarter, hid.shape[2]), wd[...],
                           preferred_element_type=F32).astype(BF).reshape(2, quarter, width)
        pltpu.make_async_copy(dn.at[slot], down_hbm.at[both], out_sems.at[3 + slot]).start()
        return 0

    before = jnp.where((place > 0) & (place < places - 1), 2, 0)
    lax.fori_loop(0, before, weights, 0)
    pass_on(places - 1)
    lax.fori_loop(before, 4, weights, 0)
    outs = [pltpu.make_async_copy(source, target, out_sems.at[i]) for i, (source, target) in enumerate(
        ((dwd, dwd_hbm), (dwg, dwg_hbm), (dwu, dwu_hbm)))]
    for out in outs:
        out.start()
    for c in range(chunks):
        across(place, c).wait_recv()
        add(place, c, pair, place)

        @pl.when(place > 0)
        def _():
            right(place, c).wait_recv()
            add(place, c, line, place)

        @pl.when(place < places - 1)
        def _():
            left(place, c, True).wait_recv()
            add(place, c, line, places)

        sum_ref[part(c)] = gr[2 * place + side, part(c)].astype(F32)
    for out in outs:
        out.wait()
    for slot in range(2):
        pltpu.make_async_copy(dn.at[slot], down_hbm.at[pl.ds(0, 2)], out_sems.at[3 + slot]).wait()

    def settle(t, _):
        for c in range(chunks):
            across(t, c).wait_send()
            move(2 * t + side, 0, c).wait_send()

            @pl.when((place < places - 1) & (t <= place))
            def _():
                move(2 * t + side, 1, c).wait_send()

            @pl.when((place > 0) & (t >= place))
            def _():
                move(2 * t + side, 2, c).wait_send()

            @pl.when(t > place)
            def _():
                right(t, c).wait_send()

            @pl.when(t < place)
            def _():
                left(t, c).wait_send()
        return 0

    lax.fori_loop(0, places, settle, 0)


def feed(own, cot, w_gate, w_up, w_down, call_id, chunks=4):
    count = lax.axis_size("wide")
    places = count // 2
    quarter, width = own.shape
    units = w_down.shape[0]
    hbm, vmem = pl.BlockSpec(memory_space=pl.ANY), pl.BlockSpec(memory_space=pltpu.VMEM)
    blocks = lambda columns: pltpu.VMEM((count, quarter, columns), BF)
    line = lambda amount: pltpu.VMEM((amount, quarter, width), BF)
    sems = pltpu.SemaphoreType.DMA((places, chunks))
    return pl.pallas_call(
        functools.partial(feed_kernel, places, chunks),
        in_specs=[vmem, hbm, hbm, hbm, hbm],
        out_specs=[vmem, hbm, hbm, hbm, hbm],
        out_shape=[jax.ShapeDtypeStruct((quarter, width), F32), jax.ShapeDtypeStruct((count, quarter, width), BF),
                   jax.ShapeDtypeStruct((units, width), BF), jax.ShapeDtypeStruct((units, width), BF),
                   jax.ShapeDtypeStruct((units, width), BF)],
        scratch_shapes=[blocks(width), blocks(width), pltpu.VMEM((units, width), BF), pltpu.VMEM((units, width), BF),
                        pltpu.VMEM((units, width), BF), blocks(units), blocks(units), blocks(units), blocks(width),
                        line(places), line(places + 1), pltpu.VMEM((2, 2, quarter, width), BF), pltpu.VMEM((units, width), BF),
                        pltpu.VMEM((units, width), BF), pltpu.VMEM((units, width), BF), pltpu.SemaphoreType.DMA((4,)),
                        pltpu.SemaphoreType.DMA((5,)), pltpu.SemaphoreType.DMA, pltpu.SemaphoreType.DMA((3, count, chunks)),
                        pltpu.SemaphoreType.DMA((count, chunks))] + [sems] * 6,
        compiler_params=pltpu.CompilerParams(collective_id=call_id, has_side_effects=True, vmem_limit_bytes=60 * 2**20),
    )(own, cot.reshape(count, quarter, width), w_gate, w_up, w_down)


CONV = 4


def rms_norm(value, gain):
    return value * lax.rsqrt(jnp.mean(value * value, axis=-1, keepdims=True) + EPS) * gain


def after(value, *others):
    return lax.optimization_barrier((value,) + others)[0]


def part(value, axis, index, count=2):
    size = value.shape[axis] // count
    return lax.dynamic_slice_in_dim(value, index * size, size, axis)


def ordered(mine, theirs, side, axis):
    return jnp.concatenate([jnp.where(side == 0, mine, theirs), jnp.where(side == 0, theirs, mine)], axis=axis)


def sequence_tables(doc_lengths, first_row, row_count, block_size):
    padded = (doc_lengths + block_size - 1) // block_size * block_size
    seq_ends = jnp.cumsum(padded)
    seq_starts = seq_ends - padded
    row_places = first_row + jnp.arange(row_count, dtype=jnp.int32)
    inside_mask = (row_places[:, None] >= seq_starts[None, :]) & (row_places[:, None] < seq_ends[None, :])
    live_mask = jnp.any(inside_mask & (row_places[:, None] < (seq_starts + doc_lengths)[None, :]), axis=1, keepdims=True)
    fresh_block = jnp.any(row_places[::block_size][:, None] == seq_starts[None, :], axis=1)
    return live_mask.astype(F32), jnp.where(fresh_block, 0.0, 1.0).astype(F32)


def contract_rows(left, right):
    return lax.dot_general(left, right, (((0,), (0,)), ((), ())), preferred_element_type=F32)


def contract_cols(left, right):
    return lax.dot_general(left, right, (((1,), (1,)), ((), ())), preferred_element_type=F32)


def feed_apart(own, cot, w_gate, w_up, w_down):
    quarter = own.shape[0]
    blocks = lambda a: a.astype(BF).reshape(-1, quarter, a.shape[1])
    gathered_rows = line_gather([own], 3)[0]
    gate_pre = contract_cols(gathered_rows, w_gate)
    up_pre = contract_cols(gathered_rows, w_up)
    gate_sig = jax.nn.sigmoid(gate_pre)
    gate_act = gate_pre * gate_sig
    hidden_low = (gate_act * up_pre).astype(BF)
    grad_hidden = contract_cols(cot, w_down)
    grad_gate_low = (grad_hidden * up_pre * gate_sig * (1.0 + gate_pre * (1.0 - gate_sig))).astype(BF)
    grad_up_low = (grad_hidden * gate_act).astype(BF)
    grad_rows = (jnp.dot(grad_gate_low, w_gate, preferred_element_type=F32)
                 + jnp.dot(grad_up_low, w_up, preferred_element_type=F32))
    grad_sum = line_scatter([], [blocks(grad_rows)], [], [], 4)[1][0]
    down_rows = blocks(jnp.dot(hidden_low, w_down, preferred_element_type=F32))
    grad_w_down = contract_rows(hidden_low, cot).astype(BF)
    grad_w_gate = contract_rows(grad_gate_low, gathered_rows).astype(BF)
    grad_w_up = contract_rows(grad_up_low, gathered_rows).astype(BF)
    return grad_sum, down_rows, grad_w_down, grad_w_gate, grad_w_up


def shards(block_input, gain_attn, w_query, w_key, w_value, w_gate_out, w_decay, w_beta, conv_query, conv_key,
           conv_value, a_log, dt_bias, out_gain, w_out, gain_mlp, w_gate, w_up, w_down, doc_lengths, cotangent):
    d_model = block_input.shape[1]
    row_count = 2 * block_input.shape[0]
    quarter = cotangent.shape[0]
    depth = w_query.shape[0]
    heads = a_log.shape[0] // 2
    narrow = lax.axis_size("narrow")
    wide = lax.axis_size("wide")
    wide_index = lax.axis_index("wide")
    place, side = wide_index // 2, wide_index % 2
    live, flags = sequence_tables(doc_lengths, place * row_count, row_count, BLOCK)
    gain_row, a_row, dt_row = out_gain[None, :], part(a_log, 0, side)[None, :], part(dt_bias, 0, side)[None, :]
    key_width, value_width = heads * DK, heads * DV
    columns = 2 * key_width + value_width
    row_blocks = lambda a: a.astype(BF).reshape(-1, quarter, a.shape[1])
    halves = lambda *arrays: tuple(
        jnp.concatenate([part(a, 1, s) for a in arrays], axis=1) for s in (side, 1 - side))
    padded = lambda a: jnp.pad(a, ((0, 16 - 4 * heads), (0, 0)))

    first, small_weight, their_input, rim_input = line_gather(
        [halves(w_query, w_key, w_value), padded(jnp.concatenate([w_decay.T, w_beta.T], axis=0))], 1, rows=block_input)
    rim_input = jnp.where(place > 0, rim_input, jnp.zeros_like(rim_input))
    small_weight = small_weight.reshape(wide, 16, depth).transpose(1, 0, 2).reshape(16, d_model)
    small_weight = jnp.concatenate([part(small_weight[:2 * heads], 0, side), part(small_weight[2 * heads:4 * heads], 0, side)],
                                   axis=0)
    taps = jnp.concatenate([part(conv_query, 1, side), part(conv_key, 1, side), part(conv_value, 1, side)], axis=1)
    side_word = side.astype(jnp.int32)[None]
    padded_small = jnp.pad(small_weight, ((0, 16 - 2 * heads), (0, 0)))
    normed_low, mixed, small = project(side_word, block_input, their_input, rim_input, gain_attn[None, :], first, padded_small)
    small = small[:, :2 * heads]

    (local_out, reach, inverses, states, end, entry), (gate_weight, gathered_cot, out_weight) = forward_gather(
        flags, mixed, taps, small, live, a_row, dt_row, heads, [halves(w_gate_out), cotangent, halves(w_out)], 7)
    gate_rows, mixer_low, head_part = mix(normed_low, gate_weight, out_weight, local_out, reach, entry, live,
                                          gain_row, heads)
    own_rows = cube_scatter(row_blocks(head_part), 9) + part(
        block_input, 0, lax.axis_index("narrow"), narrow).astype(F32)
    mlp_normed, mlp_norm_back = jax.vjp(rms_norm, own_rows, gain_mlp)
    feed_forward = feed_apart if wide > 8 else functools.partial(feed, call_id=3)
    grad_mlp_normed, down_rows, grad_w_down, grad_w_gate, grad_w_up = feed_forward(
        mlp_normed.astype(BF), gathered_cot, w_gate.T, w_up.T, w_down)
    grad_own_norm, grad_gain_mlp = mlp_norm_back(grad_mlp_normed)
    grad_own = cotangent.astype(F32) + grad_own_norm
    grad_attn = cube_gather(grad_own.astype(BF), 10)

    grad_mixer = jnp.dot(grad_attn, out_weight, preferred_element_type=F32)
    grad_outputs, grad_gate_rows, grad_out_gain, direct = unfinish(local_out, reach, entry, gate_rows, live, gain_row,
                                                                   grad_mixer, heads)
    (grad_mixed, grad_small, grad_taps, grad_scalars), (sum_w_out, sum_w_gate_out), (sum_down,), shares = backward_scatter(
        flags, mixed, taps, small, live, a_row, dt_row, inverses, states, grad_outputs, entry, direct, end, heads,
        [(grad_attn, mixer_low), (normed_low, grad_gate_rows)], [down_rows], [grad_w_gate, grad_w_up, grad_w_down], 8)
    output = (own_rows + sum_down).astype(BF)
    grad_small = grad_small.astype(BF)
    grad_small_weight = contract_rows(grad_small, normed_low[:row_count]).astype(BF)
    both_sides = lambda a: ordered(a, jnp.zeros_like(a), side, 0)
    grad_small_weight = padded(jnp.concatenate([both_sides(grad_small_weight[:heads]), both_sides(grad_small_weight[heads:])],
                                               axis=0))
    small_blocks = grad_small_weight.reshape(16, wide, depth).transpose(1, 0, 2)
    grad_input_part, grad_rim, grad_gain_attn = unproject(
        side_word, block_input, their_input, rim_input, gain_attn[None, :], grad_mixed, grad_gate_rows, grad_small.astype(F32),
        first, gate_weight, small_weight.astype(F32))
    grad_rim = jnp.pad(grad_rim[None], ((7, 0), (0, 0), (0, 0)))

    lanes = lambda a: jnp.pad(a, (0, -a.shape[0] % 1024)).reshape(-1, 128)
    head_sums = lanes(jnp.concatenate([grad_taps.reshape(-1), grad_scalars[0], grad_scalars[1]]))
    whole_sums = lanes(jnp.concatenate([grad_gain_attn[0], grad_gain_mlp, grad_out_gain[0]]))
    (sum_first,), (sum_small,), (input_sum, _), (every,) = line_scatter(
        [(normed_low, grad_mixed)], [small_blocks], [row_blocks(grad_input_part), grad_rim],
        [jnp.concatenate([head_sums, whole_sums], axis=0)], 6)
    grad_input = input_sum + grad_own
    whole_sums = jnp.sum(every[:, head_sums.shape[0]:], axis=0).reshape(-1)
    every = every[:, :head_sums.shape[0]].reshape(2, narrow, -1)
    conv_all = every[:, :, :4 * columns].reshape(2, narrow, 4, columns)
    conv_parts = [conv_all[:, :, :, lo:hi].transpose(2, 1, 0, 3).reshape(4, -1) for lo, hi in
                  ((0, key_width), (key_width, 2 * key_width), (2 * key_width, columns))]
    scalars = [every[:, :, lo:lo + heads].transpose(1, 0, 2).reshape(-1) for lo in (4 * columns, 4 * columns + heads)]
    joined = lambda found, lo, hi: ordered(found[0][:, lo:hi], found[1][:, lo:hi], side, 1)
    return (
        output, grad_input, whole_sums[:d_model],
        joined(sum_first, 0, key_width), joined(sum_first, key_width, 2 * key_width), joined(sum_first, 2 * key_width, columns),
        joined(sum_w_gate_out, 0, value_width),
        sum_small[:2 * heads].T, sum_small[2 * heads:4 * heads].T, conv_parts[0], conv_parts[1], conv_parts[2],
        scalars[0], scalars[1], whole_sums[2 * d_model:2 * d_model + DV], joined(sum_w_out, 0, value_width),
        whole_sums[d_model:2 * d_model], shares[0].T, shares[1].T, shares[2],
    )


def solution(mesh):
    both = P("wide", "narrow")
    rows = P(("wide", "narrow"), None)
    return jax.shard_map(
        shards,
        mesh=mesh,
        in_specs=(P("wide", None), P(), both, both, both, both, both, both, P(None, "narrow"), P(None, "narrow"),
                  P(None, "narrow"), P("narrow"), P("narrow"), P(), both, P(), P(None, "wide"), P(None, "wide"),
                  P("wide", None), P(), rows),
        out_specs=(rows, rows, P(), both, both, both, both, both, both, P(), P(), P(), P(), P(), P(), both, P(),
                   P("narrow", "wide"), P("narrow", "wide"), both),
        check_vma=False,
    )
```
